512 devices in a mesh: ep: 128 (over z, y, core), rep: 4 (over x).
Axes of the slice: x: 4, y: 8, z: 8, core: 2. Of those that a mesh axis runs over, the one named last changes fastest.
Arguments:
- tokens: bfloat16 [16384, 4096], P('ep'), may hold values from -54 to 54
- expert_ids: int32 [16384, 8], P('ep'), may hold values from 0 to 127, all different within a row; in each aligned block of 128 rows (0 to 127, 128 to 255, ...) at most 10 rows name the same one
- hidden_grads: bfloat16 [16384, 8, 768], P('ep', None, 'rep'), may hold values from -6 to 6
- gate_weight: bfloat16 [128, 768, 4096], P('ep', 'rep'), may hold values from -0.09375 to 0.09375
- probes: bfloat16 [128, 4096], replicated, may hold values from -1.5 to 1.5
- grad_probes: bfloat16 [128, 768], replicated, may hold values from -6 to 6
- window_counts: int32 [128], P('ep'), may hold values from 1024 to 4095
Outputs:
- input_sketch: float32 [128, 4096, 128], P('ep', 'rep')
- grad_sketch: float32 [128, 768, 128], P('ep', 'rep')
The draws below stay inside these ranges and needn't reach their ends.
Inputs may be any that keep to these rules, and one draw needn't show every extreme that they name: `expert_ids`: each row names 8 different experts; among the 128 tokens of one index of ep no expert is named more than 10 times, and 10 is reached.
All inputs are finite; a program needn't handle non-finite values.
Results may differ from the reference program's by a relative error of at most 0.0032.
Values may be sent and summed in bfloat16 or wider, within the bound.
No kernel may reach another device: no remote copies, remote signals or barrier semaphores. Data moves between devices by JAX's collectives and lax.ppermute only.
A program may use at most 128 MiB of HBM per device.

```python
import math
import jax
import jax.numpy as jnp
import numpy as np
from jax import lax

D = 4096
FFW = 768
TOP = 8
R = 128
TOK_DEV = 128
EXPERTS = 128
TOKENS = 16384
MOST = 10
N_EP = 128


def draw_tokens(key, part):
    key = jax.random.fold_in(key, 11)
    key_rows, key_cols, key_base = jax.random.split(key, 3)
    low = math.log(0.3)
    high = math.log(3.0)
    row_scale = jnp.exp(jax.random.uniform(key_rows, (TOKENS, 1), jnp.float32, low, high))
    col_scale = jnp.exp(jax.random.uniform(key_cols, (1, D), jnp.float32, low, high))
    base = jax.random.truncated_normal(key_base, -6.0, 6.0, (TOKENS, D), jnp.float32)
    return (base * row_scale * col_scale).astype(jnp.bfloat16)


def set_ends(drawn, rng, smallest, high):
    spot = [jax.random.randint(jax.random.fold_in(rng, axis), (), 0, length) for axis, length in enumerate(drawn.shape)]
    main_axis = drawn.shape.index(max(drawn.shape))
    neighbour = spot[:main_axis] + [(spot[main_axis] + 1) % drawn.shape[main_axis]] + spot[main_axis + 1:]
    return drawn.at[tuple(spot)].set(smallest).at[tuple(neighbour)].set(high)


def level_of(key, extent, cuts, smallest, top_value):
    def one(dim, parts):
        draws = jax.random.uniform(jax.random.fold_in(jax.random.fold_in(key, 6), dim), (parts,), jnp.float32, smallest / len(cuts), top_value / len(cuts))
        return jnp.repeat(jnp.exp(draws), extent[dim] // parts).reshape((-1,) + (1,) * (len(extent) - dim - 1))

    level = one(*cuts[0])
    for cut in cuts[1:]:
        level = level * one(*cut)
    return level


def deal_out(own_key, own, number, rows, count, top, bound, lean):
    ranking = jax.random.permutation(own_key, count)
    crowded, usual = shares(count, rows * top, bound, lean, True), shares(count, rows * top, bound, lean, False)
    places = jnp.arange(count)

    def named(tallies, offset_by):
        used = int((tallies > 0).sum())
        fixed = max(1, used // 4)
        passed = fixed + (places - fixed + offset_by * (used - fixed)) % max(1, count - fixed)
        return jnp.zeros((count,), jnp.int32).at[ranking[jnp.where(places < fixed, places, passed)]].set(jnp.asarray(tallies, jnp.int32))

    tallies = jnp.where(number % 4 == 0, named(crowded, number // 4), named(usual, number - number // 4 - 1))
    mixed = jax.random.permutation(jax.random.fold_in(own, 3), count)
    source_of, sink = mixed[0:count // 2 * 2:2], mixed[1:count // 2 * 2:2]
    slack = jnp.minimum(tallies[source_of] - 1, bound - tallies[sink]) // 2
    slack = jnp.where((source_of == ranking[0]) | (sink == ranking[0]) | (tallies[sink] == 0), 0, jnp.maximum(slack, 0))
    passed = jax.random.randint(jax.random.fold_in(own, 4), (count // 2,), 0, 1 << 20) % (slack + 1)
    tallies = tallies.at[source_of].add(-passed).at[sink].add(passed)
    items = jnp.searchsorted(jnp.cumsum(tallies), jnp.arange(rows * top), side="right").astype(jnp.int32)
    listing = items.reshape(top, rows).T
    listing = listing[jax.random.permutation(jax.random.fold_in(own, 1), rows)]
    offset_by = jax.random.randint(jax.random.fold_in(own, 2), (rows, 1), 0, top)
    return jnp.take_along_axis(listing, (jnp.arange(top)[None, :] + offset_by) % top, axis=1)


def shares(count, total, reach, slope, full):
    loads = [(1 << 20) // math.isqrt(grade ** slope) + 1 for grade in range(1, count + 1)]
    largest = reach if full else min(reach, max(-(-total // count), total * loads[0] // sum(loads)))
    least = 1 if total - largest >= count - 1 else 0
    counts, spare = [largest] + [least] * (count - 1), total - largest - least * (count - 1)
    while spare > 0:
        candidates = [i for i in range(1, count) if counts[i] < largest] or [i for i in range(1, count) if counts[i] < reach]
        whole, left = sum([loads[i] for i in candidates]), spare
        for i in candidates:
            more = min(reach - counts[i], max(1, left * loads[i] // whole), spare)
            counts[i] = counts[i] + more
            spare = spare - more
    return np.array(counts)


def bell_draw(own_key, shape, scale, bound, shards=(), kind=jnp.bfloat16):
    array = scale * jax.random.normal(own_key, shape, jnp.float32)
    if shards:
        array = array * level_of(own_key, shape, shards, -0.22, 0.18)
    return jnp.clip(array, -bound, bound).astype(kind)


def setup_inputs(seed: int = 0) -> dict:
    splits = jax.random.split(jax.random.key(seed), 8)
    tokens = draw_tokens(jax.random.fold_in(splits[7], 71), 0)
    expert_ids_keys = jax.random.split(jax.random.fold_in(splits[1], 1), TOKENS // TOK_DEV)
    expert_ids_turns = jax.random.permutation(jax.random.fold_in(splits[1], 3), TOKENS // TOK_DEV)
    expert_ids = jax.vmap(lambda own, number: deal_out(jax.random.fold_in(splits[1], 2), own, number, TOK_DEV, EXPERTS, TOP, MOST, 2))(expert_ids_keys, expert_ids_turns).reshape((TOKENS, TOP))
    hidden_grads = bell_draw(splits[2], (TOKENS, TOP, FFW), 1.0, 6.0, ((0, 128), (2, 4)))
    gate_weight = bell_draw(splits[3], (EXPERTS, FFW, D), D ** -0.5, 0.09375, ((0, 128), (1, 4)))
    probes = bell_draw(splits[4], (R, D), 0.25, 1.5)
    grad_probes = bell_draw(splits[5], (R, FFW), 1.0, 6.0)
    window_counts = set_ends(jax.random.randint(splits[6], (EXPERTS,), TOK_DEV * TOP, 4 * TOK_DEV * TOP), jax.random.fold_in(splits[6], 1), TOK_DEV * TOP, (4 * TOK_DEV * TOP) - 1).astype(jnp.int32)
    return dict(tokens=tokens, expert_ids=expert_ids, hidden_grads=hidden_grads, gate_weight=gate_weight, probes=probes, grad_probes=grad_probes, window_counts=window_counts)


def derivative_silu(values):
    sigmoid = jax.nn.sigmoid(values)
    return sigmoid * (1.0 + values * (1.0 - sigmoid))


def reference(tokens, expert_ids, hidden_grads, gate_weight, probes, grad_probes, window_counts):
    assigned = TOKENS * TOP
    capacity = N_EP * MOST
    flat_ids = expert_ids.reshape(assigned).astype(jnp.int32)
    ordering = jnp.argsort(flat_ids, stable=True).astype(jnp.int32)
    sorted_ids = flat_ids[ordering]
    per_expert = jax.ops.segment_sum(jnp.ones((assigned,), jnp.int32), flat_ids, num_segments=EXPERTS).astype(jnp.int32)
    offsets = (jnp.cumsum(per_expert) - per_expert).astype(jnp.int32)
    ranks = (jnp.arange(assigned, dtype=jnp.int32) - offsets[sorted_ids]).astype(jnp.int32)
    table = jnp.full((EXPERTS, capacity), assigned, jnp.int32).at[sorted_ids, ranks].set(ordering)
    padded_rows = jnp.concatenate([tokens, jnp.zeros((1, D), tokens.dtype)], 0)
    padded_grads = jnp.concatenate([hidden_grads.reshape(assigned, FFW), jnp.zeros((1, FFW), hidden_grads.dtype)], 0)
    projected_all = jnp.dot(padded_rows, probes.T, preferred_element_type=jnp.float32).astype(jnp.bfloat16)

    def one_expert(inputs):
        slots, weight, amount = inputs
        token_index = (slots // TOP).astype(jnp.int32)
        rows = padded_rows[token_index]
        projected = projected_all[token_index]
        inverse = 1.0 / amount.astype(jnp.float32)
        input_part = jnp.dot(rows.T, projected, preferred_element_type=jnp.float32) * inverse
        gate_pre = jnp.dot(rows, weight.T, preferred_element_type=jnp.float32)
        gate_grad = (padded_grads[slots].astype(jnp.float32) * derivative_silu(gate_pre)).astype(jnp.bfloat16)
        grad_projected = jnp.dot(gate_grad, grad_probes.T, preferred_element_type=jnp.float32).astype(jnp.bfloat16)
        grad_part = jnp.dot(gate_grad.T, grad_projected, preferred_element_type=jnp.float32) * inverse
        return input_part, grad_part

    input_sketch, grad_sketch = lax.map(one_expert, (table, gate_weight, window_counts))
    return input_sketch, grad_sketch
```

```python
import jax
import jax.numpy as jnp
from jax import lax
from jax.experimental import pallas as pl
from jax.experimental.pallas import tpu as pltpu
from jax.sharding import PartitionSpec as P

OWNERS = 128
REPS = 4
TOK = 128
TOP = 8
D = 4096
SHARE = D // REPS
FFW = 768
UNITS = FFW // REPS
R = 128
FIRST = 8
EXTRA = 2
ROWS = OWNERS * FIRST
QUARTER = ROWS // REPS
EXTRA_ROWS = OWNERS * EXTRA
EXTRA_QUARTER = EXTRA_ROWS // REPS
STACK = FFW + R
HALF = STACK // 2

BF = jnp.bfloat16
F32 = jnp.float32
NT = (((1,), (1,)), ((), ()))
NN = (((1,), (0,)), ((), ()))

VM = pl.BlockSpec(memory_space=pltpu.VMEM)
SM = pl.BlockSpec(memory_space=pltpu.SMEM)


def dot(a, b, dims=NN):
    return lax.dot_general(a, b, dims, preferred_element_type=F32)


def iota(shape, axis):
    return lax.broadcasted_iota(jnp.int32, shape, axis)


def ones_where(mask):
    return jnp.where(mask, 1.0, 0.0).astype(BF)


def kernel_call(body, out_shape, in_specs, flops, bytes_accessed, scratch=()):
    return pl.pallas_call(
        body,
        out_shape=out_shape,
        in_specs=in_specs,
        out_specs=jax.tree.map(lambda _: VM, out_shape),
        scratch_shapes=list(scratch),
        compiler_params=pltpu.CompilerParams(vmem_limit_bytes=50 * 1024 * 1024),
        cost_estimate=pl.CostEstimate(
            flops=flops, bytes_accessed=bytes_accessed, transcendentals=0
        ),
    )


def places(ids_t):
    experts = iota((OWNERS, TOK), 0)
    named = jnp.zeros((OWNERS, TOK), F32)
    for k in range(TOP):
        named += jnp.where(ids_t[k : k + 1, :] == experts, 1.0, 0.0)
    before = ones_where(iota((TOK, TOK), 0) < iota((TOK, TOK), 1))
    rank = dot(named.astype(BF), before)
    return jnp.where(named > 0.0, rank, -1.0)


def each_eight(table):
    spread = ones_where(iota((ROWS, OWNERS), 0) // FIRST == iota((ROWS, OWNERS), 1))
    return dot(spread, table.astype(BF))


def send_first(ids_ref, tokens_ref, out_ref):
    spread = each_eight(places(ids_ref[...]))
    place = iota((ROWS, TOK), 0) % FIRST
    chosen = ones_where(spread == place.astype(F32))
    out_ref[...] = dot(chosen, tokens_ref[...]).astype(BF)


def send_second(ids_ref, flat_ref, tokens_ref, grads_ref, out_ref):
    table = places(ids_ref[...])
    width = SHARE // 4
    spread = each_eight(table)
    row = iota((ROWS, TOK), 0)
    wanted = (FIRST + (row % 8) // 4).astype(F32)
    rows = jnp.zeros((ROWS, width), F32)
    for b in range(4):
        chosen = ones_where((spread == wanted) & (row % 4 == b))
        rows += dot(chosen, tokens_ref[:, b * width : (b + 1) * width])
    out_ref[:, :width] = rows.astype(BF)

    pairs = TOK * TOP
    widen = ones_where(iota((TOK, pairs), 1) // TOP == iota((TOK, pairs), 0))
    ranks = dot(table.astype(BF), widen)
    named = flat_ref[...] == iota((OWNERS, pairs), 0)
    pair_table = jnp.where(named, ranks, -1.0).astype(BF)
    source, lane = iota((UNITS, width), 0), iota((UNITS, width), 1)
    grads = grads_ref[...]
    main = dot(grads, ones_where(source == lane)).astype(BF)
    tails = [
        dot(grads, ones_where((source // 64 == b) & (lane == 192 + source % 64))).astype(BF)
        for b in range(3)
    ]
    block = 256
    for start in range(0, ROWS, block):
        spread = dot(
            ones_where(
                (iota((block, OWNERS), 0) + start) // FIRST == iota((block, OWNERS), 1)
            ),
            pair_table,
        )
        row = iota((block, pairs), 0)
        total = dot(ones_where(spread == (row % 8).astype(F32)), main)
        late = spread == (FIRST + (row % 8) // 4).astype(F32)
        for b in range(3):
            total += dot(ones_where(late & (row % 4 == b)), tails[b])
        out_ref[start : start + block, width:] = total.astype(BF)


def stack_weights(pos_ref, probes_ref, w0, w1, w2, w3, out_ref):
    x = pos_ref[0]
    for k, w in enumerate((w0, w1, w2, w3)):
        block = lax.rem(x - k + REPS, REPS)
        out_ref[pl.ds(pl.multiple_of(block * UNITS, UNITS), UNITS), :] = w[...]
    out_ref[FFW:, :] = probes_ref[...]


def first_products(pos_ref, rows_ref, weights_ref, *outs):
    x = pos_ref[0]
    for k, out in enumerate(outs):
        q = lax.rem(x + k, REPS)
        rows = rows_ref[pl.ds(pl.multiple_of(q * QUARTER, QUARTER), QUARTER), :]
        out[...] = dot(weights_ref[...], rows, NT)


def second_products(pos_ref, got_ref, weights_ref, extra_ref, *outs):
    x = pos_ref[0]
    width = SHARE // 4
    target, source = iota((EXTRA_ROWS, ROWS), 0), iota((EXTRA_ROWS, ROWS), 1)
    got = got_ref[:, :width]
    for b in range(4):
        extra_ref[:, b * width : (b + 1) * width] = dot(
            ones_where(source == 4 * target + b), got
        ).astype(BF)
    blank = jnp.zeros((EXTRA_QUARTER, SHARE), BF)
    for k, out in enumerate(outs):
        q = lax.rem(x + k, REPS)
        rows = extra_ref[
            pl.ds(pl.multiple_of(q * EXTRA_QUARTER, EXTRA_QUARTER), EXTRA_QUARTER), :
        ]
        low = dot(weights_ref[:HALF, :], jnp.concatenate([rows, blank], 0), NT)
        high = dot(weights_ref[HALF:, :], jnp.concatenate([blank, rows], 0), NT)
        out[:HALF, :] = (low + high).astype(BF)
        at = pl.ds(pl.multiple_of(q * QUARTER, QUARTER), QUARTER)
        out[HALF : HALF + QUARTER, :] = got_ref[at, width : width + 128]
        out[HALF + QUARTER :, :] = got_ref[at, width + 128 : width + 256]


def gate_part(pos_ref, inverse_ref, grad_probes_ref, *refs):
    firsts, seconds, outs = refs[:4], refs[4:8], refs[8:12]
    grads_ref, sketch_ref = refs[12], refs[13]
    x = pos_ref[0]
    same = ones_where(iota((128, 128), 0) == iota((128, 128), 1))
    picked, lane = iota((QUARTER, 128), 0), iota((QUARTER, 128), 1)
    for k, second in enumerate(seconds):
        base = lax.rem(x - k + REPS, REPS) * UNITS
        low = dot(same, second[HALF : HALF + QUARTER, :], NT)
        high = dot(same, second[HALF + QUARTER :, :], NT)
        grads_ref[pl.ds(pl.multiple_of(base, 64), 128), :QUARTER] = low
        grads_ref[pl.ds(pl.multiple_of(base + 128, 64), 64), :QUARTER] = high[:64]
        tail = high[64:].astype(BF)
        for b in range(3):
            pick = ones_where((picked == 4 * lane + b) & (lane < EXTRA_QUARTER))
            grads_ref[pl.ds(pl.multiple_of(base + 64 * b, 64), 64), QUARTER:] = dot(tail, pick)
    first = firsts[0][...] + firsts[1][...] + firsts[2][...] + firsts[3][...]
    second = (
        seconds[0][:HALF, :].astype(F32)
        + seconds[1][:HALF, :].astype(F32)
        + seconds[2][:HALF, :].astype(F32)
        + seconds[3][:HALF, :].astype(F32)
    )
    turned = pltpu.roll(second, EXTRA_QUARTER, 1)
    late = jnp.concatenate([second, turned[: FFW - HALF]], 0)
    gate = jnp.concatenate([first[:FFW], late], 1)
    s = 1.0 / (1.0 + jnp.exp(-gate))
    gate_grad = (grads_ref[...] * (s * (1.0 + gate * (1.0 - s)))).astype(BF)
    projected = dot(grad_probes_ref[...], gate_grad).astype(BF)
    sketch_ref[...] = dot(gate_grad, projected, NT) * inverse_ref[0]
    rows = first[FFW:].astype(BF).astype(F32)
    rows_late = jnp.where(
        iota((R, 128), 1) < EXTRA_QUARTER, turned[FFW - HALF :], 0.0
    ).astype(BF).astype(F32)
    for k, out in enumerate(outs):
        base = lax.rem(x + k, REPS) * UNITS
        out[:UNITS, :] = sketch_ref[pl.ds(pl.multiple_of(base, UNITS), UNITS), :]
        out[UNITS : UNITS + R, :] = rows[:, :128]
        out[UNITS + R : UNITS + 2 * R, :] = rows[:, 128:]
        out[UNITS + 2 * R :, :] = rows_late


def finish(pos_ref, inverse_ref, rows_ref, extra_ref, q0, q1, q2, q3, input_ref, grad_ref):
    x = pos_ref[0]
    grad_ref[...] = (q0[:UNITS] + q1[:UNITS]) + (q2[:UNITS] + q3[:UNITS])
    total = jnp.zeros((R, SHARE), F32)
    for k, got in enumerate((q0, q1, q2, q3)):
        q = lax.rem(x - k + REPS, REPS)
        start = pl.multiple_of(q * QUARTER, QUARTER)
        rows = rows_ref[pl.ds(start, QUARTER), :]
        low = got[UNITS : UNITS + R, :].astype(BF)
        high = got[UNITS + R : UNITS + 2 * R, :].astype(BF)
        total += dot(jnp.concatenate([low, high], 1), rows)
        late = got[UNITS + 2 * R :, :].astype(BF)[:, :EXTRA_QUARTER]
        start = pl.multiple_of(q * EXTRA_QUARTER, EXTRA_QUARTER)
        total += dot(late, extra_ref[pl.ds(start, EXTRA_QUARTER), :])
    input_ref[...] = (total * inverse_ref[0]).T


def shifted(blocks):
    got = [blocks[0]]
    for k in range(1, REPS):
        got.append(lax.ppermute(blocks[k], "rep", [(i, (i + k) % REPS) for i in range(REPS)]))
    return got


def local(tokens, expert_ids, hidden_grads, gate_weight, probes, grad_probes, window_counts):
    sds = jax.ShapeDtypeStruct
    x = lax.axis_index("rep")
    pos = x.astype(jnp.int32).reshape(1)
    inverse = 1.0 / window_counts.astype(F32)
    ids_t = expert_ids.T
    flat_ids = expert_ids.reshape(1, TOK * TOP)
    columns = lax.dynamic_slice_in_dim(tokens, x * SHARE, SHARE, 1)

    out_first = kernel_call(
        send_first, sds((ROWS, SHARE), BF), [VM] * 2, 2 * ROWS * TOK * SHARE, 3 << 20
    )(ids_t, columns)
    rows = lax.all_to_all(
        out_first.reshape(OWNERS, FIRST, SHARE), "ep", split_axis=0, concat_axis=0, tiled=True
    ).reshape(ROWS, SHARE)

    weights = shifted(
        [
            lax.dynamic_slice_in_dim(gate_weight[0], lax.rem(x + k, REPS) * SHARE, SHARE, 1)
            for k in range(REPS)
        ]
    )
    probe_columns = lax.dynamic_slice_in_dim(probes, x * SHARE, SHARE, 1)
    stacked = kernel_call(
        stack_weights, sds((STACK, SHARE), BF), [SM] + [VM] * 5, 1000, 4 << 20
    )(pos, probe_columns, *weights)

    out_second = kernel_call(
        send_second, sds((ROWS, 512), BF), [VM] * 4, 3 << 30, 4 << 20
    )(ids_t, flat_ids, columns, hidden_grads.reshape(TOK * TOP, UNITS))

    firsts = kernel_call(
        first_products,
        [sds((STACK, QUARTER), F32)] * REPS,
        [SM] + [VM] * 2,
        2 * ROWS * SHARE * STACK,
        8 << 20,
    )(pos, rows, stacked)
    firsts = shifted(firsts)

    got = lax.all_to_all(
        out_second.reshape(OWNERS, FIRST, 512), "ep", split_axis=0, concat_axis=0, tiled=True
    ).reshape(ROWS, 512)
    extra, *seconds = kernel_call(
        second_products,
        [sds((EXTRA_ROWS, SHARE), BF)] + [sds((HALF + 2 * QUARTER, 128), BF)] * REPS,
        [SM] + [VM] * 2,
        2 << 30,
        6 << 20,
    )(pos, got, stacked)
    seconds = shifted(seconds)

    thirds = kernel_call(
        gate_part,
        [sds((UNITS + 3 * R, 128), F32)] * REPS,
        [SM] * 2 + [VM] * 9,
        1 << 30,
        8 << 20,
        [pltpu.VMEM((FFW, QUARTER + 128), F32), pltpu.VMEM((FFW, R), F32)],
    )(pos, inverse, grad_probes, *firsts, *seconds)
    thirds = shifted(thirds)

    input_sketch, grad_sketch = kernel_call(
        finish,
        [sds((SHARE, R), F32), sds((UNITS, R), F32)],
        [SM] * 2 + [VM] * 6,
        1 << 29,
        5 << 20,
    )(pos, inverse, rows, extra, *thirds)
    return input_sketch[None], grad_sketch[None]


def solution(mesh):
    placed = (
        P("ep", None),
        P("ep", None),
        P("ep", None, "rep"),
        P("ep", "rep", None),
        P(),
        P(),
        P("ep"),
    )
    return jax.shard_map(
        local,
        mesh=mesh,
        in_specs=placed,
        out_specs=(P("ep", "rep", None), P("ep", "rep", None)),
        check_vma=False,
    )
```

```python
import jax
import jax.numpy as jnp
from jax import lax
from jax.experimental import pallas as pl
from jax.experimental.pallas import tpu as pltpu
from jax.sharding import PartitionSpec as P

OWNERS = 128
REPS = 4
TOK = 128
TOP = 8
D = 4096
SHARE = D // REPS
FFW = 768
UNITS = FFW // REPS
R = 128
FIRST = 8
FOLD = 8
ROWS = OWNERS * FOLD
SLOTS = OWNERS * 2
STRIP = SHARE // 4

BF = jnp.bfloat16
F32 = jnp.float32
NT = (((1,), (1,)), ((), ()))
NN = (((1,), (0,)), ((), ()))

VM = pl.BlockSpec(memory_space=pltpu.VMEM)
SM = pl.BlockSpec(memory_space=pltpu.SMEM)


def dot(a, b, dims=NN):
    return lax.dot_general(a, b, dims, preferred_element_type=F32)


def iota(shape, axis):
    return lax.broadcasted_iota(jnp.int32, shape, axis)


def ones_where(mask):
    return jnp.where(mask, 1.0, 0.0).astype(BF)


def kernel_call(body, out_shape, in_specs, flops, bytes_accessed, scratch=()):
    return pl.pallas_call(
        body,
        out_shape=out_shape,
        in_specs=in_specs,
        out_specs=jax.tree.map(lambda _: VM, out_shape),
        scratch_shapes=list(scratch),
        compiler_params=pltpu.CompilerParams(vmem_limit_bytes=50 * 1024 * 1024),
        cost_estimate=pl.CostEstimate(
            flops=flops, bytes_accessed=bytes_accessed, transcendentals=0
        ),
    )


def places(ids_t):
    experts = iota((OWNERS, TOK), 0)
    named = jnp.zeros((OWNERS, TOK), F32)
    for k in range(TOP):
        named += jnp.where(ids_t[k : k + 1, :] == experts, 1.0, 0.0)
    before = ones_where(iota((TOK, TOK), 0) < iota((TOK, TOK), 1))
    rank = dot(named.astype(BF), before)
    return jnp.where(named > 0.0, rank, -1.0)


def spread(table, times):
    shape = (OWNERS * times, OWNERS)
    return dot(ones_where(iota(shape, 0) // times == iota(shape, 1)), table.astype(BF))


def send_rows(pos_ref, ids_ref, tokens_ref, out_ref):
    x = pos_ref[0]
    table = spread(places(ids_ref[...]), FOLD)
    row = iota((ROWS, TOK), 0)
    half, quarter = row % 8 // 4, row % 4
    whole = table == (2 * x + half).astype(F32)
    picks = jnp.concatenate([ones_where(whole & (quarter == b)) for b in range(4)], 1)
    parts = jnp.concatenate([tokens_ref[:, b * SHARE : (b + 1) * SHARE] for b in range(4)], 0)
    out_ref[:, :SHARE] = dot(picks, parts).astype(BF)
    cut = table == (FIRST + half).astype(F32)
    picks = jnp.concatenate([ones_where(cut & (quarter == b)) for b in range(4)], 1)
    parts = jnp.concatenate(
        [
            tokens_ref[:, pl.ds(pl.multiple_of(x * SHARE + b * STRIP, STRIP), STRIP)]
            for b in range(4)
        ],
        0,
    )
    out_ref[:, SHARE:] = dot(picks, parts).astype(BF)


def pick_grads(pos_ref, ids_ref, flat_ref, grads_ref, tail_ref, *outs):
    x = pos_ref[0]
    pairs = TOK * TOP
    widen = ones_where(iota((TOK, pairs), 1) // TOP == iota((TOK, pairs), 0))
    ranks = dot(places(ids_ref[...]).astype(BF), widen)
    named = flat_ref[...] == iota((OWNERS, pairs), 0)
    table = jnp.where(named, ranks, -1.0)
    source, lane = iota((UNITS, STRIP), 0), iota((UNITS, STRIP), 1)
    grads = grads_ref[...]
    main = dot(grads, ones_where(source == lane)).astype(BF)
    twice = spread(table, 2)
    second = iota((SLOTS, pairs), 0) % 2
    for k, out in enumerate(outs):
        place = 2 * lax.rem(x + k, REPS) + second
        out[...] = dot(ones_where(twice == place.astype(F32)), main).astype(BF)
    tails = [
        dot(grads, ones_where((source // 64 == b) & (lane == 192 + source % 64))).astype(BF)
        for b in range(3)
    ]
    block = 256
    for start in range(0, ROWS, block):
        shape = (block, OWNERS)
        owner = (iota(shape, 0) + start) // FOLD == iota(shape, 1)
        eight = dot(ones_where(owner), table.astype(BF))
        row = iota((block, pairs), 0)
        late = eight == (FIRST + row % 8 // 4).astype(F32)
        total = jnp.zeros((block, STRIP), F32)
        for b in range(3):
            total += dot(ones_where(late & (row % 4 == b)), tails[b])
        tail_ref[start : start + block, :] = total.astype(BF)


def fold_grads(pos_ref, tail_ref, g0, g1, g2, g3, out_ref):
    x = pos_ref[0]
    row, column = iota((ROWS, SLOTS), 0), iota((ROWS, SLOTS), 1)
    total = tail_ref[...].astype(F32)
    for k, got in enumerate((g0, g1, g2, g3)):
        unit = lax.rem(x - k + REPS, REPS)
        total += dot(ones_where((row // 4 == column) & (row % 4 == unit)), got[...])
    out_ref[...] = total.astype(BF)


def products(
    pos_ref, rows_ref, probes_ref, own_ref, left_ref, right_ref, top_ref, bottom_ref,
    gate_ref, cut_ref, o0, o1, o2, o3, i0, i1, i2, i3, whole_ref, partial_ref,
):
    x = pos_ref[0]
    target, source = iota((SLOTS, ROWS), 0), iota((SLOTS, ROWS), 1)
    for b in range(4):
        got = dot(ones_where(source == 4 * target + b), rows_ref[...]).astype(BF)
        whole_ref[:, b * SHARE : (b + 1) * SHARE] = got[:, :SHARE]
        cut_ref[:, b * STRIP : (b + 1) * STRIP] = got[:, SHARE:]
    whole, cut = whole_ref[...], cut_ref[...]
    share = pl.ds(pl.multiple_of(x * SHARE, SHARE), SHARE)
    half = UNITS // 2
    for w, k, start, size, out in (
        (own_ref, 0, 0, UNITS, o0),
        (right_ref, 1, 0, UNITS, o1),
        (top_ref, 2, 0, half, o2),
        (bottom_ref, 2, half, half, o2),
        (left_ref, 3, 0, UNITS, o3),
    ):
        base = lax.rem(x + k, REPS) * UNITS + start
        gate_ref[pl.ds(pl.multiple_of(base, half), size), :] = dot(w[...], whole, NT)
        out[start : start + size, :] = dot(w[:, share], cut, NT).astype(out.dtype)
    cut_projected = dot(probes_ref[:, share], cut, NT)
    for out in (o0, o1, o2, o3):
        out[UNITS:, :] = cut_projected.astype(out.dtype)
    projected = dot(probes_ref[...], whole, NT).astype(BF)
    partial_ref[...] = dot(projected, whole)
    for k, out in enumerate((i0, i1, i2, i3)):
        base = lax.rem(x + k, REPS) * SHARE
        out[...] = partial_ref[:, pl.ds(pl.multiple_of(base, SHARE), SHARE)].astype(out.dtype)


def finish_input(inverse_ref, cut_ref, s0, s1, s2, s3, i0, i1, i2, i3, out_ref):
    projected = s0[UNITS:, :] + (
        s1[UNITS:, :].astype(F32) + s2[UNITS:, :].astype(F32) + s3[UNITS:, :].astype(F32)
    )
    total = dot(projected.astype(BF), cut_ref[...])
    total += i0[...] + (i1[...].astype(F32) + i2[...].astype(F32) + i3[...].astype(F32))
    out_ref[...] = (total * inverse_ref[0]).T


def gate_gradient(gate, grads):
    s = 1.0 / (1.0 + jnp.exp(-gate))
    return (grads * (s * (1.0 + gate * (1.0 - s)))).astype(BF)


def gate_part(
    pos_ref, grad_probes_ref, probe_share_ref, gate_ref, got_ref, s0, s1, s2, s3,
    cut_grad_ref, t0, t1, t2, t3, grads_ref, sketch_ref,
):
    x = pos_ref[0]
    same = ones_where(iota((STRIP, STRIP), 0) == iota((STRIP, STRIP), 1))
    turned = dot(same, got_ref[...], NT).astype(BF)
    source, target = iota((ROWS, SLOTS), 0), iota((ROWS, SLOTS), 1)
    cut_parts = []
    for b in range(4):
        taken = dot(turned, ones_where(source == 4 * target + b))
        grads_ref[b * UNITS : (b + 1) * UNITS, :] = taken[:UNITS]
        if b < 3:
            cut_parts.append(taken[UNITS:])
    cut_gate = s0[:UNITS, :] + (
        s1[:UNITS, :].astype(F32) + s2[:UNITS, :].astype(F32) + s3[:UNITS, :].astype(F32)
    )
    cut_grad = gate_gradient(cut_gate, jnp.concatenate(cut_parts, 0))
    cut_grad_ref[...] = cut_grad
    cut_projected = dot(probe_share_ref[...], cut_grad)
    gate_grad = gate_gradient(gate_ref[...], grads_ref[...])
    projected = dot(grad_probes_ref[...], gate_grad).astype(BF)
    sketch_ref[...] = dot(gate_grad, projected, NT)
    for k, out in enumerate((t0, t1, t2, t3)):
        base = lax.rem(x + k, REPS) * UNITS
        sketch = sketch_ref[pl.ds(pl.multiple_of(base, UNITS), UNITS), :]
        out[:UNITS, :] = sketch.astype(out.dtype)
        out[UNITS : UNITS + R, :] = cut_projected[:, :128].astype(out.dtype)
        out[UNITS + R :, :] = cut_projected[:, 128:].astype(out.dtype)


def finish_grad(inverse_ref, cut_grad_ref, t0, t1, t2, t3, out_ref):
    total = t0[...] + (t1[...].astype(F32) + t2[...].astype(F32) + t3[...].astype(F32))
    projected = total[UNITS:].astype(BF)
    sketch = total[:UNITS] + dot(cut_grad_ref[:, :128], projected[:R], NT)
    sketch += dot(cut_grad_ref[:, 128:], projected[R:], NT)
    out_ref[...] = sketch * inverse_ref[0]


def shift(block, k):
    return lax.ppermute(block, "rep", [(i, (i + k) % REPS) for i in range(REPS)])


def shifted(blocks):
    return [blocks[0]] + [shift(blocks[k], k) for k in range(1, REPS)]


def to_owners(rows):
    width = rows.shape[1]
    rows = rows.reshape(OWNERS, FOLD, width)
    return lax.all_to_all(rows, "ep", split_axis=0, concat_axis=0, tiled=True).reshape(ROWS, width)


def local(tokens, expert_ids, hidden_grads, gate_weight, probes, grad_probes, window_counts):
    sds = jax.ShapeDtypeStruct
    x = lax.axis_index("rep")
    pos = x.astype(jnp.int32).reshape(1)
    inverse = 1.0 / window_counts.astype(F32)
    ids_t = expert_ids.T
    flat_ids = expert_ids.reshape(1, TOK * TOP)
    probe_share = lax.dynamic_slice_in_dim(grad_probes, x * UNITS, UNITS, 1)

    out_rows = kernel_call(
        send_rows, sds((ROWS, SHARE + STRIP), BF), [SM] + [VM] * 2, 1 << 31, 4 << 20
    )(pos, ids_t, tokens)
    rows = to_owners(out_rows)

    own = gate_weight[0]
    own, _ = lax.optimization_barrier((own, out_rows))
    left, right = shift(own, 1), shift(own, REPS - 1)
    top = shift(left[: UNITS // 2], 1)
    bottom = shift(right[UNITS // 2 :], REPS - 1)

    tail, *picked = kernel_call(
        pick_grads,
        [sds((ROWS, STRIP), BF)] + [sds((SLOTS, STRIP), BF)] * REPS,
        [SM] + [VM] * 3,
        4 << 30,
        3 << 20,
    )(pos, ids_t, flat_ids, hidden_grads.reshape(TOK * TOP, UNITS))
    picked = shifted(picked)
    out_grads = kernel_call(
        fold_grads, sds((ROWS, STRIP), BF), [SM] + [VM] * 5, 1 << 29, 3 << 20
    )(pos, tail, *picked)
    out_grads, left, right, top, bottom = lax.optimization_barrier(
        (out_grads, left, right, top, bottom)
    )
    got = to_owners(out_grads)

    kinds = [F32, BF, BF, BF]
    gate, cut, *sums = kernel_call(
        products,
        [sds((FFW, SLOTS), F32), sds((SLOTS, SHARE), BF)]
        + [sds((UNITS + R, SLOTS), kind) for kind in kinds]
        + [sds((R, SHARE), kind) for kind in kinds],
        [SM] + [VM] * 7,
        6 << 30,
        14 << 20,
        [pltpu.VMEM((SLOTS, D), BF), pltpu.VMEM((R, D), F32)],
    )(pos, rows, probes, own, left, right, top, bottom)
    cut_sums = shifted(sums[:REPS])
    input_sums = shifted(sums[REPS:])

    cut_grad, *sketches = kernel_call(
        gate_part,
        [sds((UNITS, SLOTS), BF)] + [sds((UNITS + 2 * R, 128), kind) for kind in kinds],
        [SM] + [VM] * 8,
        2 << 30,
        4 << 20,
        [pltpu.VMEM((FFW, SLOTS), F32), pltpu.VMEM((FFW, R), F32)],
    )(pos, grad_probes, probe_share, gate, got, *cut_sums)
    sketches = shifted(sketches)

    input_sketch = kernel_call(
        finish_input, sds((SHARE, R), F32), [SM] + [VM] * 9, 1 << 28, 4 << 20
    )(inverse, cut, *cut_sums, *input_sums)
    grad_sketch = kernel_call(
        finish_grad, sds((UNITS, R), F32), [SM] + [VM] * 5, 1 << 24, 1 << 20
    )(inverse, cut_grad, *sketches)
    return input_sketch[None], grad_sketch[None]


def solution(mesh):
    placed = (
        P("ep", None),
        P("ep", None),
        P("ep", None, "rep"),
        P("ep", "rep", None),
        P(),
        P(),
        P("ep"),
    )
    return jax.shard_map(
        local,
        mesh=mesh,
        in_specs=placed,
        out_specs=(P("ep", "rep", None), P("ep", "rep", None)),
        check_vma=False,
    )
```

```python
import jax
import jax.numpy as jnp
from jax import lax
from jax.experimental import pallas as pl
from jax.experimental.pallas import tpu as pltpu
from jax.sharding import PartitionSpec as P

OWNERS = 128
REPS = 4
TOK = 128
TOP = 8
D = 4096
SHARE = D // REPS
FFW = 768
UNITS = FFW // REPS
R = 128
FIRST = 8
FOLD = 8
ROWS = OWNERS * FOLD
SLOTS = OWNERS * 2
STRIP = SHARE // 4
LIMIT = 30 * 1024 * 1024

BF = jnp.bfloat16
F32 = jnp.float32
NT = (((1,), (1,)), ((), ()))
NN = (((1,), (0,)), ((), ()))

VM = pl.BlockSpec(memory_space=pltpu.VMEM)
SM = pl.BlockSpec(memory_space=pltpu.SMEM)


def dot(a, b, dims=NN):
    return lax.dot_general(a, b, dims, preferred_element_type=F32)


def iota(shape, axis):
    return lax.broadcasted_iota(jnp.int32, shape, axis)


def ones_where(mask):
    return jnp.where(mask, 1.0, 0.0).astype(BF)


def kernel_call(body, out_shape, in_specs, flops, bytes_accessed, scratch=(), grid=()):
    return pl.pallas_call(
        body,
        grid=grid,
        out_shape=out_shape,
        in_specs=in_specs,
        out_specs=jax.tree.map(lambda _: VM, out_shape),
        scratch_shapes=list(scratch),
        compiler_params=pltpu.CompilerParams(vmem_limit_bytes=LIMIT),
        cost_estimate=pl.CostEstimate(
            flops=flops, bytes_accessed=bytes_accessed, transcendentals=0
        ),
    )


def places(ids_t):
    experts = iota((OWNERS, TOK), 0)
    named = jnp.zeros((OWNERS, TOK), F32)
    for k in range(TOP):
        named += jnp.where(ids_t[k : k + 1, :] == experts, 1.0, 0.0)
    before = ones_where(iota((TOK, TOK), 0) < iota((TOK, TOK), 1))
    rank = dot(named.astype(BF), before)
    return jnp.where(named > 0.0, rank, -1.0)


def spread(table, times):
    shape = (OWNERS * times, OWNERS)
    return dot(ones_where(iota(shape, 0) // times == iota(shape, 1)), table.astype(BF))


def send_rows(pos_ref, ids_ref, tokens_ref, out_ref):
    x = pos_ref[0]
    table = spread(places(ids_ref[...]), FOLD)
    row = iota((ROWS, TOK), 0)
    half, quarter = row % 8 // 4, row % 4
    whole = table == (2 * x + half).astype(F32)
    picks = jnp.concatenate([ones_where(whole & (quarter == b)) for b in range(4)], 1)
    parts = jnp.concatenate([tokens_ref[:, b * SHARE : (b + 1) * SHARE] for b in range(4)], 0)
    out_ref[:, :SHARE] = dot(picks, parts).astype(BF)
    cut = table == (FIRST + half).astype(F32)
    picks = jnp.concatenate([ones_where(cut & (quarter == b)) for b in range(4)], 1)
    parts = jnp.concatenate(
        [
            tokens_ref[:, pl.ds(pl.multiple_of(x * SHARE + b * STRIP, STRIP), STRIP)]
            for b in range(4)
        ],
        0,
    )
    out_ref[:, SHARE:] = dot(picks, parts).astype(BF)


def pick_grads(pos_ref, ids_ref, flat_ref, grads_ref, tail_ref, *outs):
    x = pos_ref[0]
    pairs = TOK * TOP
    widen = ones_where(iota((TOK, pairs), 1) // TOP == iota((TOK, pairs), 0))
    ranks = dot(places(ids_ref[...]).astype(BF), widen)
    named = flat_ref[...] == iota((OWNERS, pairs), 0)
    table = jnp.where(named, ranks, -1.0)
    source, lane = iota((UNITS, STRIP), 0), iota((UNITS, STRIP), 1)
    grads = grads_ref[...]
    main = dot(grads, ones_where(source == lane)).astype(BF)
    twice = spread(table, 2)
    second = iota((SLOTS, pairs), 0) % 2
    for k, out in enumerate(outs):
        place = 2 * lax.rem(x + k, REPS) + second
        out[...] = dot(ones_where(twice == place.astype(F32)), main).astype(BF)
    tails = [
        dot(grads, ones_where((source // 64 == b) & (lane == 192 + source % 64))).astype(BF)
        for b in range(3)
    ]
    block = 256
    for start in range(0, ROWS, block):
        shape = (block, OWNERS)
        owner = (iota(shape, 0) + start) // FOLD == iota(shape, 1)
        eight = dot(ones_where(owner), table.astype(BF))
        row = iota((block, pairs), 0)
        late = eight == (FIRST + row % 8 // 4).astype(F32)
        total = jnp.zeros((block, STRIP), F32)
        for b in range(3):
            total += dot(ones_where(late & (row % 4 == b)), tails[b])
        tail_ref[start : start + block, :] = total.astype(BF)


def fold_grads(pos_ref, tail_ref, g0, g1, g2, g3, out_ref):
    x = pos_ref[0]
    row, column = iota((ROWS, SLOTS), 0), iota((ROWS, SLOTS), 1)
    total = tail_ref[...].astype(F32)
    for k, got in enumerate((g0, g1, g2, g3)):
        unit = lax.rem(x - k + REPS, REPS)
        total += dot(ones_where((row // 4 == column) & (row % 4 == unit)), got[...])
    out_ref[...] = total.astype(BF)


def stack_weights(pos_ref, probes_ref, own_ref, right_ref, top_ref, bottom_ref, left_ref, out_ref):
    x = pos_ref[0]
    half = UNITS // 2
    for w, k, start, size in (
        (own_ref, 0, 0, UNITS),
        (right_ref, 1, 0, UNITS),
        (top_ref, 2, 0, half),
        (bottom_ref, 2, half, half),
        (left_ref, 3, 0, UNITS),
    ):
        base = lax.rem(x + k, REPS) * UNITS + start
        out_ref[pl.ds(pl.multiple_of(base, half), size), :] = w[...]
    out_ref[FFW:, :] = probes_ref[...]


def unfold(source, put):
    shape = (256, 256)
    order = ones_where(iota(shape, 1) == 4 * (iota(shape, 0) % 64) + iota(shape, 0) // 64)
    for g in range(4):
        got = dot(order, source[g * 256 : (g + 1) * 256, :]).astype(BF)
        for b in range(4):
            put(b, slice(g * 64, (g + 1) * 64), got[b * 64 : (b + 1) * 64])


def cut_products(pos_ref, rows_ref, weights_ref, cut_ref, o0, o1, o2, o3):
    x = pos_ref[0]

    def put(b, at, got):
        cut_ref[at, b * STRIP : (b + 1) * STRIP] = got

    unfold(rows_ref, put)
    cut = cut_ref[...]
    projected = dot(weights_ref[FFW:, :], cut, NT)
    for k, out in enumerate((o0, o1, o2, o3)):
        base = lax.rem(x + k, REPS) * UNITS
        weights = weights_ref[pl.ds(pl.multiple_of(base, UNITS), UNITS), :]
        out[:UNITS, :] = dot(weights, cut, NT).astype(out.dtype)
        out[UNITS:, :] = projected.astype(out.dtype)


def whole_products(pos_ref, rows_ref, weights_ref, gate_ref, partial_ref, own_ref, whole_ref, sum_ref):
    x = pos_ref[0]

    def put(b, at, got):
        whole_ref[at, b * SHARE : (b + 1) * SHARE] = got

    unfold(rows_ref, put)
    whole = whole_ref[...]
    both = dot(weights_ref[...], whole, NT)
    gate_ref[...] = both[:FFW]
    sum_ref[...] = dot(both[FFW:].astype(BF), whole)
    partial_ref[...] = sum_ref[...].astype(BF)
    own_ref[...] = sum_ref[:, pl.ds(pl.multiple_of(x * SHARE, SHARE), SHARE)]


def gate_gradient(gate, grads):
    s = 1.0 / (1.0 + jnp.exp(-gate))
    return (grads * (s * (1.0 + gate * (1.0 - s)))).astype(BF)


def gate_part(
    pos_ref, grad_probes_ref, probe_share_ref, gate_ref, partial_ref, got_ref, s0, s1, s2, s3,
    cut_grad_ref, t0, t1, t2, t3, grads_ref, sketch_ref,
):
    x = pos_ref[0]

    def put(b, at, got):
        grads_ref[b * SLOTS + at.start : b * SLOTS + at.stop, :] = got

    unfold(got_ref, put)
    same = ones_where(iota((STRIP, STRIP), 0) == iota((STRIP, STRIP), 1))
    turned = dot(same, grads_ref[...], NT)
    parts = [turned[:, b * SLOTS : (b + 1) * SLOTS] for b in range(4)]
    cut_gate = s0[:UNITS, :] + (
        s1[:UNITS, :].astype(F32) + s2[:UNITS, :].astype(F32) + s3[:UNITS, :].astype(F32)
    )
    cut_grad = gate_gradient(cut_gate, jnp.concatenate([p[UNITS:] for p in parts[:3]], 0))
    cut_grad_ref[...] = cut_grad
    cut_projected = dot(probe_share_ref[...], cut_grad)
    whole = jnp.concatenate([p[:UNITS] for p in parts], 0)
    gate_grad = gate_gradient(gate_ref[...], whole)
    projected = dot(grad_probes_ref[...], gate_grad).astype(BF)
    sketch_ref[...] = dot(gate_grad, projected, NT)
    for k, out in enumerate((t0, t1, t2, t3)):
        base = lax.rem(x + k, REPS) * UNITS
        sketch = sketch_ref[pl.ds(pl.multiple_of(base, UNITS), UNITS), :]
        out[:UNITS, :] = sketch.astype(out.dtype)
        out[UNITS : UNITS + R, :] = cut_projected[:, :128].astype(out.dtype)
        out[UNITS + R : UNITS + 2 * R, :] = cut_projected[:, 128:].astype(out.dtype)
        if k > 0:
            base = lax.rem(x + k, REPS) * SHARE
            for j in range(SHARE // 128):
                start = UNITS + (2 + j) * R
                columns = pl.ds(pl.multiple_of(base + j * 128, 128), 128)
                out[start : start + R, :] = partial_ref[:, columns]


def finish(
    inverse_ref, cut_ref, own_ref, s0, s1, s2, s3, cut_grad_ref, t0, t1, t2, t3,
    input_ref, grad_ref,
):
    inverse = inverse_ref[0]
    others = (t1, t2, t3)
    mixed = UNITS + 2 * R
    total = t0[...] + (
        t1[:mixed, :].astype(F32) + t2[:mixed, :].astype(F32) + t3[:mixed, :].astype(F32)
    )
    projected = total[UNITS:].astype(BF)
    sketch = total[:UNITS] + dot(cut_grad_ref[:, :128], projected[:R], NT)
    sketch += dot(cut_grad_ref[:, 128:], projected[R:], NT)
    grad_ref[...] = sketch * inverse

    projected = s0[UNITS:, :] + (
        s1[UNITS:, :].astype(F32) + s2[UNITS:, :].astype(F32) + s3[UNITS:, :].astype(F32)
    )
    total = own_ref[...] + dot(projected.astype(BF), cut_ref[...])
    for j in range(SHARE // 128):
        start = mixed + j * R
        block = total[:, j * 128 : (j + 1) * 128]
        for other in others:
            block += other[start : start + R, :].astype(F32)
        input_ref[j * 128 : (j + 1) * 128, :] = (block * inverse).T


def shift(block, k):
    return lax.ppermute(block, "rep", [(i, (i + k) % REPS) for i in range(REPS)])


def shifted(blocks):
    return [blocks[0]] + [shift(blocks[k], k) for k in range(1, REPS)]


def to_owners(rows):
    width = rows.shape[1]
    rows = rows.reshape(OWNERS, FOLD, width)
    return lax.all_to_all(rows, "ep", split_axis=0, concat_axis=0, tiled=True).reshape(ROWS, width)


def local(tokens, expert_ids, hidden_grads, gate_weight, probes, grad_probes, window_counts):
    sds = jax.ShapeDtypeStruct
    x = lax.axis_index("rep")
    pos = x.astype(jnp.int32).reshape(1)
    inverse = 1.0 / window_counts.astype(F32)
    ids_t = expert_ids.T
    flat_ids = expert_ids.reshape(1, TOK * TOP)
    probe_share = lax.dynamic_slice_in_dim(grad_probes, x * UNITS, UNITS, 1)

    out_rows = kernel_call(
        send_rows, sds((ROWS, SHARE + STRIP), BF), [SM] + [VM] * 2, 1 << 31, 4 << 20
    )(pos, ids_t, tokens)
    rows = to_owners(out_rows)

    own = gate_weight[0]
    own, _ = lax.optimization_barrier((own, out_rows))
    left, right = shift(own, 1), shift(own, REPS - 1)

    tail, *picked = kernel_call(
        pick_grads,
        [sds((ROWS, STRIP), BF)] + [sds((SLOTS, STRIP), BF)] * REPS,
        [SM] + [VM] * 3,
        4 << 30,
        3 << 20,
    )(pos, ids_t, flat_ids, hidden_grads.reshape(TOK * TOP, UNITS))
    picked = shifted(picked)
    out_grads = kernel_call(
        fold_grads, sds((ROWS, STRIP), BF), [SM] + [VM] * 5, 1 << 29, 3 << 20
    )(pos, tail, *picked)
    out_grads, left, right = lax.optimization_barrier((out_grads, left, right))
    top = shift(left[: UNITS // 2], 1)
    bottom = shift(right[UNITS // 2 :], REPS - 1)
    weights = kernel_call(
        stack_weights, sds((FFW + R, D), BF), [SM] + [VM] * 6, 1000, 14 << 20
    )(pos, probes, own, right, top, bottom, left)
    got = to_owners(out_grads)

    kinds = [F32, BF, BF, BF]
    cut, *cut_sums = pl.pallas_call(
        cut_products,
        out_shape=[sds((SLOTS, SHARE), BF)] + [sds((UNITS + R, SLOTS), kind) for kind in kinds],
        grid_spec=pltpu.PrefetchScalarGridSpec(
            num_scalar_prefetch=1,
            grid=(1,),
            in_specs=[
                pl.BlockSpec((ROWS, STRIP), lambda i, pos: (0, SHARE // STRIP)),
                pl.BlockSpec((FFW + R, SHARE), lambda i, pos: (0, pos[0])),
            ],
            out_specs=[VM] * 5,
        ),
        compiler_params=pltpu.CompilerParams(vmem_limit_bytes=LIMIT),
        cost_estimate=pl.CostEstimate(
            flops=1 << 29, bytes_accessed=4 << 20, transcendentals=0
        ),
    )(pos, rows, weights)
    cut_sums = shifted(cut_sums)
    gate, partial, own_partial = kernel_call(
        whole_products,
        [sds((FFW, SLOTS), F32), sds((R, D), BF), sds((R, SHARE), F32)],
        [SM, pl.BlockSpec((ROWS, SHARE), lambda i: (0, 0)), VM],
        3 << 30,
        14 << 20,
        [pltpu.VMEM((SLOTS, D), BF), pltpu.VMEM((R, D), F32)],
        (1,),
    )(pos, rows, weights)

    mixed = UNITS + 2 * R
    cut_grad, *sums = kernel_call(
        gate_part,
        [sds((UNITS, SLOTS), BF), sds((mixed, 128), F32)]
        + [sds((mixed + SHARE, 128), BF)] * (REPS - 1),
        [SM] + [VM] * 9,
        2 << 30,
        4 << 20,
        [pltpu.VMEM((ROWS, STRIP), BF), pltpu.VMEM((FFW, R), F32)],
    )(pos, grad_probes, probe_share, gate, partial, got, *cut_sums)
    sums = shifted(sums)

    input_sketch, grad_sketch = kernel_call(
        finish,
        [sds((SHARE, R), F32), sds((UNITS, R), F32)],
        [SM] + [VM] * 11,
        1 << 28,
        4 << 20,
    )(inverse, cut, own_partial, *cut_sums, cut_grad, *sums)
    return input_sketch[None], grad_sketch[None]


def solution(mesh):
    placed = (
        P("ep", None),
        P("ep", None),
        P("ep", None, "rep"),
        P("ep", "rep", None),
        P(),
        P(),
        P("ep"),
    )
    return jax.shard_map(
        local,
        mesh=mesh,
        in_specs=placed,
        out_specs=(P("ep", "rep", None), P("ep", "rep", None)),
        check_vma=False,
    )
```

```python
import jax
import jax.numpy as jnp
from jax import lax
from jax.experimental import pallas as pl
from jax.experimental.pallas import tpu as pltpu
from jax.sharding import PartitionSpec as P

OWNERS = 128
PAIRS = OWNERS // 2
REPS = 4
TOK = 128
TOP = 8
D = 4096
HALF = D // 2
SHARE = D // REPS
FFW = 768
UNITS = FFW // REPS
R = 128
FIRST = 8
FOLD = 8
ROWS = OWNERS * FOLD
SLOTS = OWNERS * 2
ALL = SLOTS + 128
STRIP = HALF // FOLD
MIB = 1 << 20

BF = jnp.bfloat16
F32 = jnp.float32
NT = (((1,), (1,)), ((), ()))
NN = (((1,), (0,)), ((), ()))

VM = pl.BlockSpec(memory_space=pltpu.VMEM)
SM = pl.BlockSpec(memory_space=pltpu.SMEM)


def dot(a, b, dims=NN):
    return lax.dot_general(a, b, dims, preferred_element_type=F32)


def iota(shape, axis):
    return lax.broadcasted_iota(jnp.int32, shape, axis)


def ones_where(mask):
    return jnp.where(mask, 1.0, 0.0).astype(BF)


def kernel_call(body, out_shape, in_specs, flops, bytes_accessed, limit, scratch=()):
    return pl.pallas_call(
        body,
        out_shape=out_shape,
        in_specs=in_specs,
        out_specs=jax.tree.map(lambda _: VM, out_shape),
        scratch_shapes=list(scratch),
        compiler_params=pltpu.CompilerParams(vmem_limit_bytes=limit * MIB),
        cost_estimate=pl.CostEstimate(
            flops=flops, bytes_accessed=bytes_accessed, transcendentals=0
        ),
    )


def places(ids_t):
    experts = iota((OWNERS, TOK), 0)
    named = jnp.zeros((OWNERS, TOK), F32)
    for k in range(TOP):
        named += jnp.where(ids_t[k : k + 1, :] == experts, 1.0, 0.0)
    before = ones_where(iota((TOK, TOK), 0) < iota((TOK, TOK), 1))
    rank = dot(named.astype(BF), before)
    return jnp.where(named > 0.0, rank, -1.0)


def pair_places(ids_t):
    pairs = TOK * TOP
    widen = ones_where(iota((TOK, pairs), 1) // TOP == iota((TOK, pairs), 0))
    ranks = dot(places(ids_t).astype(BF), widen)
    ids = dot(ids_t.astype(F32).astype(BF), widen)
    mine = iota((TOP, pairs), 1) % TOP == iota((TOP, pairs), 0)
    flat = jnp.sum(jnp.where(mine, ids, 0.0), axis=0, keepdims=True)
    return jnp.where(flat == iota((OWNERS, pairs), 0).astype(F32), ranks, -1.0)


def spread(table, times):
    shape = (OWNERS * times, OWNERS)
    return dot(ones_where(iota(shape, 0) // times == iota(shape, 1)), table.astype(BF))


def pack_half(pos_ref, ids_ref, tokens_ref, out_ref):
    out_ref[:TOK, :] = tokens_ref[...]
    out_ref[TOK:, :] = jnp.zeros((16, HALF), BF)
    ids = jnp.concatenate([ids_ref[...].astype(F32), jnp.zeros((8, TOK), F32)], 0)
    out_ref[TOK:, :TOK] = ids.astype(BF)


def other_ids(other_ref):
    return other_ref[TOK:, :TOK].astype(F32)[:TOP].astype(jnp.int32)


def send_rows(pos_ref, ids_ref, tokens_ref, other_ref, out_ref, half_ref, half_ids_ref):
    x, c = pos_ref[0], pos_ref[1]
    mine = x // 2 == c
    table = spread(places(ids_ref[...]), FOLD)
    row = iota((ROWS, TOK), 0)
    whole = table == (2 * x + row % 8 // 4).astype(F32)
    picks = jnp.concatenate([ones_where(whole & (row % 4 == b)) for b in range(4)], 1)
    parts = jnp.concatenate([tokens_ref[:, b * SHARE : (b + 1) * SHARE] for b in range(4)], 0)
    out_ref[:, :SHARE] = dot(picks, parts).astype(BF)

    @pl.when(mine)
    def _():
        half_ref[...] = tokens_ref[:, pl.ds(pl.multiple_of(c * HALF, HALF), HALF)]
        half_ids_ref[...] = ids_ref[...]

    @pl.when(jnp.logical_not(mine))
    def _():
        half_ref[...] = other_ref[:TOK, :]
        half_ids_ref[...] = other_ids(other_ref)

    table = spread(places(half_ids_ref[...]), FOLD)
    shared = table == (FIRST + x % 2).astype(F32)
    picks = jnp.concatenate([ones_where(shared & (row % 8 == b)) for b in range(8)], 1)
    parts = jnp.concatenate([half_ref[:, b * STRIP : (b + 1) * STRIP] for b in range(8)], 0)
    out_ref[:, SHARE:] = dot(picks, parts).astype(BF)


def pick_grads(pos_ref, ids_ref, other_ref, grads_ref, other_grads_ref, *outs):
    x, c = pos_ref[0], pos_ref[1]
    pairs = TOK * TOP
    table, other_table = pair_places(ids_ref[...]), pair_places(other_ids(other_ref))
    embed = ones_where(iota((UNITS, 256), 0) == iota((UNITS, 256), 1))
    grads = dot(grads_ref[...], embed).astype(BF)
    other_grads = dot(other_grads_ref[...], embed).astype(BF)
    twice = spread(table, 2)
    second = iota((SLOTS, pairs), 0) % 2
    for k, out in enumerate(outs):
        to = lax.rem(x + k, REPS)
        out[:SLOTS, :] = dot(ones_where(twice == (2 * to + second).astype(F32)), grads).astype(BF)
        shared = FIRST + to % 2
        place = jnp.where(to // 2 == c, shared, -2).astype(F32)
        other_place = jnp.where(to // 2 == c, -2, shared).astype(F32)
        out[SLOTS:, :] = (
            dot(ones_where(table == place), grads)
            + dot(ones_where(other_table == other_place), other_grads)
        ).astype(BF)


def fold_grads(pos_ref, g0, g1, g2, g3, out_ref):
    x, c = pos_ref[0], pos_ref[1]
    row, column = iota((ROWS, SLOTS), 0), iota((ROWS, SLOTS), 1)
    total = jnp.zeros((ROWS, 256), F32)
    for k, got in enumerate((g0, g1, g2, g3)):
        unit = lax.rem(x - k + REPS, REPS)
        total += dot(ones_where((row // 4 == column) & (row % 4 == unit)), got[:SLOTS, :])
        for u in range(3):
            at = jnp.where(unit // 2 == c, unit % 2 * 3 + u, -1)
            source, lane = iota((256, 256), 0), iota((256, 256), 1)
            move = ones_where((source // 64 == u) & (lane == UNITS + source % 64))
            moved = dot(got[SLOTS:, :], move).astype(BF)
            row5, column5 = iota((ROWS, OWNERS), 0), iota((ROWS, OWNERS), 1)
            total += dot(ones_where((row5 // 8 == column5) & (row5 % 8 == at)), moved)
    out_ref[...] = total.astype(BF)


def regroup(source, many, put):
    size = 256 // many
    shape = (256, 256)
    to = iota(shape, 0)
    order = ones_where(iota(shape, 1) == many * (to % size) + to // size)
    for g in range(ROWS // 256):
        got = dot(order, source(slice(g * 256, (g + 1) * 256))).astype(BF)
        for p in range(many):
            put(p, slice(g * size, (g + 1) * size), got[p * size : (p + 1) * size])


def products(
    pos_ref, rows_ref, probes_ref, own_ref, right_ref, top_ref, bottom_ref, left_ref,
    gate_ref, i0, i1, i2, i3, rows_all_ref, sum_ref,
):
    x = pos_ref[0]

    def put_whole(p, at, got):
        rows_all_ref[at, p * SHARE : (p + 1) * SHARE] = got

    def put_shared(p, at, got):
        rows_all_ref[SLOTS + at.start : SLOTS + at.stop, p * STRIP : (p + 1) * STRIP] = got

    regroup(lambda at: rows_ref[at, :SHARE], 4, put_whole)
    regroup(lambda at: rows_ref[at, SHARE:], 16, put_shared)
    rows_all_ref[SLOTS + PAIRS :, :] = jnp.zeros((ALL - SLOTS - PAIRS, D), BF)
    rows = rows_all_ref[...]
    projected = dot(probes_ref[...], rows, NT).astype(BF)
    sum_ref[...] = dot(projected, rows)
    for k, out in enumerate((i0, i1, i2, i3)):
        base = lax.rem(x + k, REPS) * SHARE
        out[...] = sum_ref[:, pl.ds(pl.multiple_of(base, SHARE), SHARE)].astype(out.dtype)
    half = UNITS // 2
    for w, k, start, size in (
        (own_ref, 0, 0, UNITS),
        (right_ref, 1, 0, UNITS),
        (top_ref, 2, 0, half),
        (bottom_ref, 2, half, half),
        (left_ref, 3, 0, UNITS),
    ):
        base = lax.rem(x + k, REPS) * UNITS + start
        gate_ref[pl.ds(pl.multiple_of(base, half), size), :] = dot(w[...], rows, NT)


def gate_part(
    pos_ref, grad_probes_ref, gate_ref, got_ref, t0, t1, t2, t3,
    whole_ref, shared_ref, sketch_ref,
):
    x = pos_ref[0]

    def put_whole(p, at, got):
        whole_ref[p * SLOTS + at.start : p * SLOTS + at.stop, :] = got

    def put_shared(p, at, got):
        shared_ref[p * PAIRS + at.start : p * PAIRS + at.stop, :] = got

    regroup(lambda at: got_ref[at, :], 4, put_whole)
    regroup(lambda at: got_ref[at, :], 16, put_shared)
    same = ones_where(iota((UNITS, 256), 0) == iota((UNITS, 256), 1))
    whole = dot(same, whole_ref[...], NT)
    last = ones_where(iota((64, 256), 0) + UNITS == iota((64, 256), 1))
    shared = dot(last, shared_ref[...], NT)
    turned = pltpu.roll(shared, ROWS - PAIRS, 1)
    parts = []
    for p in (0, 1, 2, 3, 4, 5, 8, 9, 10, 11, 12, 13):
        at = p // 2 * 128
        parts.append((turned if p % 2 else shared)[:, at : at + 128])
    late = jnp.concatenate(parts, 0)
    late = jnp.where(iota((FFW, 128), 1) < PAIRS, late, 0.0)
    early = jnp.concatenate([whole[:, b * SLOTS : (b + 1) * SLOTS] for b in range(4)], 0)
    grads = jnp.concatenate([early, late], 1)
    gate = gate_ref[...]
    s = 1.0 / (1.0 + jnp.exp(-gate))
    gate_grad = (grads * (s * (1.0 + gate * (1.0 - s)))).astype(BF)
    projected = dot(grad_probes_ref[...], gate_grad).astype(BF)
    sketch_ref[...] = dot(gate_grad, projected, NT)
    for k, out in enumerate((t0, t1, t2, t3)):
        base = lax.rem(x + k, REPS) * UNITS
        out[...] = sketch_ref[pl.ds(pl.multiple_of(base, UNITS), UNITS), :].astype(out.dtype)


def finish_input(inverse_ref, i0, i1, i2, i3, out_ref):
    total = i0[...] + (i1[...].astype(F32) + i2[...].astype(F32) + i3[...].astype(F32))
    out_ref[...] = (total * inverse_ref[0]).T


def finish_grad(inverse_ref, t0, t1, t2, t3, out_ref):
    total = t0[...] + (t1[...].astype(F32) + t2[...].astype(F32) + t3[...].astype(F32))
    out_ref[...] = total * inverse_ref[0]


def shift(block, k):
    return lax.ppermute(block, "rep", [(i, (i + k) % REPS) for i in range(REPS)])


def shifted(blocks):
    return [blocks[0]] + [shift(blocks[k], k) for k in range(1, REPS)]


def swap(block):
    return lax.ppermute(block, "ep", [(i, i ^ 1) for i in range(OWNERS)])


def to_owners(rows):
    width = rows.shape[1]
    rows = rows.reshape(OWNERS, FOLD, width)
    return lax.all_to_all(rows, "ep", split_axis=0, concat_axis=0, tiled=True).reshape(ROWS, width)


def local(tokens, expert_ids, hidden_grads, gate_weight, probes, grad_probes, window_counts):
    sds = jax.ShapeDtypeStruct
    pos = jnp.stack([lax.axis_index("rep"), lax.axis_index("ep") % 2]).astype(jnp.int32)
    inverse = 1.0 / window_counts.astype(F32)
    ids_t = expert_ids.T

    packed = pl.pallas_call(
        pack_half,
        out_shape=sds((TOK + 16, HALF), BF),
        grid_spec=pltpu.PrefetchScalarGridSpec(
            num_scalar_prefetch=1,
            grid=(1,),
            in_specs=[VM, pl.BlockSpec((TOK, HALF), lambda i, pos: (0, 1 - pos[1]))],
            out_specs=VM,
        ),
        compiler_params=pltpu.CompilerParams(vmem_limit_bytes=6 * MIB),
        cost_estimate=pl.CostEstimate(flops=1000, bytes_accessed=MIB, transcendentals=0),
    )(pos, ids_t, tokens)
    other = swap(packed)
    out_rows = kernel_call(
        send_rows,
        sds((ROWS, SHARE + STRIP), BF),
        [SM] + [VM] * 3,
        1 << 31,
        5 * MIB,
        20,
        [pltpu.VMEM((TOK, HALF), BF), pltpu.VMEM((TOP, TOK), jnp.int32)],
    )(pos, ids_t, tokens, other)
    rows = to_owners(out_rows)

    own, grads = gate_weight[0], hidden_grads.reshape(TOK * TOP, UNITS)
    own, grads, _ = lax.optimization_barrier((own, grads, out_rows))
    left, right = shift(own, 1), shift(own, REPS - 1)
    other_grads = swap(grads)
    picked = kernel_call(
        pick_grads, [sds((SLOTS + OWNERS, 256), BF)] * REPS, [SM] + [VM] * 4, 5 << 30, 3 * MIB, 20
    )(pos, ids_t, other, grads, other_grads)
    out_grads = kernel_call(
        fold_grads, sds((ROWS, 256), BF), [SM] + [VM] * 4, 1 << 31, 3 * MIB, 12
    )(pos, *shifted(picked))
    out_grads, left, right = lax.optimization_barrier((out_grads, left, right))
    top = shift(left[: UNITS // 2], 1)
    bottom = shift(right[UNITS // 2 :], REPS - 1)
    got = to_owners(out_grads)

    kinds = [F32, BF, BF, BF]
    gate, *inputs = kernel_call(
        products,
        [sds((FFW, ALL), F32)] + [sds((R, SHARE), kind) for kind in kinds],
        [SM] + [VM] * 7,
        4 << 30,
        12 * MIB,
        16,
        [pltpu.VMEM((ALL, D), BF), pltpu.VMEM((R, D), F32)],
    )(pos, rows, probes, own, right, top, bottom, left)
    inputs = shifted(inputs)

    sketches = kernel_call(
        gate_part,
        [sds((UNITS, R), kind) for kind in kinds],
        [SM] + [VM] * 3,
        1 << 30,
        3 * MIB,
        14,
        [pltpu.VMEM((ROWS, 256), BF), pltpu.VMEM((ROWS, 256), BF), pltpu.VMEM((FFW, R), F32)],
    )(pos, grad_probes, gate, got)
    sketches = shifted(sketches)

    input_sketch = kernel_call(
        finish_input, sds((SHARE, R), F32), [SM] + [VM] * 4, 1 << 20, 2 * MIB, 6
    )(inverse, *inputs)
    grad_sketch = kernel_call(
        finish_grad, sds((UNITS, R), F32), [SM] + [VM] * 4, 1 << 18, MIB // 4, 4
    )(inverse, *sketches)
    return input_sketch[None], grad_sketch[None]


def solution(mesh):
    placed = (
        P("ep", None),
        P("ep", None),
        P("ep", None, "rep"),
        P("ep", "rep", None),
        P(),
        P(),
        P("ep"),
    )
    return jax.shard_map(
        local,
        mesh=mesh,
        in_specs=placed,
        out_specs=(P("ep", "rep", None), P("ep", "rep", None)),
        check_vma=False,
    )
```

```python
import jax
import jax.numpy as jnp
from jax import lax
from jax.experimental import pallas as pl
from jax.experimental.pallas import tpu as pltpu
from jax.sharding import PartitionSpec as P

OWNERS = 128
PAIRS = OWNERS // 2
REPS = 4
TOK = 128
TOP = 8
D = 4096
HALF = D // 2
SHARE = D // REPS
FFW = 768
UNITS = FFW // REPS
R = 128
FIRST = 8
FOLD = 8
ROWS = OWNERS * FOLD
SLOTS = OWNERS * 2
ALL = SLOTS + 128
STRIP = HALF // FOLD
MIB = 1 << 20

BF = jnp.bfloat16
F32 = jnp.float32
NT = (((1,), (1,)), ((), ()))
NN = (((1,), (0,)), ((), ()))

VM = pl.BlockSpec(memory_space=pltpu.VMEM)
SM = pl.BlockSpec(memory_space=pltpu.SMEM)


def dot(a, b, dims=NN):
    return lax.dot_general(a, b, dims, preferred_element_type=F32)


def iota(shape, axis):
    return lax.broadcasted_iota(jnp.int32, shape, axis)


def ones_where(mask):
    return jnp.where(mask, 1.0, 0.0).astype(BF)


def kernel_call(body, out_shape, in_specs, flops, bytes_accessed, limit, scratch=()):
    return pl.pallas_call(
        body,
        out_shape=out_shape,
        in_specs=in_specs,
        out_specs=jax.tree.map(lambda _: VM, out_shape),
        scratch_shapes=list(scratch),
        compiler_params=pltpu.CompilerParams(vmem_limit_bytes=limit * MIB),
        cost_estimate=pl.CostEstimate(
            flops=flops, bytes_accessed=bytes_accessed, transcendentals=0
        ),
    )


def gridded_call(
    body, out_shape, steps, in_specs, out_specs, bytes_accessed, scratch=(), aliases=None
):
    return pl.pallas_call(
        body,
        out_shape=out_shape,
        grid_spec=pltpu.PrefetchScalarGridSpec(
            num_scalar_prefetch=1,
            grid=(steps,),
            in_specs=in_specs,
            out_specs=out_specs,
            scratch_shapes=list(scratch),
        ),
        input_output_aliases=aliases or {},
        compiler_params=pltpu.CompilerParams(vmem_limit_bytes=56 * MIB),
        cost_estimate=pl.CostEstimate(
            flops=1 << 30, bytes_accessed=bytes_accessed, transcendentals=0
        ),
    )


def places(ids_t):
    experts = iota((OWNERS, TOK), 0)
    named = jnp.zeros((OWNERS, TOK), F32)
    for k in range(TOP):
        named += jnp.where(ids_t[k : k + 1, :] == experts, 1.0, 0.0)
    before = ones_where(iota((TOK, TOK), 0) < iota((TOK, TOK), 1))
    rank = dot(named.astype(BF), before)
    return jnp.where(named > 0.0, rank, -1.0)


def pair_places(ids_t):
    pairs = TOK * TOP
    widen = ones_where(iota((TOK, pairs), 1) // TOP == iota((TOK, pairs), 0))
    ranks = dot(places(ids_t).astype(BF), widen)
    ids = dot(ids_t.astype(F32).astype(BF), widen)
    mine = iota((TOP, pairs), 1) % TOP == iota((TOP, pairs), 0)
    flat = jnp.sum(jnp.where(mine, ids, 0.0), axis=0, keepdims=True)
    return jnp.where(flat == iota((OWNERS, pairs), 0).astype(F32), ranks, -1.0)


def spread(table, times):
    shape = (table.shape[0] * times, table.shape[0])
    return dot(ones_where(iota(shape, 0) // times == iota(shape, 1)), table.astype(BF))


def pack_half(pos_ref, ids_ref, tokens_ref, out_ref):
    out_ref[:TOK, :] = tokens_ref[...]
    out_ref[TOK:, :] = jnp.zeros((16, HALF), BF)
    ids = jnp.concatenate([ids_ref[...].astype(F32), jnp.zeros((8, TOK), F32)], 0)
    out_ref[TOK:, :TOK] = ids.astype(BF)


def other_ids(other_ref):
    return other_ref[TOK:, :TOK].astype(F32)[:TOP].astype(jnp.int32)


def send_whole(pos_ref, ids_ref, tokens_ref, out_ref, table_ref):
    step, x = pl.program_id(0), pos_ref[0]

    @pl.when(step == 0)
    def _():
        table_ref[...] = places(ids_ref[...])

    table = spread(table_ref[pl.ds(pl.multiple_of(step * 32, 32), 32), :], FOLD)
    row = iota(table.shape, 0)
    whole = table == (2 * x + row % 8 // 4).astype(F32)
    picks = jnp.concatenate([ones_where(whole & (row % 4 == b)) for b in range(4)], 1)
    parts = jnp.concatenate([tokens_ref[:, b * SHARE : (b + 1) * SHARE] for b in range(4)], 0)
    out_ref[...] = dot(picks, parts).astype(BF)


def send_shared(pos_ref, ids_ref, tokens_ref, other_ref, _, out_ref, half_ref, half_ids_ref):
    x, c = pos_ref[0], pos_ref[1]
    mine = x // 2 == c

    @pl.when(mine)
    def _():
        half_ref[...] = tokens_ref[...]
        half_ids_ref[...] = ids_ref[...]

    @pl.when(jnp.logical_not(mine))
    def _():
        half_ref[...] = other_ref[:TOK, :]
        half_ids_ref[...] = other_ids(other_ref)

    table = spread(places(half_ids_ref[...]), FOLD)
    row = iota(table.shape, 0)
    shared = table == (FIRST + x % 2).astype(F32)
    picks = jnp.concatenate([ones_where(shared & (row % 8 == b)) for b in range(8)], 1)
    parts = jnp.concatenate([half_ref[:, b * STRIP : (b + 1) * STRIP] for b in range(8)], 0)
    out_ref[...] = dot(picks, parts).astype(BF)


def pick_grads(pos_ref, ids_ref, other_ref, grads_ref, other_grads_ref, *outs):
    x, c = pos_ref[0], pos_ref[1]
    pairs = TOK * TOP
    table, other_table = pair_places(ids_ref[...]), pair_places(other_ids(other_ref))
    embed = ones_where(iota((UNITS, 256), 0) == iota((UNITS, 256), 1))
    grads = dot(grads_ref[...], embed).astype(BF)
    other_grads = dot(other_grads_ref[...], embed).astype(BF)
    twice = spread(table, 2)
    second = iota((SLOTS, pairs), 0) % 2
    for k, out in enumerate(outs):
        to = lax.rem(x + k, REPS)
        out[:SLOTS, :] = dot(ones_where(twice == (2 * to + second).astype(F32)), grads).astype(BF)
        shared = FIRST + to % 2
        place = jnp.where(to // 2 == c, shared, -2).astype(F32)
        other_place = jnp.where(to // 2 == c, -2, shared).astype(F32)
        out[SLOTS:, :] = (
            dot(ones_where(table == place), grads)
            + dot(ones_where(other_table == other_place), other_grads)
        ).astype(BF)


def fold_grads(pos_ref, g0, g1, g2, g3, out_ref):
    x, c = pos_ref[0], pos_ref[1]
    row, column = iota((ROWS, SLOTS), 0), iota((ROWS, SLOTS), 1)
    total = jnp.zeros((ROWS, 256), F32)
    for k, got in enumerate((g0, g1, g2, g3)):
        unit = lax.rem(x - k + REPS, REPS)
        total += dot(ones_where((row // 4 == column) & (row % 4 == unit)), got[:SLOTS, :])
        for u in range(3):
            at = jnp.where(unit // 2 == c, unit % 2 * 3 + u, -1)
            source, lane = iota((256, 256), 0), iota((256, 256), 1)
            move = ones_where((source // 64 == u) & (lane == UNITS + source % 64))
            moved = dot(got[SLOTS:, :], move).astype(BF)
            row5, column5 = iota((ROWS, OWNERS), 0), iota((ROWS, OWNERS), 1)
            total += dot(ones_where((row5 // 8 == column5) & (row5 % 8 == at)), moved)
    out_ref[...] = total.astype(BF)


def regroup(source, many, put):
    size = 256 // many
    shape = (256, 256)
    to = iota(shape, 0)
    order = ones_where(iota(shape, 1) == many * (to % size) + to // size)
    for g in range(ROWS // 256):
        got = dot(order, source(slice(g * 256, (g + 1) * 256))).astype(BF)
        for p in range(many):
            put(p, slice(g * size, (g + 1) * size), got[p * size : (p + 1) * size])


def input_products(pos_ref, rows_ref, probes_ref, all_ref, i0, i1, i2, i3, sum_ref):
    x = pos_ref[0]

    def put_whole(p, at, got):
        all_ref[at, p * SHARE : (p + 1) * SHARE] = got

    def put_shared(p, at, got):
        all_ref[SLOTS + at.start : SLOTS + at.stop, p * STRIP : (p + 1) * STRIP] = got

    regroup(lambda at: rows_ref[at, :SHARE], 4, put_whole)
    regroup(lambda at: rows_ref[at, SHARE:], 16, put_shared)
    all_ref[SLOTS + PAIRS :, :] = jnp.zeros((ALL - SLOTS - PAIRS, D), BF)
    rows = all_ref[...]
    projected = dot(probes_ref[...], rows, NT).astype(BF)
    sum_ref[...] = dot(projected, rows)
    for k, out in enumerate((i0, i1, i2, i3)):
        base = lax.rem(x + k, REPS) * SHARE
        out[...] = sum_ref[:, pl.ds(pl.multiple_of(base, SHARE), SHARE)].astype(out.dtype)


def gate_products(rows_ref, weights_ref, gate_ref):
    gate_ref[...] = dot(weights_ref[...], rows_ref[...], NT)


def gate_part(
    pos_ref, grad_probes_ref, gate_ref, got_ref, own_ref, out_ref,
    whole_ref, shared_ref, sketch_ref,
):
    x = pos_ref[0]

    def put_whole(p, at, got):
        whole_ref[p * SLOTS + at.start : p * SLOTS + at.stop, :] = got

    def put_shared(p, at, got):
        shared_ref[p * PAIRS + at.start : p * PAIRS + at.stop, :] = got

    regroup(lambda at: got_ref[at, :], 4, put_whole)
    regroup(lambda at: got_ref[at, :], 16, put_shared)
    same = ones_where(iota((UNITS, 256), 0) == iota((UNITS, 256), 1))
    whole = dot(same, whole_ref[...], NT)
    last = ones_where(iota((64, 256), 0) + UNITS == iota((64, 256), 1))
    shared = dot(last, shared_ref[...], NT)
    turned = pltpu.roll(shared, ROWS - PAIRS, 1)
    parts = []
    for p in (0, 1, 2, 3, 4, 5, 8, 9, 10, 11, 12, 13):
        at = p // 2 * 128
        parts.append((turned if p % 2 else shared)[:, at : at + 128])
    late = jnp.concatenate(parts, 0)
    late = jnp.where(iota((FFW, 128), 1) < PAIRS, late, 0.0)
    early = jnp.concatenate([whole[:, b * SLOTS : (b + 1) * SLOTS] for b in range(4)], 0)
    grads = jnp.concatenate([early, late], 1)
    gate = gate_ref[...]
    s = 1.0 / (1.0 + jnp.exp(-gate))
    gate_grad = (grads * (s * (1.0 + gate * (1.0 - s)))).astype(BF)
    projected = dot(grad_probes_ref[...], gate_grad).astype(BF)
    sketch_ref[...] = dot(gate_grad, projected, NT)
    out_ref[...] = sketch_ref[...].astype(BF)
    own_ref[...] = sketch_ref[pl.ds(pl.multiple_of(x * UNITS, UNITS), UNITS), :]


def finish_input(inverse_ref, i0, i1, i2, i3, out_ref):
    total = i0[...] + (i1[...].astype(F32) + i2[...].astype(F32) + i3[...].astype(F32))
    out_ref[...] = (total * inverse_ref[0]).T


def finish_grad(pos_ref, inverse_ref, own_ref, parts_ref, out_ref):
    total = own_ref[...]
    for k in range(1, REPS):
        total += parts_ref[lax.rem(pos_ref[0] + k, REPS)].astype(F32)
    out_ref[...] = total * inverse_ref[0]


def shift(block, k):
    return lax.ppermute(block, "rep", [(i, (i + k) % REPS) for i in range(REPS)])


def shifted(blocks):
    return [blocks[0]] + [shift(blocks[k], k) for k in range(1, REPS)]


def swap(block):
    return lax.ppermute(block, "ep", [(i, i ^ 1) for i in range(OWNERS)])


def to_owners(rows):
    width = rows.shape[1]
    rows = rows.reshape(OWNERS, FOLD, width)
    return lax.all_to_all(rows, "ep", split_axis=0, concat_axis=0, tiled=True).reshape(ROWS, width)


def local(tokens, expert_ids, hidden_grads, gate_weight, probes, grad_probes, window_counts):
    sds = jax.ShapeDtypeStruct
    pos = jnp.stack([lax.axis_index("rep"), lax.axis_index("ep") % 2]).astype(jnp.int32)
    inverse = 1.0 / window_counts.astype(F32)
    ids_t = expert_ids.T

    weights = lax.all_gather(gate_weight[0], "rep", axis=0, tiled=True)

    half = lambda other: pl.BlockSpec(
        (TOK, HALF), lambda i, pos: (0, 1 - pos[1] if other else pos[1])
    )
    packed = gridded_call(
        pack_half, sds((TOK + 16, HALF), BF), 1, [VM, half(True)], VM, MIB
    )(pos, ids_t, tokens)
    other = swap(packed)
    sent = sds((ROWS, SHARE + STRIP), BF)
    out_rows = gridded_call(
        send_whole,
        sent,
        4,
        [VM, VM],
        pl.BlockSpec((ROWS // 4, SHARE), lambda i, pos: (i, 0)),
        3 * MIB,
        [pltpu.VMEM((OWNERS, TOK), F32)],
    )(pos, ids_t, tokens)
    out_rows = gridded_call(
        send_shared,
        sent,
        1,
        [VM, half(False), VM, pl.BlockSpec(memory_space=pl.ANY)],
        pl.BlockSpec((ROWS, STRIP), lambda i, pos: (0, SHARE // STRIP)),
        2 * MIB,
        [pltpu.VMEM((TOK, HALF), BF), pltpu.VMEM((TOP, TOK), jnp.int32)],
        {4: 0},
    )(pos, ids_t, tokens, other, out_rows)
    rows = to_owners(out_rows)

    grads, _ = lax.optimization_barrier((hidden_grads.reshape(TOK * TOP, UNITS), out_rows))
    other_grads = swap(grads)
    picked = kernel_call(
        pick_grads, [sds((SLOTS + OWNERS, 256), BF)] * REPS, [SM] + [VM] * 4, 5 << 30, 3 * MIB, 20
    )(pos, ids_t, other, grads, other_grads)
    out_grads = kernel_call(
        fold_grads, sds((ROWS, 256), BF), [SM] + [VM] * 4, 1 << 31, 3 * MIB, 12
    )(pos, *shifted(picked))
    got = to_owners(out_grads)

    kinds = [F32, BF, BF, BF]
    rows_all, *inputs = kernel_call(
        input_products,
        [sds((ALL, D), BF)] + [sds((R, SHARE), kind) for kind in kinds],
        [SM] + [VM] * 2,
        1 << 30,
        8 * MIB,
        16,
        [pltpu.VMEM((R, D), F32)],
    )(pos, rows, probes)
    inputs = shifted(inputs)
    steps = 3
    gate = pl.pallas_call(
        gate_products,
        out_shape=sds((FFW, ALL), F32),
        grid=(steps,),
        in_specs=[VM, pl.BlockSpec((FFW // steps, D), lambda i: (i, 0))],
        out_specs=pl.BlockSpec((FFW // steps, ALL), lambda i: (i, 0)),
        compiler_params=pltpu.CompilerParams(vmem_limit_bytes=24 * MIB),
        cost_estimate=pl.CostEstimate(
            flops=5 << 29, bytes_accessed=10 * MIB, transcendentals=0
        ),
    )(rows_all, weights)

    own_sketch, sketch = kernel_call(
        gate_part,
        [sds((UNITS, R), F32), sds((FFW, R), BF)],
        [SM] + [VM] * 3,
        1 << 30,
        3 * MIB,
        14,
        [pltpu.VMEM((ROWS, 256), BF), pltpu.VMEM((ROWS, 256), BF), pltpu.VMEM((FFW, R), F32)],
    )(pos, grad_probes, gate, got)
    sketches = lax.all_to_all(
        sketch.reshape(REPS, UNITS, R), "rep", split_axis=0, concat_axis=0, tiled=True
    )

    input_sketch = kernel_call(
        finish_input, sds((SHARE, R), F32), [SM] + [VM] * 4, 1 << 20, 2 * MIB, 6
    )(inverse, *inputs)
    grad_sketch = kernel_call(
        finish_grad, sds((UNITS, R), F32), [SM] * 2 + [VM] * 2, 1 << 18, MIB // 4, 4
    )(pos, inverse, own_sketch, sketches)
    return input_sketch[None], grad_sketch[None]


def solution(mesh):
    placed = (
        P("ep", None),
        P("ep", None),
        P("ep", None, "rep"),
        P("ep", "rep", None),
        P(),
        P(),
        P("ep"),
    )
    return jax.shard_map(
        local,
        mesh=mesh,
        in_specs=placed,
        out_specs=(P("ep", "rep", None), P("ep", "rep", None)),
        check_vma=False,
    )
```

```python
import jax
import jax.numpy as jnp
from jax import lax
from jax.experimental import pallas as pl
from jax.experimental.pallas import tpu as pltpu
from jax.sharding import PartitionSpec as P

OWNERS = 128
PAIRS = OWNERS // 2
REPS = 4
TOK = 128
TOP = 8
D = 4096
HALF = D // 2
SHARE = D // REPS
FFW = 768
UNITS = FFW // REPS
R = 128
FIRST = 8
FOLD = 8
ROWS = OWNERS * FOLD
SLOTS = OWNERS * 2
ALL = SLOTS + 128
STRIP = HALF // FOLD
MIB = 1 << 20

BF = jnp.bfloat16
F32 = jnp.float32
NT = (((1,), (1,)), ((), ()))
NN = (((1,), (0,)), ((), ()))

VM = pl.BlockSpec(memory_space=pltpu.VMEM)
SM = pl.BlockSpec(memory_space=pltpu.SMEM)


def dot(a, b, dims=NN):
    return lax.dot_general(a, b, dims, preferred_element_type=F32)


def iota(shape, axis):
    return lax.broadcasted_iota(jnp.int32, shape, axis)


def ones_where(mask):
    return jnp.where(mask, 1.0, 0.0).astype(BF)


def kernel_call(body, out_shape, in_specs, flops, bytes_accessed, limit, scratch=()):
    return pl.pallas_call(
        body,
        out_shape=out_shape,
        in_specs=in_specs,
        out_specs=jax.tree.map(lambda _: VM, out_shape),
        scratch_shapes=list(scratch),
        compiler_params=pltpu.CompilerParams(vmem_limit_bytes=limit * MIB),
        cost_estimate=pl.CostEstimate(
            flops=flops, bytes_accessed=bytes_accessed, transcendentals=0
        ),
    )


def gridded_call(
    body, out_shape, steps, in_specs, out_specs, bytes_accessed, scratch=(), aliases=None
):
    return pl.pallas_call(
        body,
        out_shape=out_shape,
        grid_spec=pltpu.PrefetchScalarGridSpec(
            num_scalar_prefetch=1,
            grid=(steps,),
            in_specs=in_specs,
            out_specs=out_specs,
            scratch_shapes=list(scratch),
        ),
        input_output_aliases=aliases or {},
        compiler_params=pltpu.CompilerParams(vmem_limit_bytes=56 * MIB),
        cost_estimate=pl.CostEstimate(
            flops=1 << 30, bytes_accessed=bytes_accessed, transcendentals=0
        ),
    )


def places(ids_t):
    experts = iota((OWNERS, TOK), 0)
    named = jnp.zeros((OWNERS, TOK), F32)
    for k in range(TOP):
        named += jnp.where(ids_t[k : k + 1, :] == experts, 1.0, 0.0)
    before = ones_where(iota((TOK, TOK), 0) < iota((TOK, TOK), 1))
    rank = dot(named.astype(BF), before)
    return jnp.where(named > 0.0, rank, -1.0)


def pair_places(ids_t):
    pairs = TOK * TOP
    widen = ones_where(iota((TOK, pairs), 1) // TOP == iota((TOK, pairs), 0))
    ranks = dot(places(ids_t).astype(BF), widen)
    ids = dot(ids_t.astype(F32).astype(BF), widen)
    mine = iota((TOP, pairs), 1) % TOP == iota((TOP, pairs), 0)
    flat = jnp.sum(jnp.where(mine, ids, 0.0), axis=0, keepdims=True)
    return jnp.where(flat == iota((OWNERS, pairs), 0).astype(F32), ranks, -1.0)


def spread(table, times):
    shape = (table.shape[0] * times, table.shape[0])
    return dot(ones_where(iota(shape, 0) // times == iota(shape, 1)), table.astype(BF))


def pack_half(pos_ref, ids_ref, tokens_ref, out_ref):
    out_ref[:TOK, :] = tokens_ref[...]
    out_ref[TOK:, :] = jnp.zeros((16, HALF), BF)
    ids = jnp.concatenate([ids_ref[...].astype(F32), jnp.zeros((8, TOK), F32)], 0)
    out_ref[TOK:, :TOK] = ids.astype(BF)


def other_ids(other_ref):
    return other_ref[TOK:, :TOK].astype(F32)[:TOP].astype(jnp.int32)


def send_whole(pos_ref, ids_ref, tokens_ref, out_ref):
    x = pos_ref[0]
    table = spread(places(ids_ref[...]), FOLD)
    row = iota((ROWS, TOK), 0)
    whole = table == (2 * x + row % 8 // 4).astype(F32)
    picks = jnp.concatenate([ones_where(whole & (row % 4 == b)) for b in range(4)], 1)
    parts = jnp.concatenate([tokens_ref[:, b * SHARE : (b + 1) * SHARE] for b in range(4)], 0)
    out_ref[...] = dot(picks, parts).astype(BF)


def send_shared(
    pos_ref, ids_ref, tokens_ref, other_ref, _, out_ref, half_ref, half_ids_ref, fold_ref
):
    x, c = pos_ref[0], pos_ref[1]
    mine = x // 2 == c

    @pl.when(mine)
    def _():
        half_ref[...] = tokens_ref[...]
        half_ids_ref[...] = ids_ref[...]

    @pl.when(jnp.logical_not(mine))
    def _():
        half_ref[...] = other_ref[:TOK, :]
        half_ids_ref[...] = other_ids(other_ref)

    picks = ones_where(places(half_ids_ref[...]) == (FIRST + x % 2).astype(F32))
    rows = dot(picks, half_ref[...])
    for b in range(FOLD):
        for h in range(STRIP // 128):
            start = b * STRIP + h * 128
            fold_ref[h, pl.ds(b, OWNERS, stride=FOLD), :] = rows[:, start : start + 128]
    for h in range(STRIP // 128):
        out_ref[:, h * 128 : (h + 1) * 128] = fold_ref[h].astype(BF)


def pick_grads(pos_ref, ids_ref, other_ref, grads_ref, other_grads_ref, *outs):
    x, c = pos_ref[0], pos_ref[1]
    pairs = TOK * TOP
    table, other_table = pair_places(ids_ref[...]), pair_places(other_ids(other_ref))
    embed = ones_where(iota((UNITS, 256), 0) == iota((UNITS, 256), 1))
    grads = dot(grads_ref[...], embed).astype(BF)
    other_grads = dot(other_grads_ref[...], embed).astype(BF)
    twice = spread(table, 2)
    second = iota((SLOTS, pairs), 0) % 2
    for k, out in enumerate(outs):
        to = lax.rem(x + k, REPS)
        out[:SLOTS, :] = dot(ones_where(twice == (2 * to + second).astype(F32)), grads).astype(BF)
        shared = FIRST + to % 2
        place = jnp.where(to // 2 == c, shared, -2).astype(F32)
        other_place = jnp.where(to // 2 == c, -2, shared).astype(F32)
        out[SLOTS:, :] = (
            dot(ones_where(table == place), grads)
            + dot(ones_where(other_table == other_place), other_grads)
        ).astype(BF)


def fold_grads(pos_ref, g0, g1, g2, g3, out_ref):
    x, c = pos_ref[0], pos_ref[1]
    row, column = iota((ROWS, SLOTS), 0), iota((ROWS, SLOTS), 1)
    total = jnp.zeros((ROWS, 256), F32)
    for k, got in enumerate((g0, g1, g2, g3)):
        unit = lax.rem(x - k + REPS, REPS)
        total += dot(ones_where((row // 4 == column) & (row % 4 == unit)), got[:SLOTS, :])
        for u in range(3):
            at = jnp.where(unit // 2 == c, unit % 2 * 3 + u, -1)
            source, lane = iota((256, 256), 0), iota((256, 256), 1)
            move = ones_where((source // 64 == u) & (lane == UNITS + source % 64))
            moved = dot(got[SLOTS:, :], move).astype(BF)
            row5, column5 = iota((ROWS, OWNERS), 0), iota((ROWS, OWNERS), 1)
            total += dot(ones_where((row5 // 8 == column5) & (row5 % 8 == at)), moved)
    out_ref[...] = total.astype(BF)


def regroup(source, many, put):
    size = 256 // many
    shape = (256, 256)
    to = iota(shape, 0)
    order = ones_where(iota(shape, 1) == many * (to % size) + to // size)
    for g in range(ROWS // 256):
        got = dot(order, source(slice(g * 256, (g + 1) * 256))).astype(BF)
        for p in range(many):
            put(p, slice(g * size, (g + 1) * size), got[p * size : (p + 1) * size])


def gather_rows(rows_ref, all_ref):
    def put_whole(p, at, got):
        all_ref[at, p * SHARE : (p + 1) * SHARE] = got

    def put_shared(p, at, got):
        all_ref[SLOTS + at.start : SLOTS + at.stop, p * STRIP : (p + 1) * STRIP] = got

    regroup(lambda at: rows_ref[at, :SHARE], 4, put_whole)
    regroup(lambda at: rows_ref[at, SHARE:], 16, put_shared)
    all_ref[SLOTS + PAIRS :, :] = jnp.zeros((ALL - SLOTS - PAIRS, D), BF)
    return all_ref[...]


def input_products(pos_ref, rows_ref, probes_ref, i0, i1, i2, i3, all_ref, sum_ref):
    x = pos_ref[0]
    rows = gather_rows(rows_ref, all_ref)
    projected = dot(probes_ref[...], rows, NT).astype(BF)
    sum_ref[...] = dot(projected, rows)
    for k, out in enumerate((i0, i1, i2, i3)):
        base = lax.rem(x + k, REPS) * SHARE
        out[...] = sum_ref[:, pl.ds(pl.multiple_of(base, SHARE), SHARE)].astype(out.dtype)


def gate_products(pos_ref, rows_ref, w0, w1, w2, w3, w4, gate_ref, held_ref, all_ref, sems):
    x = pos_ref[0]
    half = UNITS // 2
    blocks = []
    for n, (w, k, start, size) in enumerate(
        (
            (w0, 0, 0, UNITS),
            (w1, 1, 0, UNITS),
            (w2, 2, 0, half),
            (w3, 2, half, half),
            (w4, 3, 0, UNITS),
        )
    ):
        at = slice(k * UNITS + start, k * UNITS + start + size)
        copy = pltpu.make_async_copy(w, held_ref.at[at, :], sems.at[n])
        copy.start()
        blocks.append((copy, at, lax.rem(x + k, REPS) * UNITS + start, size))
    rows = gather_rows(rows_ref, all_ref)
    for copy, at, base, size in blocks:
        copy.wait()
        gate_ref[pl.ds(pl.multiple_of(base, half), size), :] = dot(held_ref[at, :], rows, NT)


def gate_part(
    pos_ref, grad_probes_ref, gate_ref, got_ref, own_ref, out_ref,
    whole_ref, shared_ref, sketch_ref,
):
    x = pos_ref[0]

    def put_whole(p, at, got):
        whole_ref[p * SLOTS + at.start : p * SLOTS + at.stop, :] = got

    def put_shared(p, at, got):
        shared_ref[p * PAIRS + at.start : p * PAIRS + at.stop, :] = got

    regroup(lambda at: got_ref[at, :], 4, put_whole)
    regroup(lambda at: got_ref[at, :], 16, put_shared)
    same = ones_where(iota((UNITS, 256), 0) == iota((UNITS, 256), 1))
    whole = dot(same, whole_ref[...], NT)
    last = ones_where(iota((64, 256), 0) + UNITS == iota((64, 256), 1))
    shared = dot(last, shared_ref[...], NT)
    turned = pltpu.roll(shared, ROWS - PAIRS, 1)
    parts = []
    for p in (0, 1, 2, 3, 4, 5, 8, 9, 10, 11, 12, 13):
        at = p // 2 * 128
        parts.append((turned if p % 2 else shared)[:, at : at + 128])
    late = jnp.concatenate(parts, 0)
    late = jnp.where(iota((FFW, 128), 1) < PAIRS, late, 0.0)
    early = jnp.concatenate([whole[:, b * SLOTS : (b + 1) * SLOTS] for b in range(4)], 0)
    grads = jnp.concatenate([early, late], 1)
    gate = gate_ref[...]
    s = 1.0 / (1.0 + jnp.exp(-gate))
    gate_grad = (grads * (s * (1.0 + gate * (1.0 - s)))).astype(BF)
    projected = dot(grad_probes_ref[...], gate_grad).astype(BF)
    sketch_ref[...] = dot(gate_grad, projected, NT)
    out_ref[...] = sketch_ref[...].astype(BF)
    own_ref[...] = sketch_ref[pl.ds(pl.multiple_of(x * UNITS, UNITS), UNITS), :]


def finish_input(inverse_ref, i0, i1, i2, i3, out_ref):
    total = i0[...] + (i1[...].astype(F32) + i2[...].astype(F32) + i3[...].astype(F32))
    out_ref[...] = (total * inverse_ref[0]).T


def finish_grad(pos_ref, inverse_ref, own_ref, parts_ref, out_ref):
    total = own_ref[...]
    for k in range(1, REPS):
        total += parts_ref[lax.rem(pos_ref[0] + k, REPS)].astype(F32)
    out_ref[...] = total * inverse_ref[0]


def shift(block, k):
    return lax.ppermute(block, "rep", [(i, (i + k) % REPS) for i in range(REPS)])


def shifted(blocks):
    return [blocks[0]] + [shift(blocks[k], k) for k in range(1, REPS)]


def swap(block):
    return lax.ppermute(block, "ep", [(i, i ^ 1) for i in range(OWNERS)])


def to_owners(rows):
    width = rows.shape[1]
    rows = rows.reshape(OWNERS, FOLD, width)
    return lax.all_to_all(rows, "ep", split_axis=0, concat_axis=0, tiled=True).reshape(ROWS, width)


def local(tokens, expert_ids, hidden_grads, gate_weight, probes, grad_probes, window_counts):
    sds = jax.ShapeDtypeStruct
    pos = jnp.stack([lax.axis_index("rep"), lax.axis_index("ep") % 2]).astype(jnp.int32)
    inverse = 1.0 / window_counts.astype(F32)
    ids_t = expert_ids.T

    half = lambda other: pl.BlockSpec(
        (TOK, HALF), lambda i, pos: (0, 1 - pos[1] if other else pos[1])
    )
    packed = gridded_call(
        pack_half, sds((TOK + 16, HALF), BF), 1, [VM, half(True)], VM, MIB
    )(pos, ids_t, tokens)
    other = swap(packed)
    sent = sds((ROWS, SHARE + STRIP), BF)
    out_rows = gridded_call(
        send_whole,
        sent,
        1,
        [VM, VM],
        pl.BlockSpec((ROWS, SHARE), lambda i, pos: (0, 0)),
        3 * MIB,
    )(pos, ids_t, tokens)
    out_rows = gridded_call(
        send_shared,
        sent,
        1,
        [VM, half(False), VM, pl.BlockSpec(memory_space=pl.ANY)],
        pl.BlockSpec((ROWS, STRIP), lambda i, pos: (0, SHARE // STRIP)),
        2 * MIB,
        [
            pltpu.VMEM((TOK, HALF), BF),
            pltpu.VMEM((TOP, TOK), jnp.int32),
            pltpu.VMEM((STRIP // 128, ROWS, 128), F32),
        ],
        {4: 0},
    )(pos, ids_t, tokens, other, out_rows)
    rows = to_owners(out_rows)

    own, grads, _ = lax.optimization_barrier(
        (gate_weight[0], hidden_grads.reshape(TOK * TOP, UNITS), out_rows)
    )
    left, right = shift(own, 1), shift(own, REPS - 1)
    other_grads = swap(grads)
    picked = kernel_call(
        pick_grads, [sds((SLOTS + OWNERS, 256), BF)] * REPS, [SM] + [VM] * 4, 5 << 30, 3 * MIB, 20
    )(pos, ids_t, other, grads, other_grads)
    top = shift(left[: UNITS // 2], 1)
    bottom = shift(right[UNITS // 2 :], REPS - 1)
    out_grads = kernel_call(
        fold_grads, sds((ROWS, 256), BF), [SM] + [VM] * 4, 1 << 31, 3 * MIB, 12
    )(pos, *shifted(picked))
    out_grads, left, right, top, bottom = lax.optimization_barrier(
        (out_grads, left, right, top, bottom)
    )
    got = to_owners(out_grads)

    kinds = [F32, BF, BF, BF]
    inputs = kernel_call(
        input_products,
        [sds((R, SHARE), kind) for kind in kinds],
        [SM] + [VM] * 2,
        1 << 30,
        8 * MIB,
        56,
        [pltpu.VMEM((ALL, D), BF), pltpu.VMEM((R, D), F32)],
    )(pos, rows, probes)
    inputs = shifted(inputs)
    gate = kernel_call(
        gate_products,
        sds((FFW, ALL), F32),
        [SM, VM] + [pl.BlockSpec(memory_space=pl.ANY)] * 5,
        5 << 29,
        10 * MIB,
        56,
        [
            pltpu.VMEM((FFW, D), BF),
            pltpu.VMEM((ALL, D), BF),
            pltpu.SemaphoreType.DMA((5,)),
        ],
    )(pos, rows, own, right, top, bottom, left)

    own_sketch, sketch = kernel_call(
        gate_part,
        [sds((UNITS, R), F32), sds((FFW, R), BF)],
        [SM] + [VM] * 3,
        1 << 30,
        3 * MIB,
        56,
        [pltpu.VMEM((ROWS, 256), BF), pltpu.VMEM((ROWS, 256), BF), pltpu.VMEM((FFW, R), F32)],
    )(pos, grad_probes, gate, got)
    sketches = lax.all_to_all(
        sketch.reshape(REPS, UNITS, R), "rep", split_axis=0, concat_axis=0, tiled=True
    )

    input_sketch = kernel_call(
        finish_input, sds((SHARE, R), F32), [SM] + [VM] * 4, 1 << 20, 2 * MIB, 6
    )(inverse, *inputs)
    grad_sketch = kernel_call(
        finish_grad, sds((UNITS, R), F32), [SM] * 2 + [VM] * 2, 1 << 18, MIB // 4, 4
    )(pos, inverse, own_sketch, sketches)
    return input_sketch[None], grad_sketch[None]


def solution(mesh):
    placed = (
        P("ep", None),
        P("ep", None),
        P("ep", None, "rep"),
        P("ep", "rep", None),
        P(),
        P(),
        P("ep"),
    )
    return jax.shard_map(
        local,
        mesh=mesh,
        in_specs=placed,
        out_specs=(P("ep", "rep", None), P("ep", "rep", None)),
        check_vma=False,
    )
```

```python
import jax
import jax.numpy as jnp
from jax import lax
from jax.experimental import pallas as pl
from jax.experimental.pallas import tpu as pltpu
from jax.sharding import PartitionSpec as P

OWNERS = 128
REPS = 4
TOK = 128
TOP = 8
D = 4096
SHARE = D // REPS
FFW = 768
UNITS = FFW // REPS
R = 128
FIRST = 8
FOLD = 8
ROWS = OWNERS * FOLD
SLOTS = OWNERS * 2
STRIP = SHARE // 4

BF = jnp.bfloat16
F32 = jnp.float32
NT = (((1,), (1,)), ((), ()))
NN = (((1,), (0,)), ((), ()))

VM = pl.BlockSpec(memory_space=pltpu.VMEM)
SM = pl.BlockSpec(memory_space=pltpu.SMEM)


def dot(a, b, dims=NN):
    return lax.dot_general(a, b, dims, preferred_element_type=F32)


def iota(shape, axis):
    return lax.broadcasted_iota(jnp.int32, shape, axis)


def ones_where(mask):
    return jnp.where(mask, 1.0, 0.0).astype(BF)


def kernel_call(body, out_shape, in_specs, flops, bytes_accessed, limit, scratch=()):
    return pl.pallas_call(
        body,
        out_shape=out_shape,
        in_specs=in_specs,
        out_specs=jax.tree.map(lambda _: VM, out_shape),
        scratch_shapes=list(scratch),
        compiler_params=pltpu.CompilerParams(vmem_limit_bytes=limit << 20),
        cost_estimate=pl.CostEstimate(
            flops=flops, bytes_accessed=bytes_accessed, transcendentals=0
        ),
    )


def places(ids_t):
    experts = iota((OWNERS, TOK), 0)
    named = jnp.zeros((OWNERS, TOK), F32)
    for k in range(TOP):
        named += jnp.where(ids_t[k : k + 1, :] == experts, 1.0, 0.0)
    before = ones_where(iota((TOK, TOK), 0) < iota((TOK, TOK), 1))
    rank = dot(named.astype(BF), before)
    return jnp.where(named > 0.0, rank, -1.0)


def spread(table, times):
    shape = (OWNERS * times, OWNERS)
    return dot(ones_where(iota(shape, 0) // times == iota(shape, 1)), table.astype(BF))


def send_rows(pos_ref, ids_ref, tokens_ref, out_ref):
    x = pos_ref[0]
    table = spread(places(ids_ref[...]), FOLD)
    row = iota((ROWS, TOK), 0)
    half, quarter = row % 8 // 4, row % 4
    whole = table == (2 * x + half).astype(F32)
    picks = jnp.concatenate([ones_where(whole & (quarter == b)) for b in range(4)], 1)
    parts = jnp.concatenate([tokens_ref[:, b * SHARE : (b + 1) * SHARE] for b in range(4)], 0)
    out_ref[:, :SHARE] = dot(picks, parts).astype(BF)
    cut = table == (FIRST + half).astype(F32)
    picks = jnp.concatenate([ones_where(cut & (quarter == b)) for b in range(4)], 1)
    parts = jnp.concatenate(
        [
            tokens_ref[:, pl.ds(pl.multiple_of(x * SHARE + b * STRIP, STRIP), STRIP)]
            for b in range(4)
        ],
        0,
    )
    out_ref[:, SHARE:] = dot(picks, parts).astype(BF)


def pick_grads(pos_ref, ids_ref, flat_ref, grads_ref, tail_ref, *outs):
    x = pos_ref[0]
    pairs = TOK * TOP
    widen = ones_where(iota((TOK, pairs), 1) // TOP == iota((TOK, pairs), 0))
    ranks = dot(places(ids_ref[...]).astype(BF), widen)
    named = flat_ref[...] == iota((OWNERS, pairs), 0)
    table = jnp.where(named, ranks, -1.0)
    source, lane = iota((UNITS, STRIP), 0), iota((UNITS, STRIP), 1)
    grads = grads_ref[...]
    main = dot(grads, ones_where(source == lane)).astype(BF)
    twice = spread(table, 2)
    second = iota((SLOTS, pairs), 0) % 2
    for k, out in enumerate(outs):
        place = 2 * lax.rem(x + k, REPS) + second
        out[...] = dot(ones_where(twice == place.astype(F32)), main).astype(BF)
    tails = [
        dot(grads, ones_where((source // 64 == b) & (lane == 192 + source % 64))).astype(BF)
        for b in range(3)
    ]
    block = 256
    for start in range(0, ROWS, block):
        shape = (block, OWNERS)
        owner = (iota(shape, 0) + start) // FOLD == iota(shape, 1)
        eight = dot(ones_where(owner), table.astype(BF))
        row = iota((block, pairs), 0)
        late = eight == (FIRST + row % 8 // 4).astype(F32)
        total = jnp.zeros((block, STRIP), F32)
        for b in range(3):
            total += dot(ones_where(late & (row % 4 == b)), tails[b])
        tail_ref[start : start + block, :] = total.astype(BF)


def fold_grads(pos_ref, tail_ref, g0, g1, g2, g3, out_ref):
    x = pos_ref[0]
    row, column = iota((ROWS, SLOTS), 0), iota((ROWS, SLOTS), 1)
    total = tail_ref[...].astype(F32)
    for k, got in enumerate((g0, g1, g2, g3)):
        unit = lax.rem(x - k + REPS, REPS)
        total += dot(ones_where((row // 4 == column) & (row % 4 == unit)), got[...])
    out_ref[...] = total.astype(BF)


def stack_weights(pos_ref, probes_ref, own_ref, right_ref, top_ref, bottom_ref, left_ref, out_ref):
    x = pos_ref[0]
    half = UNITS // 2
    for w, k, start, size in (
        (own_ref, 0, 0, UNITS),
        (right_ref, 1, 0, UNITS),
        (top_ref, 2, 0, half),
        (bottom_ref, 2, half, half),
        (left_ref, 3, 0, UNITS),
    ):
        base = lax.rem(x + k, REPS) * UNITS + start
        out_ref[pl.ds(pl.multiple_of(base, half), size), :] = w[...]
    out_ref[FFW:, :] = probes_ref[...]


def unfold(source, put):
    shape = (256, 256)
    order = ones_where(iota(shape, 1) == 4 * (iota(shape, 0) % 64) + iota(shape, 0) // 64)
    for g in range(4):
        got = dot(order, source[g * 256 : (g + 1) * 256, :]).astype(BF)
        for b in range(4):
            put(b, slice(g * 64, (g + 1) * 64), got[b * 64 : (b + 1) * 64])


def products(
    pos_ref, rows_ref, weights_ref, gate_ref, cut_ref, own_ref, own_sum_ref, o1, o2, o3,
    whole_ref, sum_ref,
):
    x = pos_ref[0]

    def put(b, at, got):
        whole_ref[at, b * SHARE : (b + 1) * SHARE] = got[:, :SHARE]
        cut_ref[at, b * STRIP : (b + 1) * STRIP] = got[:, SHARE:]

    unfold(rows_ref, put)
    cut = cut_ref[...]
    share = pl.ds(pl.multiple_of(x * SHARE, SHARE), SHARE)
    projected = dot(weights_ref[FFW:, share], cut, NT)
    for k, out in enumerate((own_ref, o1, o2, o3)):
        base = lax.rem(x + k, REPS) * UNITS
        weights = weights_ref[pl.ds(pl.multiple_of(base, UNITS), UNITS), share]
        out[:UNITS, :] = dot(weights, cut, NT).astype(out.dtype)
        out[UNITS : UNITS + R, :] = projected.astype(out.dtype)
    whole = whole_ref[...]
    both = dot(weights_ref[...], whole, NT)
    gate_ref[...] = both[:FFW]
    sum_ref[...] = dot(both[FFW:].astype(BF), whole)
    own_sum_ref[...] = sum_ref[:, share]
    for k, out in enumerate((o1, o2, o3)):
        base = lax.rem(x + k + 1, REPS) * SHARE
        for j in range(4):
            columns = pl.ds(pl.multiple_of(base + j * 256, 256), 256)
            start = UNITS + (1 + j) * R
            out[start : start + R, :] = sum_ref[:, columns].astype(BF)


def gate_gradient(gate, grads):
    s = 1.0 / (1.0 + jnp.exp(-gate))
    return (grads * (s * (1.0 + gate * (1.0 - s)))).astype(BF)


def gate_part(
    pos_ref, grad_probes_ref, gate_ref, got_ref, s0, s1, s2, s3,
    cut_grad_ref, own_ref, out_ref, grads_ref, sketch_ref, padded_ref,
):
    x = pos_ref[0]

    def put(b, at, got):
        grads_ref[b * SLOTS + at.start : b * SLOTS + at.stop, :] = got

    unfold(got_ref, put)
    same = ones_where(iota((STRIP, STRIP), 0) == iota((STRIP, STRIP), 1))
    turned = dot(same, grads_ref[...], NT)
    parts = [turned[:, b * SLOTS : (b + 1) * SLOTS] for b in range(4)]
    cut_gate = s0[:UNITS, :] + (
        s1[:UNITS, :].astype(F32) + s2[:UNITS, :].astype(F32) + s3[:UNITS, :].astype(F32)
    )
    cut_grad = gate_gradient(cut_gate, jnp.concatenate([p[UNITS:] for p in parts[:3]], 0))
    cut_grad_ref[...] = cut_grad
    mine = pl.ds(pl.multiple_of(x * UNITS, UNITS), UNITS)
    padded_ref[...] = jnp.zeros((FFW, SLOTS), BF)
    padded_ref[mine, :] = cut_grad
    cut_projected = dot(grad_probes_ref[...], padded_ref[...])
    whole = jnp.concatenate([p[:UNITS] for p in parts], 0)
    gate_grad = gate_gradient(gate_ref[...], whole)
    projected = dot(grad_probes_ref[...], gate_grad).astype(BF)
    sketch_ref[...] = dot(gate_grad, projected, NT)
    own_ref[:UNITS, :] = sketch_ref[mine, :]
    own_ref[UNITS : UNITS + R, :] = cut_projected[:, :128]
    own_ref[UNITS + R :, :] = cut_projected[:, 128:]
    for to in range(REPS):
        out_ref[to, :UNITS, :] = sketch_ref[to * UNITS : (to + 1) * UNITS, :].astype(BF)
        out_ref[to, UNITS : UNITS + R, :] = cut_projected[:, :128].astype(BF)
        out_ref[to, UNITS + R :, :] = cut_projected[:, 128:].astype(BF)


def finish_input(inverse_ref, cut_ref, own_sum_ref, s0, s1, s2, s3, out_ref):
    at = slice(UNITS, UNITS + R)
    projected = s0[at, :] + (
        s1[at, :].astype(F32) + s2[at, :].astype(F32) + s3[at, :].astype(F32)
    )
    total = own_sum_ref[...] + dot(projected.astype(BF), cut_ref[...])
    for j in range(4):
        block = total[:, j * 256 : (j + 1) * 256]
        start = UNITS + (1 + j) * R
        for other in (s1, s2, s3):
            block += other[start : start + R, :].astype(F32)
        out_ref[j * 256 : (j + 1) * 256, :] = (block * inverse_ref[0]).T


def finish_grad(pos_ref, inverse_ref, cut_grad_ref, own_ref, parts_ref, out_ref):
    total = own_ref[...]
    for k in range(1, REPS):
        total += parts_ref[lax.rem(pos_ref[0] + k, REPS)].astype(F32)
    projected = total[UNITS:].astype(BF)
    sketch = total[:UNITS] + dot(cut_grad_ref[:, :128], projected[:R], NT)
    sketch += dot(cut_grad_ref[:, 128:], projected[R:], NT)
    out_ref[...] = sketch * inverse_ref[0]


def shift(block, k):
    return lax.ppermute(block, "rep", [(i, (i + k) % REPS) for i in range(REPS)])


def shifted(blocks):
    return [blocks[0]] + [shift(blocks[k], k) for k in range(1, REPS)]


def to_owners(rows):
    width = rows.shape[1]
    rows = rows.reshape(OWNERS, FOLD, width)
    return lax.all_to_all(rows, "ep", split_axis=0, concat_axis=0, tiled=True).reshape(ROWS, width)


def local(tokens, expert_ids, hidden_grads, gate_weight, probes, grad_probes, window_counts):
    sds = jax.ShapeDtypeStruct
    x = lax.axis_index("rep")
    pos = x.astype(jnp.int32).reshape(1)
    inverse = 1.0 / window_counts.astype(F32)
    ids_t = expert_ids.T
    flat_ids = expert_ids.reshape(1, TOK * TOP)

    out_rows = kernel_call(
        send_rows, sds((ROWS, SHARE + STRIP), BF), [SM] + [VM] * 2, 1 << 31, 4 << 20, 20
    )(pos, ids_t, tokens)
    rows = to_owners(out_rows)

    own = gate_weight[0]
    own, _ = lax.optimization_barrier((own, out_rows))
    left, right = shift(own, 1), shift(own, REPS - 1)

    tail, *picked = kernel_call(
        pick_grads,
        [sds((ROWS, STRIP), BF)] + [sds((SLOTS, STRIP), BF)] * REPS,
        [SM] + [VM] * 3,
        4 << 30,
        3 << 20,
        20,
    )(pos, ids_t, flat_ids, hidden_grads.reshape(TOK * TOP, UNITS))
    picked = shifted(picked)
    out_grads = kernel_call(
        fold_grads, sds((ROWS, STRIP), BF), [SM] + [VM] * 5, 1 << 29, 3 << 20, 12
    )(pos, tail, *picked)
    out_grads, left, right = lax.optimization_barrier((out_grads, left, right))
    top = shift(left[: UNITS // 2], 1)
    bottom = shift(right[UNITS // 2 :], REPS - 1)
    weights = kernel_call(
        stack_weights, sds((FFW + R, D), BF), [SM] + [VM] * 6, 1000, 14 << 20, 8
    )(pos, probes, own, right, top, bottom, left)
    got = to_owners(out_grads)

    gate, cut, own_sums, own_inputs, *sums = kernel_call(
        products,
        [
            sds((FFW, SLOTS), F32),
            sds((SLOTS, SHARE), BF),
            sds((UNITS + R, SLOTS), F32),
            sds((R, SHARE), F32),
        ]
        + [sds((UNITS + 5 * R, SLOTS), BF)] * (REPS - 1),
        [SM] + [VM] * 2,
        3 << 30,
        14 << 20,
        20,
        [pltpu.VMEM((SLOTS, D), BF), pltpu.VMEM((R, D), F32)],
    )(pos, rows, weights)
    sums = shifted([own_sums] + sums)

    mixed = UNITS + 2 * R
    cut_grad, own_sketch, sketch = kernel_call(
        gate_part,
        [sds((UNITS, SLOTS), BF), sds((mixed, R), F32), sds((REPS, mixed, R), BF)],
        [SM] + [VM] * 7,
        2 << 30,
        4 << 20,
        16,
        [
            pltpu.VMEM((ROWS, STRIP), BF),
            pltpu.VMEM((FFW, R), F32),
            pltpu.VMEM((FFW, SLOTS), BF),
        ],
    )(pos, grad_probes, gate, got, *sums)
    parts = lax.all_to_all(sketch, "rep", split_axis=0, concat_axis=0, tiled=True)

    input_sketch = kernel_call(
        finish_input, sds((SHARE, R), F32), [SM] + [VM] * 6, 1 << 27, 3 << 20, 8
    )(inverse, cut, own_inputs, *sums)
    grad_sketch = kernel_call(
        finish_grad, sds((UNITS, R), F32), [SM] * 2 + [VM] * 3, 1 << 24, 1 << 20, 6
    )(pos, inverse, cut_grad, own_sketch, parts)
    return input_sketch[None], grad_sketch[None]


def solution(mesh):
    placed = (
        P("ep", None),
        P("ep", None),
        P("ep", None, "rep"),
        P("ep", "rep", None),
        P(),
        P(),
        P("ep"),
    )
    return jax.shard_map(
        local,
        mesh=mesh,
        in_specs=placed,
        out_specs=(P("ep", "rep", None), P("ep", "rep", None)),
        check_vma=False,
    )
```

```python
import jax
import jax.numpy as jnp
from jax import lax
from jax.experimental import pallas as pl
from jax.experimental.pallas import tpu as pltpu
from jax.sharding import PartitionSpec as P

OWNERS = 128
REPS = 4
TOK = 128
TOP = 8
D = 4096
SHARE = D // REPS
FFW = 768
UNITS = FFW // REPS
R = 128
FIRST = 8
FOLD = 8
ROWS = OWNERS * FOLD
SLOTS = OWNERS * 2
STRIP = SHARE // 4

BF = jnp.bfloat16
F32 = jnp.float32
NT = (((1,), (1,)), ((), ()))
NN = (((1,), (0,)), ((), ()))

VM = pl.BlockSpec(memory_space=pltpu.VMEM)
SM = pl.BlockSpec(memory_space=pltpu.SMEM)


def dot(a, b, dims=NN):
    return lax.dot_general(a, b, dims, preferred_element_type=F32)


def iota(shape, axis):
    return lax.broadcasted_iota(jnp.int32, shape, axis)


def ones_where(mask):
    return jnp.where(mask, 1.0, 0.0).astype(BF)


def kernel_call(body, out_shape, in_specs, flops, bytes_accessed, limit, scratch=()):
    return pl.pallas_call(
        body,
        out_shape=out_shape,
        in_specs=in_specs,
        out_specs=jax.tree.map(lambda _: VM, out_shape),
        scratch_shapes=list(scratch),
        compiler_params=pltpu.CompilerParams(vmem_limit_bytes=limit << 20),
        cost_estimate=pl.CostEstimate(
            flops=flops, bytes_accessed=bytes_accessed, transcendentals=0
        ),
    )


def places(ids_t):
    experts = iota((OWNERS, TOK), 0)
    named = jnp.zeros((OWNERS, TOK), F32)
    for k in range(TOP):
        named += jnp.where(ids_t[k : k + 1, :] == experts, 1.0, 0.0)
    before = ones_where(iota((TOK, TOK), 0) < iota((TOK, TOK), 1))
    rank = dot(named.astype(BF), before)
    return jnp.where(named > 0.0, rank, -1.0)


def spread(table, times):
    shape = (OWNERS * times, OWNERS)
    return dot(ones_where(iota(shape, 0) // times == iota(shape, 1)), table.astype(BF))


def send_rows(pos_ref, ids_ref, tokens_ref, out_ref):
    x = pos_ref[0]
    table = spread(places(ids_ref[...]), FOLD)
    row = iota((ROWS, TOK), 0)
    half, quarter = row % 8 // 4, row % 4
    whole = table == (2 * x + half).astype(F32)
    picks = jnp.concatenate([ones_where(whole & (quarter == b)) for b in range(4)], 1)
    parts = jnp.concatenate([tokens_ref[:, b * SHARE : (b + 1) * SHARE] for b in range(4)], 0)
    out_ref[:, :SHARE] = dot(picks, parts).astype(BF)
    cut = table == (FIRST + half).astype(F32)
    picks = jnp.concatenate([ones_where(cut & (quarter == b)) for b in range(4)], 1)
    parts = jnp.concatenate(
        [
            tokens_ref[:, pl.ds(pl.multiple_of(x * SHARE + b * STRIP, STRIP), STRIP)]
            for b in range(4)
        ],
        0,
    )
    out_ref[:, SHARE:] = dot(picks, parts).astype(BF)


def pick_grads(pos_ref, ids_ref, flat_ref, grads_ref, tail_ref, *outs):
    x = pos_ref[0]
    pairs = TOK * TOP
    widen = ones_where(iota((TOK, pairs), 1) // TOP == iota((TOK, pairs), 0))
    ranks = dot(places(ids_ref[...]).astype(BF), widen)
    named = flat_ref[...] == iota((OWNERS, pairs), 0)
    table = jnp.where(named, ranks, -1.0)
    source, lane = iota((UNITS, STRIP), 0), iota((UNITS, STRIP), 1)
    grads = grads_ref[...]
    main = dot(grads, ones_where(source == lane)).astype(BF)
    twice = spread(table, 2)
    second = iota((SLOTS, pairs), 0) % 2
    for k, out in enumerate(outs):
        place = 2 * lax.rem(x + k, REPS) + second
        out[...] = dot(ones_where(twice == place.astype(F32)), main).astype(BF)
    tails = [
        dot(grads, ones_where((source // 64 == b) & (lane == 192 + source % 64))).astype(BF)
        for b in range(3)
    ]
    block = 256
    for start in range(0, ROWS, block):
        shape = (block, OWNERS)
        owner = (iota(shape, 0) + start) // FOLD == iota(shape, 1)
        eight = dot(ones_where(owner), table.astype(BF))
        row = iota((block, pairs), 0)
        late = eight == (FIRST + row % 8 // 4).astype(F32)
        total = jnp.zeros((block, STRIP), F32)
        for b in range(3):
            total += dot(ones_where(late & (row % 4 == b)), tails[b])
        tail_ref[start : start + block, :] = total.astype(BF)


def fold_grads(pos_ref, tail_ref, g0, g1, g2, g3, out_ref):
    x = pos_ref[0]
    row, column = iota((ROWS, SLOTS), 0), iota((ROWS, SLOTS), 1)
    total = tail_ref[...].astype(F32)
    for k, got in enumerate((g0, g1, g2, g3)):
        unit = lax.rem(x - k + REPS, REPS)
        total += dot(ones_where((row // 4 == column) & (row % 4 == unit)), got[...])
    out_ref[...] = total.astype(BF)


def stack_weights(pos_ref, probes_ref, own_ref, right_ref, top_ref, bottom_ref, left_ref, out_ref):
    x = pos_ref[0]
    half = UNITS // 2
    for w, k, start, size in (
        (own_ref, 0, 0, UNITS),
        (right_ref, 1, 0, UNITS),
        (top_ref, 2, 0, half),
        (bottom_ref, 2, half, half),
        (left_ref, 3, 0, UNITS),
    ):
        base = lax.rem(x + k, REPS) * UNITS + start
        out_ref[pl.ds(pl.multiple_of(base, half), size), :] = w[...]
    out_ref[FFW:, :] = probes_ref[...]


def unfold(source, put):
    shape = (256, 256)
    order = ones_where(iota(shape, 1) == 4 * (iota(shape, 0) % 64) + iota(shape, 0) // 64)
    for g in range(4):
        got = dot(order, source(slice(g * 256, (g + 1) * 256))).astype(BF)
        for b in range(4):
            put(b, slice(g * 64, (g + 1) * 64), got[b * 64 : (b + 1) * 64])


def cut_products(pos_ref, rows_ref, weights_ref, cut_ref, own_ref, o1, o2, o3):
    x = pos_ref[0]

    def put(b, at, got):
        cut_ref[at, b * STRIP : (b + 1) * STRIP] = got

    unfold(lambda at: rows_ref[at, SHARE:], put)
    cut = cut_ref[...]
    share = pl.ds(pl.multiple_of(x * SHARE, SHARE), SHARE)
    projected = dot(weights_ref[FFW:, share], cut, NT)
    for k, out in enumerate((own_ref, o1, o2, o3)):
        base = lax.rem(x + k, REPS) * UNITS
        weights = weights_ref[pl.ds(pl.multiple_of(base, UNITS), UNITS), share]
        out[:UNITS, :] = dot(weights, cut, NT).astype(out.dtype)
        out[UNITS:, :] = projected.astype(out.dtype)


def whole_products(
    pos_ref, rows_ref, weights_ref, gate_ref, own_ref, o1, o2, o3, whole_ref, sum_ref
):
    x = pos_ref[0]

    def put(b, at, got):
        whole_ref[at, b * SHARE : (b + 1) * SHARE] = got

    unfold(lambda at: rows_ref[at, :SHARE], put)
    whole = whole_ref[...]
    both = dot(weights_ref[...], whole, NT)
    gate_ref[...] = both[:FFW]
    sum_ref[...] = dot(both[FFW:].astype(BF), whole)
    for k, out in enumerate((own_ref, o1, o2, o3)):
        base = lax.rem(x + k, REPS) * SHARE
        out[...] = sum_ref[:, pl.ds(pl.multiple_of(base, SHARE), SHARE)].astype(out.dtype)


def gate_gradient(gate, grads):
    s = 1.0 / (1.0 + jnp.exp(-gate))
    return (grads * (s * (1.0 + gate * (1.0 - s)))).astype(BF)


def gate_part(
    pos_ref, grad_probes_ref, gate_ref, got_ref, s0, s1, s2, s3,
    cut_grad_ref, own_ref, out_ref, grads_ref, sketch_ref, padded_ref,
):
    x = pos_ref[0]

    def put(b, at, got):
        grads_ref[b * SLOTS + at.start : b * SLOTS + at.stop, :] = got

    unfold(lambda at: got_ref[at, :], put)
    same = ones_where(iota((STRIP, STRIP), 0) == iota((STRIP, STRIP), 1))
    turned = dot(same, grads_ref[...], NT)
    parts = [turned[:, b * SLOTS : (b + 1) * SLOTS] for b in range(4)]
    cut_gate = s0[:UNITS, :] + (
        s1[:UNITS, :].astype(F32) + s2[:UNITS, :].astype(F32) + s3[:UNITS, :].astype(F32)
    )
    cut_grad = gate_gradient(cut_gate, jnp.concatenate([p[UNITS:] for p in parts[:3]], 0))
    cut_grad_ref[...] = cut_grad
    mine = pl.ds(pl.multiple_of(x * UNITS, UNITS), UNITS)
    padded_ref[...] = jnp.zeros((FFW, SLOTS), BF)
    padded_ref[mine, :] = cut_grad
    cut_projected = dot(grad_probes_ref[...], padded_ref[...])
    whole = jnp.concatenate([p[:UNITS] for p in parts], 0)
    gate_grad = gate_gradient(gate_ref[...], whole)
    projected = dot(grad_probes_ref[...], gate_grad).astype(BF)
    sketch_ref[...] = dot(gate_grad, projected, NT)
    own_ref[:UNITS, :] = sketch_ref[mine, :]
    own_ref[UNITS : UNITS + R, :] = cut_projected[:, :128]
    own_ref[UNITS + R :, :] = cut_projected[:, 128:]
    for to in range(REPS):
        out_ref[to, :UNITS, :] = sketch_ref[to * UNITS : (to + 1) * UNITS, :].astype(BF)
        out_ref[to, UNITS : UNITS + R, :] = cut_projected[:, :128].astype(BF)
        out_ref[to, UNITS + R :, :] = cut_projected[:, 128:].astype(BF)


def finish_input(inverse_ref, cut_ref, s0, s1, s2, s3, i0, i1, i2, i3, out_ref):
    at = slice(UNITS, UNITS + R)
    projected = s0[at, :] + (
        s1[at, :].astype(F32) + s2[at, :].astype(F32) + s3[at, :].astype(F32)
    )
    total = i0[...] + dot(projected.astype(BF), cut_ref[...])
    total += i1[...].astype(F32) + i2[...].astype(F32) + i3[...].astype(F32)
    out_ref[...] = (total * inverse_ref[0]).T


def finish_grad(pos_ref, inverse_ref, cut_grad_ref, own_ref, parts_ref, out_ref):
    total = own_ref[...]
    for k in range(1, REPS):
        total += parts_ref[lax.rem(pos_ref[0] + k, REPS)].astype(F32)
    projected = total[UNITS:].astype(BF)
    sketch = total[:UNITS] + dot(cut_grad_ref[:, :128], projected[:R], NT)
    sketch += dot(cut_grad_ref[:, 128:], projected[R:], NT)
    out_ref[...] = sketch * inverse_ref[0]


def shift(block, k):
    return lax.ppermute(block, "rep", [(i, (i + k) % REPS) for i in range(REPS)])


def shifted(blocks):
    return [blocks[0]] + [shift(blocks[k], k) for k in range(1, REPS)]


def to_owners(rows):
    width = rows.shape[1]
    rows = rows.reshape(OWNERS, FOLD, width)
    return lax.all_to_all(rows, "ep", split_axis=0, concat_axis=0, tiled=True).reshape(ROWS, width)


def local(tokens, expert_ids, hidden_grads, gate_weight, probes, grad_probes, window_counts):
    sds = jax.ShapeDtypeStruct
    x = lax.axis_index("rep")
    pos = x.astype(jnp.int32).reshape(1)
    inverse = 1.0 / window_counts.astype(F32)
    ids_t = expert_ids.T
    flat_ids = expert_ids.reshape(1, TOK * TOP)

    out_rows = kernel_call(
        send_rows, sds((ROWS, SHARE + STRIP), BF), [SM] + [VM] * 2, 1 << 31, 4 << 20, 20
    )(pos, ids_t, tokens)
    rows = to_owners(out_rows)

    own = gate_weight[0]
    own, _ = lax.optimization_barrier((own, out_rows))
    left, right = shift(own, 1), shift(own, REPS - 1)

    tail, *picked = kernel_call(
        pick_grads,
        [sds((ROWS, STRIP), BF)] + [sds((SLOTS, STRIP), BF)] * REPS,
        [SM] + [VM] * 3,
        4 << 30,
        3 << 20,
        20,
    )(pos, ids_t, flat_ids, hidden_grads.reshape(TOK * TOP, UNITS))
    picked = shifted(picked)
    out_grads = kernel_call(
        fold_grads, sds((ROWS, STRIP), BF), [SM] + [VM] * 5, 1 << 29, 3 << 20, 12
    )(pos, tail, *picked)
    out_grads, left, right = lax.optimization_barrier((out_grads, left, right))
    top = shift(left[: UNITS // 2], 1)
    bottom = shift(right[UNITS // 2 :], REPS - 1)
    weights = kernel_call(
        stack_weights, sds((FFW + R, D), BF), [SM] + [VM] * 6, 1000, 14 << 20, 8
    )(pos, probes, own, right, top, bottom, left)
    got = to_owners(out_grads)

    kinds = [F32, BF, BF, BF]
    cut, *sums = kernel_call(
        cut_products,
        [sds((SLOTS, SHARE), BF)] + [sds((UNITS + R, SLOTS), kind) for kind in kinds],
        [SM] + [VM] * 2,
        1 << 29,
        4 << 20,
        12,
    )(pos, rows, weights)
    sums = shifted(sums)
    gate, *inputs = kernel_call(
        whole_products,
        [sds((FFW, SLOTS), F32)] + [sds((R, SHARE), kind) for kind in kinds],
        [SM] + [VM] * 2,
        3 << 30,
        14 << 20,
        16,
        [pltpu.VMEM((SLOTS, D), BF), pltpu.VMEM((R, D), F32)],
    )(pos, rows, weights)

    mixed = UNITS + 2 * R
    cut_grad, own_sketch, sketch = kernel_call(
        gate_part,
        [sds((UNITS, SLOTS), BF), sds((mixed, R), F32), sds((REPS, mixed, R), BF)],
        [SM] + [VM] * 7,
        2 << 30,
        4 << 20,
        16,
        [
            pltpu.VMEM((ROWS, STRIP), BF),
            pltpu.VMEM((FFW, R), F32),
            pltpu.VMEM((FFW, SLOTS), BF),
        ],
    )(pos, grad_probes, gate, got, *sums)
    *inputs, sketch = lax.optimization_barrier((*inputs, sketch))
    inputs = shifted(inputs)
    parts = lax.all_to_all(sketch, "rep", split_axis=0, concat_axis=0, tiled=True)

    input_sketch = kernel_call(
        finish_input, sds((SHARE, R), F32), [SM] + [VM] * 9, 1 << 27, 3 << 20, 8
    )(inverse, cut, *sums, *inputs)
    grad_sketch = kernel_call(
        finish_grad, sds((UNITS, R), F32), [SM] * 2 + [VM] * 3, 1 << 24, 1 << 20, 6
    )(pos, inverse, cut_grad, own_sketch, parts)
    return input_sketch[None], grad_sketch[None]


def solution(mesh):
    placed = (
        P("ep", None),
        P("ep", None),
        P("ep", None, "rep"),
        P("ep", "rep", None),
        P(),
        P(),
        P("ep"),
    )
    return jax.shard_map(
        local,
        mesh=mesh,
        in_specs=placed,
        out_specs=(P("ep", "rep", None), P("ep", "rep", None)),
        check_vma=False,
    )
```

```python
import jax
import jax.numpy as jnp
from jax import lax
from jax.experimental import pallas as pl
from jax.experimental.pallas import tpu as pltpu
from jax.sharding import PartitionSpec as P

OWNERS = 128
PAIRS = OWNERS // 2
REPS = 4
TOK = 128
TOP = 8
D = 4096
HALF = D // 2
SHARE = D // REPS
FFW = 768
UNITS = FFW // REPS
R = 128
FIRST = 8
FOLD = 8
ROWS = OWNERS * FOLD
SLOTS = OWNERS * 2
ALL = SLOTS + 128
STRIP = HALF // FOLD
MIB = 1 << 20

BF = jnp.bfloat16
F32 = jnp.float32
NT = (((1,), (1,)), ((), ()))
NN = (((1,), (0,)), ((), ()))

VM = pl.BlockSpec(memory_space=pltpu.VMEM)
SM = pl.BlockSpec(memory_space=pltpu.SMEM)


def dot(a, b, dims=NN):
    return lax.dot_general(a, b, dims, preferred_element_type=F32)


def iota(shape, axis):
    return lax.broadcasted_iota(jnp.int32, shape, axis)


def ones_where(mask):
    return jnp.where(mask, 1.0, 0.0).astype(BF)


def kernel_call(body, out_shape, in_specs, flops, bytes_accessed, limit, scratch=()):
    return pl.pallas_call(
        body,
        out_shape=out_shape,
        in_specs=in_specs,
        out_specs=jax.tree.map(lambda _: VM, out_shape),
        scratch_shapes=list(scratch),
        compiler_params=pltpu.CompilerParams(vmem_limit_bytes=limit * MIB),
        cost_estimate=pl.CostEstimate(
            flops=flops, bytes_accessed=bytes_accessed, transcendentals=0
        ),
    )


def places(ids_t):
    experts = iota((OWNERS, TOK), 0)
    named = jnp.zeros((OWNERS, TOK), F32)
    for k in range(TOP):
        named += jnp.where(ids_t[k : k + 1, :] == experts, 1.0, 0.0)
    before = ones_where(iota((TOK, TOK), 0) < iota((TOK, TOK), 1))
    rank = dot(named.astype(BF), before)
    return jnp.where(named > 0.0, rank, -1.0)


def pair_places(ids_t):
    pairs = TOK * TOP
    widen = ones_where(iota((TOK, pairs), 1) // TOP == iota((TOK, pairs), 0))
    ranks = dot(places(ids_t).astype(BF), widen)
    ids = dot(ids_t.astype(F32).astype(BF), widen)
    mine = iota((TOP, pairs), 1) % TOP == iota((TOP, pairs), 0)
    flat = jnp.sum(jnp.where(mine, ids, 0.0), axis=0, keepdims=True)
    return jnp.where(flat == iota((OWNERS, pairs), 0).astype(F32), ranks, -1.0)


def spread(table, times):
    shape = (OWNERS * times, OWNERS)
    return dot(ones_where(iota(shape, 0) // times == iota(shape, 1)), table.astype(BF))


def pack_half(pos_ref, ids_ref, tokens_ref, out_ref):
    out_ref[:TOK, :] = tokens_ref[...]
    out_ref[TOK:, :] = jnp.zeros((16, HALF), BF)
    ids = jnp.concatenate([ids_ref[...].astype(F32), jnp.zeros((8, TOK), F32)], 0)
    out_ref[TOK:, :TOK] = ids.astype(BF)


def other_ids(other_ref):
    return other_ref[TOK:, :TOK].astype(F32)[:TOP].astype(jnp.int32)


def send_rows(pos_ref, ids_ref, tokens_ref, other_ref, out_ref, half_ref, half_ids_ref, fold_ref):
    x, c = pos_ref[0], pos_ref[1]
    mine = x // 2 == c
    table = spread(places(ids_ref[...]), FOLD)
    row = iota((ROWS, TOK), 0)
    whole = table == (2 * x + row % 8 // 4).astype(F32)
    picks = jnp.concatenate([ones_where(whole & (row % 4 == b)) for b in range(4)], 1)
    parts = jnp.concatenate([tokens_ref[:, b * SHARE : (b + 1) * SHARE] for b in range(4)], 0)
    out_ref[:, :SHARE] = dot(picks, parts).astype(BF)

    @pl.when(mine)
    def _():
        half_ref[...] = tokens_ref[:, pl.ds(pl.multiple_of(c * HALF, HALF), HALF)]
        half_ids_ref[...] = ids_ref[...]

    @pl.when(jnp.logical_not(mine))
    def _():
        half_ref[...] = other_ref[:TOK, :]
        half_ids_ref[...] = other_ids(other_ref)

    picks = ones_where(places(half_ids_ref[...]) == (FIRST + x % 2).astype(F32))
    rows = dot(picks, half_ref[...])
    for b in range(FOLD):
        for h in range(2):
            start = b * STRIP + h * 128
            fold_ref[h, pl.ds(b, OWNERS, stride=FOLD), :] = rows[:, start : start + 128]
    for h in range(2):
        out_ref[:, SHARE + h * 128 : SHARE + (h + 1) * 128] = fold_ref[h].astype(BF)


def pick_grads(pos_ref, ids_ref, other_ref, grads_ref, other_grads_ref, *outs):
    x, c = pos_ref[0], pos_ref[1]
    pairs = TOK * TOP
    table, other_table = pair_places(ids_ref[...]), pair_places(other_ids(other_ref))
    embed = ones_where(iota((UNITS, 256), 0) == iota((UNITS, 256), 1))
    grads = dot(grads_ref[...], embed).astype(BF)
    other_grads = dot(other_grads_ref[...], embed).astype(BF)
    twice = spread(table, 2)
    second = iota((SLOTS, pairs), 0) % 2
    for k, out in enumerate(outs):
        to = lax.rem(x + k, REPS)
        out[:SLOTS, :] = dot(ones_where(twice == (2 * to + second).astype(F32)), grads).astype(BF)
        shared = FIRST + to % 2
        place = jnp.where(to // 2 == c, shared, -2).astype(F32)
        other_place = jnp.where(to // 2 == c, -2, shared).astype(F32)
        out[SLOTS:, :] = (
            dot(ones_where(table == place), grads)
            + dot(ones_where(other_table == other_place), other_grads)
        ).astype(BF)


def fold_grads(pos_ref, g0, g1, g2, g3, out_ref, fold_ref):
    x, c = pos_ref[0], pos_ref[1]
    for k, got in enumerate((g0, g1, g2, g3)):
        unit = lax.rem(x - k + REPS, REPS)
        for h in range(2):
            block = got[:SLOTS, h * 128 : (h + 1) * 128].astype(F32)
            fold_ref[h, pl.ds(unit, SLOTS, stride=4), :] = block
    for k, got in enumerate((g0, g1, g2, g3)):
        unit = lax.rem(x - k + REPS, REPS)

        @pl.when(unit // 2 == c)
        def _():
            source, lane = iota((256, 128), 0), iota((256, 128), 1)
            for u in range(3):
                move = ones_where((source // 64 == u) & (lane == 64 + source % 64))
                at = pl.ds(unit % 2 * 3 + u, OWNERS, stride=FOLD)
                fold_ref[1, at, :] = fold_ref[1, at, :] + dot(got[SLOTS:, :], move)

    for h in range(2):
        out_ref[:, h * 128 : (h + 1) * 128] = fold_ref[h].astype(BF)


def regroup(source, many, put):
    size = 256 // many
    shape = (256, 256)
    to = iota(shape, 0)
    order = ones_where(iota(shape, 1) == many * (to % size) + to // size)
    for g in range(ROWS // 256):
        got = dot(order, source(slice(g * 256, (g + 1) * 256))).astype(BF)
        for p in range(many):
            put(p, slice(g * size, (g + 1) * size), got[p * size : (p + 1) * size])


def stack_weights(pos_ref, probes_ref, own_ref, right_ref, top_ref, bottom_ref, left_ref, out_ref):
    x = pos_ref[0]
    half = UNITS // 2
    for w, k, start, size in (
        (own_ref, 0, 0, UNITS),
        (right_ref, 1, 0, UNITS),
        (top_ref, 2, 0, half),
        (bottom_ref, 2, half, half),
        (left_ref, 3, 0, UNITS),
    ):
        base = lax.rem(x + k, REPS) * UNITS + start
        out_ref[pl.ds(pl.multiple_of(base, half), size), :] = w[...]
    out_ref[FFW:, :] = probes_ref[...]


def products(
    pos_ref, rows_ref, weights_ref, gate_ref, i0, i1, i2, i3, rows_all_ref, sum_ref
):
    x = pos_ref[0]

    def put_whole(p, at, got):
        rows_all_ref[at, p * SHARE : (p + 1) * SHARE] = got

    def put_shared(p, at, got):
        rows_all_ref[SLOTS + at.start : SLOTS + at.stop, p * STRIP : (p + 1) * STRIP] = got

    regroup(lambda at: rows_ref[at, :SHARE], 4, put_whole)
    regroup(lambda at: rows_ref[at, SHARE:], 16, put_shared)
    rows_all_ref[SLOTS + PAIRS :, :] = jnp.zeros((ALL - SLOTS - PAIRS, D), BF)
    rows = rows_all_ref[...]
    both = dot(weights_ref[...], rows, NT)
    gate_ref[...] = both[:FFW]
    sum_ref[...] = dot(both[FFW:].astype(BF), rows)
    for k, out in enumerate((i0, i1, i2, i3)):
        base = lax.rem(x + k, REPS) * SHARE
        out[...] = sum_ref[:, pl.ds(pl.multiple_of(base, SHARE), SHARE)].astype(out.dtype)


def gate_part(
    pos_ref, grad_probes_ref, gate_ref, got_ref, own_ref, out_ref,
    whole_ref, shared_ref, sketch_ref,
):
    x = pos_ref[0]

    def put_whole(p, at, got):
        whole_ref[p * SLOTS + at.start : p * SLOTS + at.stop, :] = got

    def put_shared(p, at, got):
        shared_ref[p * PAIRS + at.start : p * PAIRS + at.stop, :] = got

    regroup(lambda at: got_ref[at, :], 4, put_whole)
    regroup(lambda at: got_ref[at, :], 16, put_shared)
    same = ones_where(iota((UNITS, 256), 0) == iota((UNITS, 256), 1))
    whole = dot(same, whole_ref[...], NT)
    last = ones_where(iota((64, 256), 0) + UNITS == iota((64, 256), 1))
    shared = dot(last, shared_ref[...], NT)
    turned = pltpu.roll(shared, ROWS - PAIRS, 1)
    parts = []
    for p in (0, 1, 2, 3, 4, 5, 8, 9, 10, 11, 12, 13):
        at = p // 2 * 128
        parts.append((turned if p % 2 else shared)[:, at : at + 128])
    late = jnp.concatenate(parts, 0)
    late = jnp.where(iota((FFW, 128), 1) < PAIRS, late, 0.0)
    early = jnp.concatenate([whole[:, b * SLOTS : (b + 1) * SLOTS] for b in range(4)], 0)
    grads = jnp.concatenate([early, late], 1)
    gate = gate_ref[...]
    s = 1.0 / (1.0 + jnp.exp(-gate))
    gate_grad = (grads * (s * (1.0 + gate * (1.0 - s)))).astype(BF)
    projected = dot(grad_probes_ref[...], gate_grad).astype(BF)
    sketch_ref[...] = dot(gate_grad, projected, NT)
    out_ref[...] = sketch_ref[...].astype(BF)
    own_ref[...] = sketch_ref[pl.ds(pl.multiple_of(x * UNITS, UNITS), UNITS), :]


def finish_input(inverse_ref, i0, i1, i2, i3, out_ref):
    total = i0[...] + (i1[...].astype(F32) + i2[...].astype(F32) + i3[...].astype(F32))
    out_ref[...] = (total * inverse_ref[0]).T


def finish_grad(pos_ref, inverse_ref, own_ref, parts_ref, out_ref):
    total = own_ref[...]
    for k in range(1, REPS):
        total += parts_ref[lax.rem(pos_ref[0] + k, REPS)].astype(F32)
    out_ref[...] = total * inverse_ref[0]


def shift(block, k):
    return lax.ppermute(block, "rep", [(i, (i + k) % REPS) for i in range(REPS)])


def shifted(blocks):
    return [blocks[0]] + [shift(blocks[k], k) for k in range(1, REPS)]


def swap(block):
    return lax.ppermute(block, "ep", [(i, i ^ 1) for i in range(OWNERS)])


def to_owners(rows):
    width = rows.shape[1]
    rows = rows.reshape(OWNERS, FOLD, width)
    return lax.all_to_all(rows, "ep", split_axis=0, concat_axis=0, tiled=True).reshape(ROWS, width)


def local(tokens, expert_ids, hidden_grads, gate_weight, probes, grad_probes, window_counts):
    sds = jax.ShapeDtypeStruct
    pos = jnp.stack([lax.axis_index("rep"), lax.axis_index("ep") % 2]).astype(jnp.int32)
    inverse = 1.0 / window_counts.astype(F32)
    ids_t = expert_ids.T

    packed = pl.pallas_call(
        pack_half,
        out_shape=sds((TOK + 16, HALF), BF),
        grid_spec=pltpu.PrefetchScalarGridSpec(
            num_scalar_prefetch=1,
            grid=(1,),
            in_specs=[VM, pl.BlockSpec((TOK, HALF), lambda i, pos: (0, 1 - pos[1]))],
            out_specs=VM,
        ),
        compiler_params=pltpu.CompilerParams(vmem_limit_bytes=6 * MIB),
        cost_estimate=pl.CostEstimate(flops=1000, bytes_accessed=MIB, transcendentals=0),
    )(pos, ids_t, tokens)
    other = swap(packed)
    out_rows = kernel_call(
        send_rows,
        sds((ROWS, SHARE + STRIP), BF),
        [SM] + [VM] * 3,
        1 << 31,
        5 * MIB,
        20,
        [
            pltpu.VMEM((TOK, HALF), BF),
            pltpu.VMEM((TOP, TOK), jnp.int32),
            pltpu.VMEM((2, ROWS, 128), F32),
        ],
    )(pos, ids_t, tokens, other)
    rows = to_owners(out_rows)

    own, grads = gate_weight[0], hidden_grads.reshape(TOK * TOP, UNITS)
    own, grads, _ = lax.optimization_barrier((own, grads, out_rows))
    left, right = shift(own, 1), shift(own, REPS - 1)
    other_grads = swap(grads)
    picked = kernel_call(
        pick_grads, [sds((SLOTS + OWNERS, 256), BF)] * REPS, [SM] + [VM] * 4, 5 << 30, 3 * MIB, 20
    )(pos, ids_t, other, grads, other_grads)
    left, right, _ = lax.optimization_barrier((left, right, picked[1]))
    top = shift(left[: UNITS // 2], 1)
    bottom = shift(right[UNITS // 2 :], REPS - 1)
    out_grads = kernel_call(
        fold_grads,
        sds((ROWS, 256), BF),
        [SM] + [VM] * 4,
        1 << 27,
        3 * MIB,
        8,
        [pltpu.VMEM((2, ROWS, 128), F32)],
    )(pos, *shifted(picked))
    weights = kernel_call(
        stack_weights, sds((FFW + R, D), BF), [SM] + [VM] * 6, 1000, 14 * MIB, 8
    )(pos, probes, own, right, top, bottom, left)
    got = to_owners(out_grads)

    kinds = [F32, BF, BF, BF]
    gate, *inputs = kernel_call(
        products,
        [sds((FFW, ALL), F32)] + [sds((R, SHARE), kind) for kind in kinds],
        [SM] + [VM] * 2,
        4 << 30,
        12 * MIB,
        20,
        [pltpu.VMEM((ALL, D), BF), pltpu.VMEM((R, D), F32)],
    )(pos, rows, weights)
    inputs = shifted(inputs)

    own_sketch, sketch = kernel_call(
        gate_part,
        [sds((UNITS, R), F32), sds((FFW, R), BF)],
        [SM] + [VM] * 3,
        1 << 30,
        3 * MIB,
        14,
        [pltpu.VMEM((ROWS, 256), BF), pltpu.VMEM((ROWS, 256), BF), pltpu.VMEM((FFW, R), F32)],
    )(pos, grad_probes, gate, got)
    sketches = lax.all_to_all(
        sketch.reshape(REPS, UNITS, R), "rep", split_axis=0, concat_axis=0, tiled=True
    )

    input_sketch = kernel_call(
        finish_input, sds((SHARE, R), F32), [SM] + [VM] * 4, 1 << 20, 2 * MIB, 6
    )(inverse, *inputs)
    grad_sketch = kernel_call(
        finish_grad, sds((UNITS, R), F32), [SM] * 2 + [VM] * 2, 1 << 18, MIB // 4, 4
    )(pos, inverse, own_sketch, sketches)
    return input_sketch[None], grad_sketch[None]


def solution(mesh):
    placed = (
        P("ep", None),
        P("ep", None),
        P("ep", None, "rep"),
        P("ep", "rep", None),
        P(),
        P(),
        P("ep"),
    )
    return jax.shard_map(
        local,
        mesh=mesh,
        in_specs=placed,
        out_specs=(P("ep", "rep", None), P("ep", "rep", None)),
        check_vma=False,
    )
```

```python
import jax
import jax.numpy as jnp
from jax import lax
from jax.experimental import pallas as pl
from jax.experimental.pallas import tpu as pltpu
from jax.sharding import PartitionSpec as P

OWNERS = 128
PAIRS = OWNERS // 2
REPS = 4
TOK = 128
TOP = 8
D = 4096
HALF = D // 2
SHARE = D // REPS
FFW = 768
UNITS = FFW // REPS
R = 128
FIRST = 8
FOLD = 8
ROWS = OWNERS * FOLD
SLOTS = OWNERS * 2
ALL = SLOTS + 128
STRIP = HALF // FOLD
MIB = 1 << 20

BF = jnp.bfloat16
F32 = jnp.float32
NT = (((1,), (1,)), ((), ()))
NN = (((1,), (0,)), ((), ()))

VM = pl.BlockSpec(memory_space=pltpu.VMEM)
SM = pl.BlockSpec(memory_space=pltpu.SMEM)


def dot(a, b, dims=NN):
    return lax.dot_general(a, b, dims, preferred_element_type=F32)


def iota(shape, axis):
    return lax.broadcasted_iota(jnp.int32, shape, axis)


def ones_where(mask):
    return jnp.where(mask, 1.0, 0.0).astype(BF)


def kernel_call(body, out_shape, in_specs, flops, bytes_accessed, limit, scratch=()):
    return pl.pallas_call(
        body,
        out_shape=out_shape,
        in_specs=in_specs,
        out_specs=jax.tree.map(lambda _: VM, out_shape),
        scratch_shapes=list(scratch),
        compiler_params=pltpu.CompilerParams(vmem_limit_bytes=limit * MIB),
        cost_estimate=pl.CostEstimate(
            flops=flops, bytes_accessed=bytes_accessed, transcendentals=0
        ),
    )


def places(ids_t):
    experts = iota((OWNERS, TOK), 0)
    named = jnp.zeros((OWNERS, TOK), F32)
    for k in range(TOP):
        named += jnp.where(ids_t[k : k + 1, :] == experts, 1.0, 0.0)
    before = ones_where(iota((TOK, TOK), 0) < iota((TOK, TOK), 1))
    rank = dot(named.astype(BF), before)
    return jnp.where(named > 0.0, rank, -1.0)


def pair_places(ids_t):
    pairs = TOK * TOP
    widen = ones_where(iota((TOK, pairs), 1) // TOP == iota((TOK, pairs), 0))
    ranks = dot(places(ids_t).astype(BF), widen)
    ids = dot(ids_t.astype(F32).astype(BF), widen)
    mine = iota((TOP, pairs), 1) % TOP == iota((TOP, pairs), 0)
    flat = jnp.sum(jnp.where(mine, ids, 0.0), axis=0, keepdims=True)
    return jnp.where(flat == iota((OWNERS, pairs), 0).astype(F32), ranks, -1.0)


def spread(table, times):
    shape = (OWNERS * times, OWNERS)
    return dot(ones_where(iota(shape, 0) // times == iota(shape, 1)), table.astype(BF))


def pack_half(pos_ref, ids_ref, tokens_ref, out_ref):
    out_ref[:TOK, :] = tokens_ref[...]
    out_ref[TOK:, :] = jnp.zeros((16, HALF), BF)
    ids = jnp.concatenate([ids_ref[...].astype(F32), jnp.zeros((8, TOK), F32)], 0)
    out_ref[TOK:, :TOK] = ids.astype(BF)


def other_ids(other_ref):
    return other_ref[TOK:, :TOK].astype(F32)[:TOP].astype(jnp.int32)


def fold(picked, many, put):
    size = 256 // many
    width = picked.shape[1] // many
    shape = (256, 256)
    to = iota(shape, 0)
    order = ones_where(iota(shape, 1) == to % many * size + to // many)
    for g in range(ROWS // 256):
        at = slice(g * size, (g + 1) * size)
        parts = [picked[at, p * width : (p + 1) * width] for p in range(many)]
        put(slice(g * 256, (g + 1) * 256), dot(order, jnp.concatenate(parts, 0)).astype(BF))


def send_rows(pos_ref, ids_ref, tokens_ref, other_ref, out_ref, half_ref, half_ids_ref):
    x, c = pos_ref[0], pos_ref[1]
    mine = x // 2 == c
    table = spread(places(ids_ref[...]), 2)
    place = 2 * x + iota(table.shape, 0) % 2
    picked = dot(ones_where(table == place.astype(F32)), tokens_ref[...]).astype(BF)

    def put_whole(at, got):
        out_ref[at, :SHARE] = got

    fold(picked, 4, put_whole)

    @pl.when(mine)
    def _():
        half_ref[...] = tokens_ref[:, pl.ds(pl.multiple_of(c * HALF, HALF), HALF)]
        half_ids_ref[...] = ids_ref[...]

    @pl.when(jnp.logical_not(mine))
    def _():
        half_ref[...] = other_ref[:TOK, :]
        half_ids_ref[...] = other_ids(other_ref)

    table = places(half_ids_ref[...])
    picked = dot(ones_where(table == (FIRST + x % 2).astype(F32)), half_ref[...]).astype(BF)

    def put_shared(at, got):
        out_ref[at, SHARE:] = got

    fold(picked, FOLD, put_shared)


def pick_grads(pos_ref, ids_ref, other_ref, grads_ref, other_grads_ref, *outs):
    x, c = pos_ref[0], pos_ref[1]
    pairs = TOK * TOP
    table, other_table = pair_places(ids_ref[...]), pair_places(other_ids(other_ref))
    embed = ones_where(iota((UNITS, 256), 0) == iota((UNITS, 256), 1))
    grads = dot(grads_ref[...], embed).astype(BF)
    other_grads = dot(other_grads_ref[...], embed).astype(BF)
    twice = spread(table, 2)
    second = iota((SLOTS, pairs), 0) % 2
    for k, out in enumerate(outs):
        to = lax.rem(x + k, REPS)
        out[:SLOTS, :] = dot(ones_where(twice == (2 * to + second).astype(F32)), grads).astype(BF)
        shared = FIRST + to % 2
        place = jnp.where(to // 2 == c, shared, -2).astype(F32)
        other_place = jnp.where(to // 2 == c, -2, shared).astype(F32)
        out[SLOTS:, :] = (
            dot(ones_where(table == place), grads)
            + dot(ones_where(other_table == other_place), other_grads)
        ).astype(BF)


def fold_grads(pos_ref, g0, g1, g2, g3, out_ref, fold_ref):
    x, c = pos_ref[0], pos_ref[1]
    for k, got in enumerate((g0, g1, g2, g3)):
        unit = lax.rem(x - k + REPS, REPS)
        for h in range(2):
            block = got[:SLOTS, h * 128 : (h + 1) * 128].astype(F32)
            fold_ref[h, pl.ds(unit, SLOTS, stride=4), :] = block
    for k, got in enumerate((g0, g1, g2, g3)):
        unit = lax.rem(x - k + REPS, REPS)

        @pl.when(unit // 2 == c)
        def _():
            source, lane = iota((256, 128), 0), iota((256, 128), 1)
            for u in range(3):
                move = ones_where((source // 64 == u) & (lane == 64 + source % 64))
                at = pl.ds(unit % 2 * 3 + u, OWNERS, stride=FOLD)
                fold_ref[1, at, :] = fold_ref[1, at, :] + dot(got[SLOTS:, :], move)

    for h in range(2):
        out_ref[:, h * 128 : (h + 1) * 128] = fold_ref[h].astype(BF)


def regroup(source, many, put):
    size = 256 // many
    shape = (256, 256)
    to = iota(shape, 0)
    order = ones_where(iota(shape, 1) == many * (to % size) + to // size)
    for g in range(ROWS // 256):
        got = dot(order, source(slice(g * 256, (g + 1) * 256))).astype(BF)
        for p in range(many):
            put(p, slice(g * size, (g + 1) * size), got[p * size : (p + 1) * size])


def stack_weights(pos_ref, probes_ref, own_ref, right_ref, top_ref, bottom_ref, left_ref, out_ref):
    x = pos_ref[0]
    half = UNITS // 2
    for w, k, start, size in (
        (own_ref, 0, 0, UNITS),
        (right_ref, 1, 0, UNITS),
        (top_ref, 2, 0, half),
        (bottom_ref, 2, half, half),
        (left_ref, 3, 0, UNITS),
    ):
        base = lax.rem(x + k, REPS) * UNITS + start
        out_ref[pl.ds(pl.multiple_of(base, half), size), :] = w[...]
    out_ref[FFW:, :] = probes_ref[...]


def products(
    pos_ref, rows_ref, weights_ref, gate_ref, i0, i1, i2, i3, rows_all_ref, sum_ref
):
    x = pos_ref[0]

    def put_whole(p, at, got):
        rows_all_ref[at, p * SHARE : (p + 1) * SHARE] = got

    def put_shared(p, at, got):
        rows_all_ref[SLOTS + at.start : SLOTS + at.stop, p * STRIP : (p + 1) * STRIP] = got

    regroup(lambda at: rows_ref[at, :SHARE], 4, put_whole)
    regroup(lambda at: rows_ref[at, SHARE:], 16, put_shared)
    rows_all_ref[SLOTS + PAIRS :, :] = jnp.zeros((ALL - SLOTS - PAIRS, D), BF)
    rows = rows_all_ref[...]
    both = dot(weights_ref[...], rows, NT)
    gate_ref[...] = both[:FFW]
    sum_ref[...] = dot(both[FFW:].astype(BF), rows)
    for k, out in enumerate((i0, i1, i2, i3)):
        base = lax.rem(x + k, REPS) * SHARE
        out[...] = sum_ref[:, pl.ds(pl.multiple_of(base, SHARE), SHARE)].astype(out.dtype)


def gate_part(
    pos_ref, grad_probes_ref, gate_ref, got_ref, own_ref, out_ref,
    whole_ref, shared_ref, sketch_ref,
):
    x = pos_ref[0]

    def put_whole(p, at, got):
        whole_ref[p * SLOTS + at.start : p * SLOTS + at.stop, :] = got

    def put_shared(p, at, got):
        shared_ref[p * PAIRS + at.start : p * PAIRS + at.stop, :] = got

    regroup(lambda at: got_ref[at, :], 4, put_whole)
    regroup(lambda at: got_ref[at, :], 16, put_shared)
    same = ones_where(iota((UNITS, 256), 0) == iota((UNITS, 256), 1))
    whole = dot(same, whole_ref[...], NT)
    last = ones_where(iota((64, 256), 0) + UNITS == iota((64, 256), 1))
    shared = dot(last, shared_ref[...], NT)
    turned = pltpu.roll(shared, ROWS - PAIRS, 1)
    parts = []
    for p in (0, 1, 2, 3, 4, 5, 8, 9, 10, 11, 12, 13):
        at = p // 2 * 128
        parts.append((turned if p % 2 else shared)[:, at : at + 128])
    late = jnp.concatenate(parts, 0)
    late = jnp.where(iota((FFW, 128), 1) < PAIRS, late, 0.0)
    early = jnp.concatenate([whole[:, b * SLOTS : (b + 1) * SLOTS] for b in range(4)], 0)
    grads = jnp.concatenate([early, late], 1)
    gate = gate_ref[...]
    s = 1.0 / (1.0 + jnp.exp(-gate))
    gate_grad = (grads * (s * (1.0 + gate * (1.0 - s)))).astype(BF)
    projected = dot(grad_probes_ref[...], gate_grad).astype(BF)
    sketch_ref[...] = dot(gate_grad, projected, NT)
    out_ref[...] = sketch_ref[...].astype(BF)
    own_ref[...] = sketch_ref[pl.ds(pl.multiple_of(x * UNITS, UNITS), UNITS), :]


def finish_input(inverse_ref, i0, i1, i2, i3, out_ref):
    total = i0[...] + (i1[...].astype(F32) + i2[...].astype(F32) + i3[...].astype(F32))
    out_ref[...] = (total * inverse_ref[0]).T


def finish_grad(pos_ref, inverse_ref, own_ref, parts_ref, out_ref):
    total = own_ref[...]
    for k in range(1, REPS):
        total += parts_ref[lax.rem(pos_ref[0] + k, REPS)].astype(F32)
    out_ref[...] = total * inverse_ref[0]


def shift(block, k):
    return lax.ppermute(block, "rep", [(i, (i + k) % REPS) for i in range(REPS)])


def shifted(blocks):
    return [blocks[0]] + [shift(blocks[k], k) for k in range(1, REPS)]


def swap(block):
    return lax.ppermute(block, "ep", [(i, i ^ 1) for i in range(OWNERS)])


def to_owners(rows):
    width = rows.shape[1]
    rows = rows.reshape(OWNERS, FOLD, width)
    return lax.all_to_all(rows, "ep", split_axis=0, concat_axis=0, tiled=True).reshape(ROWS, width)


def local(tokens, expert_ids, hidden_grads, gate_weight, probes, grad_probes, window_counts):
    sds = jax.ShapeDtypeStruct
    pos = jnp.stack([lax.axis_index("rep"), lax.axis_index("ep") % 2]).astype(jnp.int32)
    inverse = 1.0 / window_counts.astype(F32)
    ids_t = expert_ids.T

    packed = pl.pallas_call(
        pack_half,
        out_shape=sds((TOK + 16, HALF), BF),
        grid_spec=pltpu.PrefetchScalarGridSpec(
            num_scalar_prefetch=1,
            grid=(1,),
            in_specs=[VM, pl.BlockSpec((TOK, HALF), lambda i, pos: (0, 1 - pos[1]))],
            out_specs=VM,
        ),
        compiler_params=pltpu.CompilerParams(vmem_limit_bytes=6 * MIB),
        cost_estimate=pl.CostEstimate(flops=1000, bytes_accessed=MIB, transcendentals=0),
    )(pos, ids_t, tokens)
    other = swap(packed)
    out_rows = kernel_call(
        send_rows,
        sds((ROWS, SHARE + STRIP), BF),
        [SM] + [VM] * 3,
        1 << 30,
        5 * MIB,
        20,
        [pltpu.VMEM((TOK, HALF), BF), pltpu.VMEM((TOP, TOK), jnp.int32)],
    )(pos, ids_t, tokens, other)
    rows = to_owners(out_rows)

    own, grads = gate_weight[0], hidden_grads.reshape(TOK * TOP, UNITS)
    own, grads, _ = lax.optimization_barrier((own, grads, out_rows))
    left, right = shift(own, 1), shift(own, REPS - 1)
    other_grads = swap(grads)
    picked = kernel_call(
        pick_grads, [sds((SLOTS + OWNERS, 256), BF)] * REPS, [SM] + [VM] * 4, 5 << 30, 3 * MIB, 20
    )(pos, ids_t, other, grads, other_grads)
    left, right, _ = lax.optimization_barrier((left, right, picked[1]))
    top = shift(left[: UNITS // 2], 1)
    bottom = shift(right[UNITS // 2 :], REPS - 1)
    out_grads = kernel_call(
        fold_grads,
        sds((ROWS, 256), BF),
        [SM] + [VM] * 4,
        1 << 27,
        3 * MIB,
        8,
        [pltpu.VMEM((2, ROWS, 128), F32)],
    )(pos, *shifted(picked))
    weights = kernel_call(
        stack_weights, sds((FFW + R, D), BF), [SM] + [VM] * 6, 1000, 14 * MIB, 8
    )(pos, probes, own, right, top, bottom, left)
    got = to_owners(out_grads)

    kinds = [F32, BF, BF, BF]
    gate, *inputs = kernel_call(
        products,
        [sds((FFW, ALL), F32)] + [sds((R, SHARE), kind) for kind in kinds],
        [SM] + [VM] * 2,
        4 << 30,
        12 * MIB,
        20,
        [pltpu.VMEM((ALL, D), BF), pltpu.VMEM((R, D), F32)],
    )(pos, rows, weights)
    inputs = shifted(inputs)

    own_sketch, sketch = kernel_call(
        gate_part,
        [sds((UNITS, R), F32), sds((FFW, R), BF)],
        [SM] + [VM] * 3,
        1 << 30,
        3 * MIB,
        14,
        [pltpu.VMEM((ROWS, 256), BF), pltpu.VMEM((ROWS, 256), BF), pltpu.VMEM((FFW, R), F32)],
    )(pos, grad_probes, gate, got)
    sketches = lax.all_to_all(
        sketch.reshape(REPS, UNITS, R), "rep", split_axis=0, concat_axis=0, tiled=True
    )

    input_sketch = kernel_call(
        finish_input, sds((SHARE, R), F32), [SM] + [VM] * 4, 1 << 20, 2 * MIB, 6
    )(inverse, *inputs)
    own_sketch, input_sketch = lax.optimization_barrier((own_sketch, input_sketch))
    grad_sketch = kernel_call(
        finish_grad, sds((UNITS, R), F32), [SM] * 2 + [VM] * 2, 1 << 18, MIB // 4, 4
    )(pos, inverse, own_sketch, sketches)
    return input_sketch[None], grad_sketch[None]


def solution(mesh):
    placed = (
        P("ep", None),
        P("ep", None),
        P("ep", None, "rep"),
        P("ep", "rep", None),
        P(),
        P(),
        P("ep"),
    )
    return jax.shard_map(
        local,
        mesh=mesh,
        in_specs=placed,
        out_specs=(P("ep", "rep", None), P("ep", "rep", None)),
        check_vma=False,
    )
```

```python
import jax
import jax.numpy as jnp
from jax import lax
from jax.experimental import pallas as pl
from jax.experimental.pallas import tpu as pltpu
from jax.sharding import PartitionSpec as P

OWNERS = 128
PAIRS = OWNERS // 2
REPS = 4
TOK = 128
TOP = 8
D = 4096
HALF = D // 2
SHARE = D // REPS
FFW = 768
UNITS = FFW // REPS
R = 128
FIRST = 8
FOLD = 8
ROWS = OWNERS * FOLD
SLOTS = OWNERS * 2
ALL = SLOTS + 128
STRIP = HALF // FOLD
MIB = 1 << 20

BF = jnp.bfloat16
F32 = jnp.float32
NT = (((1,), (1,)), ((), ()))
NN = (((1,), (0,)), ((), ()))

VM = pl.BlockSpec(memory_space=pltpu.VMEM)
SM = pl.BlockSpec(memory_space=pltpu.SMEM)


def dot(a, b, dims=NN):
    return lax.dot_general(a, b, dims, preferred_element_type=F32)


def iota(shape, axis):
    return lax.broadcasted_iota(jnp.int32, shape, axis)


def ones_where(mask):
    return jnp.where(mask, 1.0, 0.0).astype(BF)


def kernel_call(body, out_shape, in_specs, flops, bytes_accessed, limit, scratch=(), out_specs=None):
    return pl.pallas_call(
        body,
        out_shape=out_shape,
        in_specs=in_specs,
        out_specs=out_specs or jax.tree.map(lambda _: VM, out_shape),
        scratch_shapes=list(scratch),
        compiler_params=pltpu.CompilerParams(vmem_limit_bytes=limit * MIB),
        cost_estimate=pl.CostEstimate(
            flops=flops, bytes_accessed=bytes_accessed, transcendentals=0
        ),
    )


def places(ids_t):
    experts = iota((OWNERS, TOK), 0)
    named = jnp.zeros((OWNERS, TOK), F32)
    for k in range(TOP):
        named += jnp.where(ids_t[k : k + 1, :] == experts, 1.0, 0.0)
    before = ones_where(iota((TOK, TOK), 0) < iota((TOK, TOK), 1))
    rank = dot(named.astype(BF), before)
    return jnp.where(named > 0.0, rank, -1.0)


def pair_places(ids_t):
    pairs = TOK * TOP
    widen = ones_where(iota((TOK, pairs), 1) // TOP == iota((TOK, pairs), 0))
    ranks = dot(places(ids_t).astype(BF), widen)
    ids = dot(ids_t.astype(F32).astype(BF), widen)
    mine = iota((TOP, pairs), 1) % TOP == iota((TOP, pairs), 0)
    flat = jnp.sum(jnp.where(mine, ids, 0.0), axis=0, keepdims=True)
    return jnp.where(flat == iota((OWNERS, pairs), 0).astype(F32), ranks, -1.0)


def spread(table, times):
    shape = (OWNERS * times, OWNERS)
    return dot(ones_where(iota(shape, 0) // times == iota(shape, 1)), table.astype(BF))


def pack_half(pos_ref, ids_ref, tokens_ref, out_ref):
    out_ref[:TOK, :] = tokens_ref[...]
    out_ref[TOK:, :] = jnp.zeros((16, HALF), BF)
    ids = jnp.concatenate([ids_ref[...].astype(F32), jnp.zeros((8, TOK), F32)], 0)
    out_ref[TOK:, :TOK] = ids.astype(BF)


def other_ids(other_ref):
    return other_ref[TOK:, :TOK].astype(F32)[:TOP].astype(jnp.int32)


def fold(picked, many, g):
    size = 256 // many
    width = picked.shape[1] // many
    shape = (256, 256)
    to = iota(shape, 0)
    order = ones_where(iota(shape, 1) == to % many * size + to // many)
    at = slice(g * size, (g + 1) * size)
    parts = [picked[at, p * width : (p + 1) * width] for p in range(many)]
    return dot(order, jnp.concatenate(parts, 0)).astype(BF)


def send_rows(
    pos_ref, ids_ref, tokens_ref, other_ref, out_ref, made_ref, half_ref, half_ids_ref, sems
):
    x, c = pos_ref[0], pos_ref[1]
    mine = x // 2 == c

    @pl.when(mine)
    def _():
        half_ref[...] = tokens_ref[:, pl.ds(pl.multiple_of(c * HALF, HALF), HALF)]
        half_ids_ref[...] = ids_ref[...]

    @pl.when(jnp.logical_not(mine))
    def _():
        half_ref[...] = other_ref[:TOK, :]
        half_ids_ref[...] = other_ids(other_ref)

    table = places(half_ids_ref[...])
    shared = dot(ones_where(table == (FIRST + x % 2).astype(F32)), half_ref[...]).astype(BF)
    table = spread(places(ids_ref[...]), 2)
    place = 2 * x + iota(table.shape, 0) % 2
    picks = ones_where(table == place.astype(F32))
    copies = []
    for g in range(ROWS // 256):
        at = slice(g * 256, (g + 1) * 256)
        whole = dot(picks[g * 64 : (g + 1) * 64], tokens_ref[...]).astype(BF)
        made_ref[at, :SHARE] = fold(whole, 4, 0)
        made_ref[at, SHARE:] = fold(shared, FOLD, g)
        copy = pltpu.make_async_copy(made_ref.at[at, :], out_ref.at[at, :], sems.at[g])
        copy.start()
        copies.append(copy)
    for copy in copies:
        copy.wait()


def pick_grads(pos_ref, ids_ref, other_ref, grads_ref, other_grads_ref, *outs):
    x, c = pos_ref[0], pos_ref[1]
    pairs = TOK * TOP
    table, other_table = pair_places(ids_ref[...]), pair_places(other_ids(other_ref))
    embed = ones_where(iota((UNITS, 256), 0) == iota((UNITS, 256), 1))
    grads = dot(grads_ref[...], embed).astype(BF)
    other_grads = dot(other_grads_ref[...], embed).astype(BF)
    twice = spread(table, 2)
    second = iota((SLOTS, pairs), 0) % 2
    for k, out in enumerate(outs):
        to = lax.rem(x + k, REPS)
        out[:SLOTS, :] = dot(ones_where(twice == (2 * to + second).astype(F32)), grads).astype(BF)
        shared = FIRST + to % 2
        place = jnp.where(to // 2 == c, shared, -2).astype(F32)
        other_place = jnp.where(to // 2 == c, -2, shared).astype(F32)
        out[SLOTS:, :] = (
            dot(ones_where(table == place), grads)
            + dot(ones_where(other_table == other_place), other_grads)
        ).astype(BF)


def fold_grads(pos_ref, g0, g1, g2, g3, out_ref, fold_ref):
    x, c = pos_ref[0], pos_ref[1]
    for k, got in enumerate((g0, g1, g2, g3)):
        unit = lax.rem(x - k + REPS, REPS)
        for h in range(2):
            block = got[:SLOTS, h * 128 : (h + 1) * 128].astype(F32)
            fold_ref[h, pl.ds(unit, SLOTS, stride=4), :] = block
    for k, got in enumerate((g0, g1, g2, g3)):
        unit = lax.rem(x - k + REPS, REPS)

        @pl.when(unit // 2 == c)
        def _():
            source, lane = iota((256, 128), 0), iota((256, 128), 1)
            for u in range(3):
                move = ones_where((source // 64 == u) & (lane == 64 + source % 64))
                at = pl.ds(unit % 2 * 3 + u, OWNERS, stride=FOLD)
                fold_ref[1, at, :] = fold_ref[1, at, :] + dot(got[SLOTS:, :], move)

    for h in range(2):
        out_ref[:, h * 128 : (h + 1) * 128] = fold_ref[h].astype(BF)


def regroup(source, many, put):
    size = 256 // many
    shape = (256, 256)
    to = iota(shape, 0)
    order = ones_where(iota(shape, 1) == many * (to % size) + to // size)
    for g in range(ROWS // 256):
        got = dot(order, source(slice(g * 256, (g + 1) * 256))).astype(BF)
        for p in range(many):
            put(p, slice(g * size, (g + 1) * size), got[p * size : (p + 1) * size])


def stack_weights(pos_ref, probes_ref, own_ref, right_ref, top_ref, bottom_ref, left_ref, out_ref):
    x = pos_ref[0]
    half = UNITS // 2
    for w, k, start, size in (
        (own_ref, 0, 0, UNITS),
        (right_ref, 1, 0, UNITS),
        (top_ref, 2, 0, half),
        (bottom_ref, 2, half, half),
        (left_ref, 3, 0, UNITS),
    ):
        base = lax.rem(x + k, REPS) * UNITS + start
        out_ref[pl.ds(pl.multiple_of(base, half), size), :] = w[...]
    out_ref[FFW:, :] = probes_ref[...]


def products(
    pos_ref, rows_ref, weights_ref, slope_ref, i0, i1, i2, i3, rows_all_ref, sum_ref
):
    x = pos_ref[0]

    def put_whole(p, at, got):
        rows_all_ref[at, p * SHARE : (p + 1) * SHARE] = got

    def put_shared(p, at, got):
        rows_all_ref[SLOTS + at.start : SLOTS + at.stop, p * STRIP : (p + 1) * STRIP] = got

    regroup(lambda at: rows_ref[at, :SHARE], 4, put_whole)
    regroup(lambda at: rows_ref[at, SHARE:], 16, put_shared)
    rows_all_ref[SLOTS + PAIRS :, :] = jnp.zeros((ALL - SLOTS - PAIRS, D), BF)
    rows = rows_all_ref[...]
    both = dot(weights_ref[...], rows, NT)
    gate = both[:FFW]
    sigmoid = 1.0 / (1.0 + jnp.exp(-gate))
    slope_ref[...] = sigmoid * (1.0 + gate * (1.0 - sigmoid))
    sum_ref[...] = dot(both[FFW:].astype(BF), rows)
    for k, out in enumerate((i0, i1, i2, i3)):
        base = lax.rem(x + k, REPS) * SHARE
        out[...] = sum_ref[:, pl.ds(pl.multiple_of(base, SHARE), SHARE)].astype(out.dtype)


def gate_part(
    pos_ref, grad_probes_ref, slope_ref, got_ref, own_ref, out_ref,
    whole_ref, shared_ref, sketch_ref, held_ref, sem,
):
    x = pos_ref[0]
    copy = pltpu.make_async_copy(slope_ref, held_ref, sem)
    copy.start()

    def put_whole(p, at, got):
        whole_ref[p * SLOTS + at.start : p * SLOTS + at.stop, :] = got

    def put_shared(p, at, got):
        shared_ref[p * PAIRS + at.start : p * PAIRS + at.stop, :] = got

    regroup(lambda at: got_ref[at, :], 4, put_whole)
    regroup(lambda at: got_ref[at, :], 16, put_shared)
    same = ones_where(iota((UNITS, 256), 0) == iota((UNITS, 256), 1))
    whole = dot(same, whole_ref[...], NT)
    last = ones_where(iota((64, 256), 0) + UNITS == iota((64, 256), 1))
    shared = dot(last, shared_ref[...], NT)
    turned = pltpu.roll(shared, ROWS - PAIRS, 1)
    parts = []
    for p in (0, 1, 2, 3, 4, 5, 8, 9, 10, 11, 12, 13):
        at = p // 2 * 128
        parts.append((turned if p % 2 else shared)[:, at : at + 128])
    late = jnp.concatenate(parts, 0)
    late = jnp.where(iota((FFW, 128), 1) < PAIRS, late, 0.0)
    early = jnp.concatenate([whole[:, b * SLOTS : (b + 1) * SLOTS] for b in range(4)], 0)
    grads = jnp.concatenate([early, late], 1)
    copy.wait()
    gate_grad = (grads * held_ref[...]).astype(BF)
    projected = dot(grad_probes_ref[...], gate_grad).astype(BF)
    sketch_ref[...] = dot(gate_grad, projected, NT)
    out_ref[...] = sketch_ref[...].astype(BF)
    own_ref[...] = sketch_ref[pl.ds(pl.multiple_of(x * UNITS, UNITS), UNITS), :]


def finish_input(inverse_ref, i0, i1, i2, i3, out_ref):
    total = i0[...] + (i1[...].astype(F32) + i2[...].astype(F32) + i3[...].astype(F32))
    out_ref[...] = (total * inverse_ref[0]).T


def finish_grad(pos_ref, inverse_ref, own_ref, parts_ref, out_ref):
    total = own_ref[...]
    for k in range(1, REPS):
        total += parts_ref[lax.rem(pos_ref[0] + k, REPS)].astype(F32)
    out_ref[...] = total * inverse_ref[0]


def shift(block, k):
    return lax.ppermute(block, "rep", [(i, (i + k) % REPS) for i in range(REPS)])


def shifted(blocks):
    return [blocks[0]] + [shift(blocks[k], k) for k in range(1, REPS)]


def swap(block):
    return lax.ppermute(block, "ep", [(i, i ^ 1) for i in range(OWNERS)])


def to_owners(rows):
    width = rows.shape[1]
    rows = rows.reshape(OWNERS, FOLD, width)
    return lax.all_to_all(rows, "ep", split_axis=0, concat_axis=0, tiled=True).reshape(ROWS, width)


def local(tokens, expert_ids, hidden_grads, gate_weight, probes, grad_probes, window_counts):
    sds = jax.ShapeDtypeStruct
    pos = jnp.stack([lax.axis_index("rep"), lax.axis_index("ep") % 2]).astype(jnp.int32)
    inverse = 1.0 / window_counts.astype(F32)
    ids_t = expert_ids.T

    packed = pl.pallas_call(
        pack_half,
        out_shape=sds((TOK + 16, HALF), BF),
        grid_spec=pltpu.PrefetchScalarGridSpec(
            num_scalar_prefetch=1,
            grid=(1,),
            in_specs=[VM, pl.BlockSpec((TOK, HALF), lambda i, pos: (0, 1 - pos[1]))],
            out_specs=VM,
        ),
        compiler_params=pltpu.CompilerParams(vmem_limit_bytes=6 * MIB),
        cost_estimate=pl.CostEstimate(flops=1000, bytes_accessed=MIB, transcendentals=0),
    )(pos, ids_t, tokens)
    other = swap(packed)
    out_rows = kernel_call(
        send_rows,
        sds((ROWS, SHARE + STRIP), BF),
        [SM] + [VM] * 3,
        1 << 30,
        5 * MIB,
        20,
        [
            pltpu.VMEM((ROWS, SHARE + STRIP), BF),
            pltpu.VMEM((TOK, HALF), BF),
            pltpu.VMEM((TOP, TOK), jnp.int32),
            pltpu.SemaphoreType.DMA((ROWS // 256,)),
        ],
        pl.BlockSpec(memory_space=pl.ANY),
    )(pos, ids_t, tokens, other)
    rows = to_owners(out_rows)

    own, grads = gate_weight[0], hidden_grads.reshape(TOK * TOP, UNITS)
    own, grads, _ = lax.optimization_barrier((own, grads, out_rows))
    left, right = shift(own, 1), shift(own, REPS - 1)
    other_grads = swap(grads)
    picked = kernel_call(
        pick_grads, [sds((SLOTS + OWNERS, 256), BF)] * REPS, [SM] + [VM] * 4, 5 << 30, 3 * MIB, 20
    )(pos, ids_t, other, grads, other_grads)
    left, right, _ = lax.optimization_barrier((left, right, picked[1]))
    top = shift(left[: UNITS // 2], 1)
    bottom = shift(right[UNITS // 2 :], REPS - 1)
    out_grads = kernel_call(
        fold_grads,
        sds((ROWS, 256), BF),
        [SM] + [VM] * 4,
        1 << 27,
        3 * MIB,
        8,
        [pltpu.VMEM((2, ROWS, 128), F32)],
    )(pos, *shifted(picked))
    weights = kernel_call(
        stack_weights, sds((FFW + R, D), BF), [SM] + [VM] * 6, 1000, 14 * MIB, 8
    )(pos, probes, own, right, top, bottom, left)
    got = to_owners(out_grads)

    kinds = [F32, BF, BF, BF]
    slope, *inputs = kernel_call(
        products,
        [sds((FFW, ALL), F32)] + [sds((R, SHARE), kind) for kind in kinds],
        [SM] + [VM] * 2,
        4 << 30,
        12 * MIB,
        20,
        [pltpu.VMEM((ALL, D), BF), pltpu.VMEM((R, D), F32)],
    )(pos, rows, weights)
    inputs = shifted(inputs)

    own_sketch, sketch = kernel_call(
        gate_part,
        [sds((UNITS, R), F32), sds((FFW, R), BF)],
        [SM, VM, pl.BlockSpec(memory_space=pl.ANY), VM],
        1 << 30,
        3 * MIB,
        16,
        [
            pltpu.VMEM((ROWS, 256), BF),
            pltpu.VMEM((ROWS, 256), BF),
            pltpu.VMEM((FFW, R), F32),
            pltpu.VMEM((FFW, ALL), F32),
            pltpu.SemaphoreType.DMA,
        ],
    )(pos, grad_probes, slope, got)
    sketches = lax.all_to_all(
        sketch.reshape(REPS, UNITS, R), "rep", split_axis=0, concat_axis=0, tiled=True
    )

    input_sketch = kernel_call(
        finish_input, sds((SHARE, R), F32), [SM] + [VM] * 4, 1 << 20, 2 * MIB, 6
    )(inverse, *inputs)
    own_sketch, input_sketch = lax.optimization_barrier((own_sketch, input_sketch))
    grad_sketch = kernel_call(
        finish_grad, sds((UNITS, R), F32), [SM] * 2 + [VM] * 2, 1 << 18, MIB // 4, 4
    )(pos, inverse, own_sketch, sketches)
    return input_sketch[None], grad_sketch[None]


def solution(mesh):
    placed = (
        P("ep", None),
        P("ep", None),
        P("ep", None, "rep"),
        P("ep", "rep", None),
        P(),
        P(),
        P("ep"),
    )
    return jax.shard_map(
        local,
        mesh=mesh,
        in_specs=placed,
        out_specs=(P("ep", "rep", None), P("ep", "rep", None)),
        check_vma=False,
    )
```

```python
import jax
import jax.numpy as jnp
from jax import lax
from jax.experimental import pallas as pl
from jax.experimental.pallas import tpu as pltpu
from jax.sharding import PartitionSpec as P

OWNERS = 128
PAIRS = OWNERS // 2
REPS = 4
TOK = 128
TOP = 8
D = 4096
HALF = D // 2
SHARE = D // REPS
FFW = 768
UNITS = FFW // REPS
R = 128
FIRST = 8
FOLD = 8
ROWS = OWNERS * FOLD
SLOTS = OWNERS * 2
ALL = SLOTS + 128
STRIP = HALF // FOLD
MIB = 1 << 20

BF = jnp.bfloat16
F32 = jnp.float32
NT = (((1,), (1,)), ((), ()))
NN = (((1,), (0,)), ((), ()))

VM = pl.BlockSpec(memory_space=pltpu.VMEM)
SM = pl.BlockSpec(memory_space=pltpu.SMEM)


def dot(a, b, dims=NN):
    return lax.dot_general(a, b, dims, preferred_element_type=F32)


def iota(shape, axis):
    return lax.broadcasted_iota(jnp.int32, shape, axis)


def ones_where(mask):
    return jnp.where(mask, 1.0, 0.0).astype(BF)


def kernel_call(body, out_shape, in_specs, flops, bytes_accessed, limit, scratch=(), out_specs=None):
    return pl.pallas_call(
        body,
        out_shape=out_shape,
        in_specs=in_specs,
        out_specs=out_specs or jax.tree.map(lambda _: VM, out_shape),
        scratch_shapes=list(scratch),
        compiler_params=pltpu.CompilerParams(vmem_limit_bytes=limit * MIB),
        cost_estimate=pl.CostEstimate(
            flops=flops, bytes_accessed=bytes_accessed, transcendentals=0
        ),
    )


def places(ids_t):
    experts = iota((OWNERS, TOK), 0)
    named = jnp.zeros((OWNERS, TOK), F32)
    for k in range(TOP):
        named += jnp.where(ids_t[k : k + 1, :] == experts, 1.0, 0.0)
    before = ones_where(iota((TOK, TOK), 0) < iota((TOK, TOK), 1))
    rank = dot(named.astype(BF), before)
    return jnp.where(named > 0.0, rank, -1.0)


def pair_places(ids_t):
    pairs = TOK * TOP
    widen = ones_where(iota((TOK, pairs), 1) // TOP == iota((TOK, pairs), 0))
    ranks = dot(places(ids_t).astype(BF), widen)
    ids = dot(ids_t.astype(F32).astype(BF), widen)
    mine = iota((TOP, pairs), 1) % TOP == iota((TOP, pairs), 0)
    flat = jnp.sum(jnp.where(mine, ids, 0.0), axis=0, keepdims=True)
    return jnp.where(flat == iota((OWNERS, pairs), 0).astype(F32), ranks, -1.0)


def spread(table, times):
    shape = (OWNERS * times, OWNERS)
    return dot(ones_where(iota(shape, 0) // times == iota(shape, 1)), table.astype(BF))


def fold(picked, many, g):
    size = 256 // many
    width = picked.shape[1] // many
    shape = (256, 256)
    to = iota(shape, 0)
    order = ones_where(iota(shape, 1) == to % many * size + to // many)
    at = slice(g * size, (g + 1) * size)
    parts = [picked[at, p * width : (p + 1) * width] for p in range(many)]
    return dot(order, jnp.concatenate(parts, 0)).astype(BF)


def send_rows(
    pos_ref, ids_ref, tokens_ref, other_ids_ref, other_ref,
    out_ref, made_ref, half_ref, half_ids_ref, sems,
):
    x, c = pos_ref[0], pos_ref[1]
    mine = x // 2 == c
    columns = pl.ds(pl.multiple_of(c * HALF, HALF), HALF)

    @pl.when(mine)
    def _():
        half_ref[...] = tokens_ref[:, columns]
        half_ids_ref[...] = ids_ref[...]

    @pl.when(jnp.logical_not(mine))
    def _():
        half_ref[...] = other_ref[:, columns]
        half_ids_ref[...] = other_ids_ref[...]

    table = places(half_ids_ref[...])
    shared = dot(ones_where(table == (FIRST + x % 2).astype(F32)), half_ref[...]).astype(BF)
    table = spread(places(ids_ref[...]), 2)
    place = 2 * x + iota(table.shape, 0) % 2
    picks = ones_where(table == place.astype(F32))
    copies = []
    for g in range(ROWS // 256):
        at = slice(g * 256, (g + 1) * 256)
        whole = dot(picks[g * 64 : (g + 1) * 64], tokens_ref[...]).astype(BF)
        made_ref[at, :SHARE] = fold(whole, 4, 0)
        made_ref[at, SHARE:] = fold(shared, FOLD, g)
        copy = pltpu.make_async_copy(made_ref.at[at, :], out_ref.at[at, :], sems.at[g])
        copy.start()
        copies.append(copy)
    for copy in copies:
        copy.wait()


def pick_grads(pos_ref, ids_ref, other_ids_ref, grads_ref, other_grads_ref, *outs):
    x, c = pos_ref[0], pos_ref[1]
    pairs = TOK * TOP
    table, other_table = pair_places(ids_ref[...]), pair_places(other_ids_ref[...])
    embed = ones_where(iota((UNITS, 256), 0) == iota((UNITS, 256), 1))
    grads = dot(grads_ref[...], embed).astype(BF)
    other_grads = dot(other_grads_ref[...], embed).astype(BF)
    twice = spread(table, 2)
    second = iota((SLOTS, pairs), 0) % 2
    for k, out in enumerate(outs):
        to = lax.rem(x + k, REPS)
        out[:SLOTS, :] = dot(ones_where(twice == (2 * to + second).astype(F32)), grads).astype(BF)
        shared = FIRST + to % 2
        place = jnp.where(to // 2 == c, shared, -2).astype(F32)
        other_place = jnp.where(to // 2 == c, -2, shared).astype(F32)
        out[SLOTS:, :] = (
            dot(ones_where(table == place), grads)
            + dot(ones_where(other_table == other_place), other_grads)
        ).astype(BF)


def fold_grads(pos_ref, g0, g1, g2, g3, out_ref, fold_ref):
    x, c = pos_ref[0], pos_ref[1]
    for k, got in enumerate((g0, g1, g2, g3)):
        unit = lax.rem(x - k + REPS, REPS)
        for h in range(2):
            block = got[:SLOTS, h * 128 : (h + 1) * 128].astype(F32)
            fold_ref[h, pl.ds(unit, SLOTS, stride=4), :] = block
    for k, got in enumerate((g0, g1, g2, g3)):
        unit = lax.rem(x - k + REPS, REPS)

        @pl.when(unit // 2 == c)
        def _():
            source, lane = iota((256, 128), 0), iota((256, 128), 1)
            for u in range(3):
                move = ones_where((source // 64 == u) & (lane == 64 + source % 64))
                at = pl.ds(unit % 2 * 3 + u, OWNERS, stride=FOLD)
                fold_ref[1, at, :] = fold_ref[1, at, :] + dot(got[SLOTS:, :], move)

    for h in range(2):
        out_ref[:, h * 128 : (h + 1) * 128] = fold_ref[h].astype(BF)


def regroup(source, many, put):
    size = 256 // many
    shape = (256, 256)
    to = iota(shape, 0)
    order = ones_where(iota(shape, 1) == many * (to % size) + to // size)
    for g in range(ROWS // 256):
        got = dot(order, source(slice(g * 256, (g + 1) * 256))).astype(BF)
        for p in range(many):
            put(p, slice(g * size, (g + 1) * size), got[p * size : (p + 1) * size])


def stack_weights(pos_ref, probes_ref, own_ref, right_ref, top_ref, bottom_ref, left_ref, out_ref):
    x = pos_ref[0]
    half = UNITS // 2
    for w, k, start, size in (
        (own_ref, 0, 0, UNITS),
        (right_ref, 1, 0, UNITS),
        (top_ref, 2, 0, half),
        (bottom_ref, 2, half, half),
        (left_ref, 3, 0, UNITS),
    ):
        base = lax.rem(x + k, REPS) * UNITS + start
        out_ref[pl.ds(pl.multiple_of(base, half), size), :] = w[...]
    out_ref[FFW:, :] = probes_ref[...]


def products(
    pos_ref, rows_ref, weights_ref, slope_ref, i0, i1, i2, i3, rows_all_ref, sum_ref
):
    x = pos_ref[0]

    def put_whole(p, at, got):
        rows_all_ref[at, p * SHARE : (p + 1) * SHARE] = got

    def put_shared(p, at, got):
        rows_all_ref[SLOTS + at.start : SLOTS + at.stop, p * STRIP : (p + 1) * STRIP] = got

    regroup(lambda at: rows_ref[at, :SHARE], 4, put_whole)
    regroup(lambda at: rows_ref[at, SHARE:], 16, put_shared)
    rows_all_ref[SLOTS + PAIRS :, :] = jnp.zeros((ALL - SLOTS - PAIRS, D), BF)
    rows = rows_all_ref[...]
    both = dot(weights_ref[...], rows, NT)
    gate = both[:FFW]
    sigmoid = 1.0 / (1.0 + jnp.exp(-gate))
    slope_ref[...] = sigmoid * (1.0 + gate * (1.0 - sigmoid))
    sum_ref[...] = dot(both[FFW:].astype(BF), rows)
    for k, out in enumerate((i0, i1, i2, i3)):
        base = lax.rem(x + k, REPS) * SHARE
        out[...] = sum_ref[:, pl.ds(pl.multiple_of(base, SHARE), SHARE)].astype(out.dtype)


def gate_part(
    pos_ref, grad_probes_ref, slope_ref, got_ref, own_ref, out_ref,
    whole_ref, shared_ref, sketch_ref, held_ref, sem,
):
    x = pos_ref[0]
    copy = pltpu.make_async_copy(slope_ref, held_ref, sem)
    copy.start()

    def put_whole(p, at, got):
        whole_ref[p * SLOTS + at.start : p * SLOTS + at.stop, :] = got

    def put_shared(p, at, got):
        shared_ref[p * PAIRS + at.start : p * PAIRS + at.stop, :] = got

    regroup(lambda at: got_ref[at, :], 4, put_whole)
    regroup(lambda at: got_ref[at, :], 16, put_shared)
    same = ones_where(iota((UNITS, 256), 0) == iota((UNITS, 256), 1))
    whole = dot(same, whole_ref[...], NT)
    last = ones_where(iota((64, 256), 0) + UNITS == iota((64, 256), 1))
    shared = dot(last, shared_ref[...], NT)
    turned = pltpu.roll(shared, ROWS - PAIRS, 1)
    parts = []
    for p in (0, 1, 2, 3, 4, 5, 8, 9, 10, 11, 12, 13):
        at = p // 2 * 128
        parts.append((turned if p % 2 else shared)[:, at : at + 128])
    late = jnp.concatenate(parts, 0)
    late = jnp.where(iota((FFW, 128), 1) < PAIRS, late, 0.0)
    early = jnp.concatenate([whole[:, b * SLOTS : (b + 1) * SLOTS] for b in range(4)], 0)
    grads = jnp.concatenate([early, late], 1)
    copy.wait()
    gate_grad = (grads * held_ref[...]).astype(BF)
    projected = dot(grad_probes_ref[...], gate_grad).astype(BF)
    sketch_ref[...] = dot(gate_grad, projected, NT)
    out_ref[...] = sketch_ref[...].astype(BF)
    own_ref[...] = sketch_ref[pl.ds(pl.multiple_of(x * UNITS, UNITS), UNITS), :]


def finish_input(inverse_ref, i0, i1, i2, i3, out_ref):
    total = i0[...] + (i1[...].astype(F32) + i2[...].astype(F32) + i3[...].astype(F32))
    out_ref[...] = (total * inverse_ref[0]).T


def finish_grad(pos_ref, inverse_ref, own_ref, parts_ref, out_ref):
    total = own_ref[...]
    for k in range(1, REPS):
        total += parts_ref[lax.rem(pos_ref[0] + k, REPS)].astype(F32)
    out_ref[...] = total * inverse_ref[0]


def shift(block, k):
    return lax.ppermute(block, "rep", [(i, (i + k) % REPS) for i in range(REPS)])


def shifted(blocks):
    return [blocks[0]] + [shift(blocks[k], k) for k in range(1, REPS)]


def swap(block):
    return lax.ppermute(block, "ep", [(i, i ^ 1) for i in range(OWNERS)])


def to_owners(rows):
    width = rows.shape[1]
    rows = rows.reshape(OWNERS, FOLD, width)
    return lax.all_to_all(rows, "ep", split_axis=0, concat_axis=0, tiled=True).reshape(ROWS, width)


def local(tokens, expert_ids, hidden_grads, gate_weight, probes, grad_probes, window_counts):
    sds = jax.ShapeDtypeStruct
    pos = jnp.stack([lax.axis_index("rep"), lax.axis_index("ep") % 2]).astype(jnp.int32)
    inverse = 1.0 / window_counts.astype(F32)
    ids_t = expert_ids.T

    other, other_ids = swap(tokens), swap(ids_t)
    out_rows = kernel_call(
        send_rows,
        sds((ROWS, SHARE + STRIP), BF),
        [SM] + [VM] * 4,
        1 << 30,
        5 * MIB,
        20,
        [
            pltpu.VMEM((ROWS, SHARE + STRIP), BF),
            pltpu.VMEM((TOK, HALF), BF),
            pltpu.VMEM((TOP, TOK), jnp.int32),
            pltpu.SemaphoreType.DMA((ROWS // 256,)),
        ],
        pl.BlockSpec(memory_space=pl.ANY),
    )(pos, ids_t, tokens, other_ids, other)
    rows = to_owners(out_rows)

    own, grads = gate_weight[0], hidden_grads.reshape(TOK * TOP, UNITS)
    own, grads, _ = lax.optimization_barrier((own, grads, out_rows))
    left, right = shift(own, 1), shift(own, REPS - 1)
    other_grads = swap(grads)
    picked = kernel_call(
        pick_grads, [sds((SLOTS + OWNERS, 256), BF)] * REPS, [SM] + [VM] * 4, 5 << 30, 3 * MIB, 20
    )(pos, ids_t, other_ids, grads, other_grads)
    left, right, _ = lax.optimization_barrier((left, right, picked[1]))
    top = shift(left[: UNITS // 2], 1)
    bottom = shift(right[UNITS // 2 :], REPS - 1)
    out_grads = kernel_call(
        fold_grads,
        sds((ROWS, 256), BF),
        [SM] + [VM] * 4,
        1 << 27,
        3 * MIB,
        8,
        [pltpu.VMEM((2, ROWS, 128), F32)],
    )(pos, *shifted(picked))
    weights = kernel_call(
        stack_weights, sds((FFW + R, D), BF), [SM] + [VM] * 6, 1000, 14 * MIB, 8
    )(pos, probes, own, right, top, bottom, left)
    got = to_owners(out_grads)

    kinds = [F32, BF, BF, BF]
    slope, *inputs = kernel_call(
        products,
        [sds((FFW, ALL), F32)] + [sds((R, SHARE), kind) for kind in kinds],
        [SM] + [VM] * 2,
        4 << 30,
        12 * MIB,
        20,
        [pltpu.VMEM((ALL, D), BF), pltpu.VMEM((R, D), F32)],
    )(pos, rows, weights)
    inputs = shifted(inputs)

    own_sketch, sketch = kernel_call(
        gate_part,
        [sds((UNITS, R), F32), sds((FFW, R), BF)],
        [SM, VM, pl.BlockSpec(memory_space=pl.ANY), VM],
        1 << 30,
        3 * MIB,
        16,
        [
            pltpu.VMEM((ROWS, 256), BF),
            pltpu.VMEM((ROWS, 256), BF),
            pltpu.VMEM((FFW, R), F32),
            pltpu.VMEM((FFW, ALL), F32),
            pltpu.SemaphoreType.DMA,
        ],
    )(pos, grad_probes, slope, got)
    sketches = lax.all_to_all(
        sketch.reshape(REPS, UNITS, R), "rep", split_axis=0, concat_axis=0, tiled=True
    )

    input_sketch = kernel_call(
        finish_input, sds((SHARE, R), F32), [SM] + [VM] * 4, 1 << 20, 2 * MIB, 6
    )(inverse, *inputs)
    own_sketch, input_sketch = lax.optimization_barrier((own_sketch, input_sketch))
    grad_sketch = kernel_call(
        finish_grad, sds((UNITS, R), F32), [SM] * 2 + [VM] * 2, 1 << 18, MIB // 4, 4
    )(pos, inverse, own_sketch, sketches)
    return input_sketch[None], grad_sketch[None]


def solution(mesh):
    placed = (
        P("ep", None),
        P("ep", None),
        P("ep", None, "rep"),
        P("ep", "rep", None),
        P(),
        P(),
        P("ep"),
    )
    return jax.shard_map(
        local,
        mesh=mesh,
        in_specs=placed,
        out_specs=(P("ep", "rep", None), P("ep", "rep", None)),
        check_vma=False,
    )
```

```python
import jax
import jax.numpy as jnp
from jax import lax
from jax.experimental import pallas as pl
from jax.experimental.pallas import tpu as pltpu
from jax.sharding import PartitionSpec as P

OWNERS = 128
PAIRS = OWNERS // 2
REPS = 4
TOK = 128
TOP = 8
D = 4096
HALF = D // 2
SHARE = D // REPS
FFW = 768
UNITS = FFW // REPS
R = 128
FIRST = 8
FOLD = 8
ROWS = OWNERS * FOLD
SLOTS = OWNERS * 2
ALL = SLOTS + 128
STRIP = HALF // FOLD
MIB = 1 << 20

BF = jnp.bfloat16
F32 = jnp.float32
NT = (((1,), (1,)), ((), ()))
NN = (((1,), (0,)), ((), ()))

VM = pl.BlockSpec(memory_space=pltpu.VMEM)
SM = pl.BlockSpec(memory_space=pltpu.SMEM)


def dot(a, b, dims=NN):
    return lax.dot_general(a, b, dims, preferred_element_type=F32)


def iota(shape, axis):
    return lax.broadcasted_iota(jnp.int32, shape, axis)


def ones_where(mask):
    return jnp.where(mask, 1.0, 0.0).astype(BF)


def kernel_call(body, out_shape, in_specs, flops, bytes_accessed, limit, scratch=(), out_specs=None):
    return pl.pallas_call(
        body,
        out_shape=out_shape,
        in_specs=in_specs,
        out_specs=out_specs or jax.tree.map(lambda _: VM, out_shape),
        scratch_shapes=list(scratch),
        compiler_params=pltpu.CompilerParams(vmem_limit_bytes=limit * MIB),
        cost_estimate=pl.CostEstimate(
            flops=flops, bytes_accessed=bytes_accessed, transcendentals=0
        ),
    )


def places(ids_t):
    experts = iota((OWNERS, TOK), 0)
    named = jnp.zeros((OWNERS, TOK), F32)
    for k in range(TOP):
        named += jnp.where(ids_t[k : k + 1, :] == experts, 1.0, 0.0)
    before = ones_where(iota((TOK, TOK), 0) < iota((TOK, TOK), 1))
    rank = dot(named.astype(BF), before)
    return jnp.where(named > 0.0, rank, -1.0)


def pair_places(ids_t):
    pairs = TOK * TOP
    widen = ones_where(iota((TOK, pairs), 1) // TOP == iota((TOK, pairs), 0))
    ranks = dot(places(ids_t).astype(BF), widen)
    ids = dot(ids_t.astype(F32).astype(BF), widen)
    mine = iota((TOP, pairs), 1) % TOP == iota((TOP, pairs), 0)
    flat = jnp.sum(jnp.where(mine, ids, 0.0), axis=0, keepdims=True)
    return jnp.where(flat == iota((OWNERS, pairs), 0).astype(F32), ranks, -1.0)


def spread(table, times):
    shape = (OWNERS * times, OWNERS)
    return dot(ones_where(iota(shape, 0) // times == iota(shape, 1)), table.astype(BF))


def pack_half(pos_ref, ids_ref, tokens_ref, out_ref):
    out_ref[:TOK, :] = tokens_ref[...]
    out_ref[TOK:, :] = jnp.zeros((16, HALF), BF)
    ids = jnp.concatenate([ids_ref[...].astype(F32), jnp.zeros((8, TOK), F32)], 0)
    out_ref[TOK:, :TOK] = ids.astype(BF)


def other_ids(other_ref):
    return other_ref[TOK:, :TOK].astype(F32)[:TOP].astype(jnp.int32)


def fold(picked, many, g):
    size = 256 // many
    width = picked.shape[1] // many
    shape = (256, 256)
    to = iota(shape, 0)
    order = ones_where(iota(shape, 1) == to % many * size + to // many)
    at = slice(g * size, (g + 1) * size)
    parts = [picked[at, p * width : (p + 1) * width] for p in range(many)]
    return dot(order, jnp.concatenate(parts, 0)).astype(BF)


def send_rows(
    pos_ref, ids_ref, tokens_ref, other_ref, out_ref, made_ref, half_ref, half_ids_ref, sems
):
    x, c = pos_ref[0], pos_ref[1]
    mine = x // 2 == c

    @pl.when(mine)
    def _():
        half_ref[...] = tokens_ref[:, pl.ds(pl.multiple_of(c * HALF, HALF), HALF)]
        half_ids_ref[...] = ids_ref[...]

    @pl.when(jnp.logical_not(mine))
    def _():
        half_ref[...] = other_ref[:TOK, :]
        half_ids_ref[...] = other_ids(other_ref)

    table = places(half_ids_ref[...])
    shared = dot(ones_where(table == (FIRST + x % 2).astype(F32)), half_ref[...]).astype(BF)
    table = spread(places(ids_ref[...]), 2)
    place = 2 * x + iota(table.shape, 0) % 2
    picks = ones_where(table == place.astype(F32))
    copies = []
    for g in range(ROWS // 256):
        at = slice(g * 256, (g + 1) * 256)
        whole = dot(picks[g * 64 : (g + 1) * 64], tokens_ref[...]).astype(BF)
        made_ref[at, :SHARE] = fold(whole, 4, 0)
        made_ref[at, SHARE:] = fold(shared, FOLD, g)
        copy = pltpu.make_async_copy(made_ref.at[at, :], out_ref.at[at, :], sems.at[g])
        copy.start()
        copies.append(copy)
    for copy in copies:
        copy.wait()


def pick_grads(pos_ref, ids_ref, other_ref, grads_ref, other_grads_ref, *outs):
    x, c = pos_ref[0], pos_ref[1]
    pairs = TOK * TOP
    table, other_table = pair_places(ids_ref[...]), pair_places(other_ids(other_ref))
    embed = ones_where(iota((UNITS, 256), 0) == iota((UNITS, 256), 1))
    grads = dot(grads_ref[...], embed).astype(BF)
    other_grads = dot(other_grads_ref[...], embed).astype(BF)
    twice = spread(table, 2)
    second = iota((SLOTS, pairs), 0) % 2
    for k, out in enumerate(outs):
        to = lax.rem(x + k, REPS)
        out[:SLOTS, :] = dot(ones_where(twice == (2 * to + second).astype(F32)), grads).astype(BF)
        shared = FIRST + to % 2
        place = jnp.where(to // 2 == c, shared, -2).astype(F32)
        other_place = jnp.where(to // 2 == c, -2, shared).astype(F32)
        out[SLOTS:, :] = (
            dot(ones_where(table == place), grads)
            + dot(ones_where(other_table == other_place), other_grads)
        ).astype(BF)


def fold_grads(pos_ref, g0, g1, g2, g3, out_ref, fold_ref):
    x, c = pos_ref[0], pos_ref[1]
    for k, got in enumerate((g0, g1, g2, g3)):
        unit = lax.rem(x - k + REPS, REPS)
        for h in range(2):
            block = got[:SLOTS, h * 128 : (h + 1) * 128].astype(F32)
            fold_ref[h, pl.ds(unit, SLOTS, stride=4), :] = block
    for k, got in enumerate((g0, g1, g2, g3)):
        unit = lax.rem(x - k + REPS, REPS)

        @pl.when(unit // 2 == c)
        def _():
            source, lane = iota((256, 128), 0), iota((256, 128), 1)
            for u in range(3):
                move = ones_where((source // 64 == u) & (lane == 64 + source % 64))
                at = pl.ds(unit % 2 * 3 + u, OWNERS, stride=FOLD)
                fold_ref[1, at, :] = fold_ref[1, at, :] + dot(got[SLOTS:, :], move)

    for h in range(2):
        out_ref[:, h * 128 : (h + 1) * 128] = fold_ref[h].astype(BF)


def regroup(source, many, put):
    size = 256 // many
    shape = (256, 256)
    to = iota(shape, 0)
    order = ones_where(iota(shape, 1) == many * (to % size) + to // size)
    for g in range(ROWS // 256):
        got = dot(order, source(slice(g * 256, (g + 1) * 256))).astype(BF)
        for p in range(many):
            put(p, slice(g * size, (g + 1) * size), got[p * size : (p + 1) * size])


def stack_weights(pos_ref, probes_ref, own_ref, right_ref, top_ref, bottom_ref, left_ref, out_ref):
    x = pos_ref[0]
    half = UNITS // 2
    for w, k, start, size in (
        (own_ref, 0, 0, UNITS),
        (right_ref, 1, 0, UNITS),
        (top_ref, 2, 0, half),
        (bottom_ref, 2, half, half),
        (left_ref, 3, 0, UNITS),
    ):
        base = lax.rem(x + k, REPS) * UNITS + start
        out_ref[pl.ds(pl.multiple_of(base, half), size), :] = w[...]
    out_ref[FFW:, :] = probes_ref[...]


def products(
    pos_ref, rows_ref, weights_ref, slope_ref, i0, i1, i2, i3, rows_all_ref, sum_ref
):
    x = pos_ref[0]

    def put_whole(p, at, got):
        rows_all_ref[at, p * SHARE : (p + 1) * SHARE] = got

    def put_shared(p, at, got):
        rows_all_ref[SLOTS + at.start : SLOTS + at.stop, p * STRIP : (p + 1) * STRIP] = got

    regroup(lambda at: rows_ref[at, :SHARE], 4, put_whole)
    regroup(lambda at: rows_ref[at, SHARE:], 16, put_shared)
    rows_all_ref[SLOTS + PAIRS :, :] = jnp.zeros((ALL - SLOTS - PAIRS, D), BF)
    rows = rows_all_ref[...]
    both = dot(weights_ref[...], rows, NT)
    gate = both[:FFW]
    sigmoid = 1.0 / (1.0 + jnp.exp(-gate))
    slope_ref[...] = sigmoid * (1.0 + gate * (1.0 - sigmoid))
    sum_ref[...] = dot(both[FFW:].astype(BF), rows)
    for k, out in enumerate((i0, i1, i2, i3)):
        base = lax.rem(x + k, REPS) * SHARE
        out[...] = sum_ref[:, pl.ds(pl.multiple_of(base, SHARE), SHARE)].astype(out.dtype)


def gate_part(
    pos_ref, grad_probes_ref, slope_ref, got_ref, own_ref, out_ref,
    whole_ref, shared_ref, sketch_ref, held_ref, probes_ref, sems,
):
    x = pos_ref[0]
    copy = pltpu.make_async_copy(slope_ref, held_ref, sems.at[0])
    copy.start()
    second_copy = pltpu.make_async_copy(grad_probes_ref, probes_ref, sems.at[1])
    second_copy.start()

    def put_whole(p, at, got):
        whole_ref[p * SLOTS + at.start : p * SLOTS + at.stop, :] = got

    def put_shared(p, at, got):
        shared_ref[p * PAIRS + at.start : p * PAIRS + at.stop, :] = got

    regroup(lambda at: got_ref[at, :], 4, put_whole)
    regroup(lambda at: got_ref[at, :], 16, put_shared)
    same = ones_where(iota((UNITS, 256), 0) == iota((UNITS, 256), 1))
    whole = dot(same, whole_ref[...], NT)
    last = ones_where(iota((64, 256), 0) + UNITS == iota((64, 256), 1))
    shared = dot(last, shared_ref[...], NT)
    turned = pltpu.roll(shared, ROWS - PAIRS, 1)
    parts = []
    for p in (0, 1, 2, 3, 4, 5, 8, 9, 10, 11, 12, 13):
        at = p // 2 * 128
        parts.append((turned if p % 2 else shared)[:, at : at + 128])
    late = jnp.concatenate(parts, 0)
    late = jnp.where(iota((FFW, 128), 1) < PAIRS, late, 0.0)
    early = jnp.concatenate([whole[:, b * SLOTS : (b + 1) * SLOTS] for b in range(4)], 0)
    grads = jnp.concatenate([early, late], 1)
    copy.wait()
    gate_grad = (grads * held_ref[...]).astype(BF)
    second_copy.wait()
    projected = dot(probes_ref[...], gate_grad).astype(BF)
    sketch_ref[...] = dot(gate_grad, projected, NT)
    out_ref[...] = sketch_ref[...].astype(BF)
    own_ref[...] = sketch_ref[pl.ds(pl.multiple_of(x * UNITS, UNITS), UNITS), :]


def finish_input(inverse_ref, i0, i1, i2, i3, out_ref):
    total = i0[...] + (i1[...].astype(F32) + i2[...].astype(F32) + i3[...].astype(F32))
    out_ref[...] = (total * inverse_ref[0]).T


def finish_grad(pos_ref, inverse_ref, own_ref, parts_ref, out_ref):
    total = own_ref[...]
    for k in range(1, REPS):
        total += parts_ref[lax.rem(pos_ref[0] + k, REPS)].astype(F32)
    out_ref[...] = total * inverse_ref[0]


def shift(block, k):
    return lax.ppermute(block, "rep", [(i, (i + k) % REPS) for i in range(REPS)])


def shifted(blocks):
    return [blocks[0]] + [shift(blocks[k], k) for k in range(1, REPS)]


def swap(block):
    return lax.ppermute(block, "ep", [(i, i ^ 1) for i in range(OWNERS)])


def to_owners(rows):
    width = rows.shape[1]
    rows = rows.reshape(OWNERS, FOLD, width)
    return lax.all_to_all(rows, "ep", split_axis=0, concat_axis=0, tiled=True).reshape(ROWS, width)


def local(tokens, expert_ids, hidden_grads, gate_weight, probes, grad_probes, window_counts):
    sds = jax.ShapeDtypeStruct
    pos = jnp.stack([lax.axis_index("rep"), lax.axis_index("ep") % 2]).astype(jnp.int32)
    inverse = 1.0 / window_counts.astype(F32)
    ids_t = expert_ids.T

    packed = pl.pallas_call(
        pack_half,
        out_shape=sds((TOK + 16, HALF), BF),
        grid_spec=pltpu.PrefetchScalarGridSpec(
            num_scalar_prefetch=1,
            grid=(1,),
            in_specs=[VM, pl.BlockSpec((TOK, HALF), lambda i, pos: (0, 1 - pos[1]))],
            out_specs=VM,
        ),
        compiler_params=pltpu.CompilerParams(vmem_limit_bytes=6 * MIB),
        cost_estimate=pl.CostEstimate(flops=1000, bytes_accessed=MIB, transcendentals=0),
    )(pos, ids_t, tokens)
    other = swap(packed)
    out_rows = kernel_call(
        send_rows,
        sds((ROWS, SHARE + STRIP), BF),
        [SM] + [VM] * 3,
        1 << 30,
        5 * MIB,
        20,
        [
            pltpu.VMEM((ROWS, SHARE + STRIP), BF),
            pltpu.VMEM((TOK, HALF), BF),
            pltpu.VMEM((TOP, TOK), jnp.int32),
            pltpu.SemaphoreType.DMA((ROWS // 256,)),
        ],
        pl.BlockSpec(memory_space=pl.ANY),
    )(pos, ids_t, tokens, other)
    rows = to_owners(out_rows)

    own, grads = gate_weight[0], hidden_grads.reshape(TOK * TOP, UNITS)
    own, grads, _ = lax.optimization_barrier((own, grads, out_rows))
    left, right = shift(own, 1), shift(own, REPS - 1)
    other_grads = swap(grads)
    picked = kernel_call(
        pick_grads, [sds((SLOTS + OWNERS, 256), BF)] * REPS, [SM] + [VM] * 4, 5 << 30, 3 * MIB, 20
    )(pos, ids_t, other, grads, other_grads)
    left, right, _ = lax.optimization_barrier((left, right, picked[1]))
    top = shift(left[: UNITS // 2], 1)
    bottom = shift(right[UNITS // 2 :], REPS - 1)
    out_grads = kernel_call(
        fold_grads,
        sds((ROWS, 256), BF),
        [SM] + [VM] * 4,
        1 << 27,
        3 * MIB,
        8,
        [pltpu.VMEM((2, ROWS, 128), F32)],
    )(pos, *shifted(picked))
    weights = kernel_call(
        stack_weights, sds((FFW + R, D), BF), [SM] + [VM] * 6, 1000, 14 * MIB, 8
    )(pos, probes, own, right, top, bottom, left)
    got = to_owners(out_grads)

    kinds = [F32, BF, BF, BF]
    slope, *inputs = kernel_call(
        products,
        [sds((FFW, ALL), F32)] + [sds((R, SHARE), kind) for kind in kinds],
        [SM] + [VM] * 2,
        4 << 30,
        12 * MIB,
        20,
        [pltpu.VMEM((ALL, D), BF), pltpu.VMEM((R, D), F32)],
    )(pos, rows, weights)
    inputs = shifted(inputs)

    own_sketch, sketch = kernel_call(
        gate_part,
        [sds((UNITS, R), F32), sds((FFW, R), BF)],
        [SM] + [pl.BlockSpec(memory_space=pl.ANY)] * 2 + [VM],
        1 << 30,
        3 * MIB,
        16,
        [
            pltpu.VMEM((ROWS, 256), BF),
            pltpu.VMEM((ROWS, 256), BF),
            pltpu.VMEM((FFW, R), F32),
            pltpu.VMEM((FFW, ALL), F32),
            pltpu.VMEM((R, FFW), BF),
            pltpu.SemaphoreType.DMA((2,)),
        ],
    )(pos, grad_probes, slope, got)
    sketches = lax.all_to_all(
        sketch.reshape(REPS, UNITS, R), "rep", split_axis=0, concat_axis=0, tiled=True
    )

    input_sketch = kernel_call(
        finish_input, sds((SHARE, R), F32), [SM] + [VM] * 4, 1 << 20, 2 * MIB, 6
    )(inverse, *inputs)
    own_sketch, input_sketch = lax.optimization_barrier((own_sketch, input_sketch))
    grad_sketch = kernel_call(
        finish_grad, sds((UNITS, R), F32), [SM] * 2 + [VM] * 2, 1 << 18, MIB // 4, 4
    )(pos, inverse, own_sketch, sketches)
    return input_sketch[None], grad_sketch[None]


def solution(mesh):
    placed = (
        P("ep", None),
        P("ep", None),
        P("ep", None, "rep"),
        P("ep", "rep", None),
        P(),
        P(),
        P("ep"),
    )
    return jax.shard_map(
        local,
        mesh=mesh,
        in_specs=placed,
        out_specs=(P("ep", "rep", None), P("ep", "rep", None)),
        check_vma=False,
    )
```

```python
import jax
import jax.numpy as jnp
from jax import lax
from jax.experimental import pallas as pl
from jax.experimental.pallas import tpu as pltpu
from jax.sharding import PartitionSpec as P

OWNERS = 128
PAIRS = OWNERS // 2
REPS = 4
TOK = 128
TOP = 8
D = 4096
HALF = D // 2
SHARE = D // REPS
FFW = 768
UNITS = FFW // REPS
R = 128
FIRST = 8
FOLD = 8
ROWS = OWNERS * FOLD
SLOTS = OWNERS * 2
ALL = SLOTS + 128
STRIP = HALF // FOLD
MIB = 1 << 20

BF = jnp.bfloat16
F32 = jnp.float32
NT = (((1,), (1,)), ((), ()))
NN = (((1,), (0,)), ((), ()))

VM = pl.BlockSpec(memory_space=pltpu.VMEM)
SM = pl.BlockSpec(memory_space=pltpu.SMEM)


def dot(a, b, dims=NN):
    return lax.dot_general(a, b, dims, preferred_element_type=F32)


def iota(shape, axis):
    return lax.broadcasted_iota(jnp.int32, shape, axis)


def ones_where(mask):
    return jnp.where(mask, 1.0, 0.0).astype(BF)


def kernel_call(body, out_shape, in_specs, flops, bytes_accessed, limit, scratch=()):
    return pl.pallas_call(
        body,
        out_shape=out_shape,
        in_specs=in_specs,
        out_specs=jax.tree.map(lambda _: VM, out_shape),
        scratch_shapes=list(scratch),
        compiler_params=pltpu.CompilerParams(vmem_limit_bytes=limit * MIB),
        cost_estimate=pl.CostEstimate(
            flops=flops, bytes_accessed=bytes_accessed, transcendentals=0
        ),
    )


def places(ids_t):
    experts = iota((OWNERS, TOK), 0)
    named = jnp.zeros((OWNERS, TOK), F32)
    for k in range(TOP):
        named += jnp.where(ids_t[k : k + 1, :] == experts, 1.0, 0.0)
    before = ones_where(iota((TOK, TOK), 0) < iota((TOK, TOK), 1))
    rank = dot(named.astype(BF), before)
    return jnp.where(named > 0.0, rank, -1.0)


def pair_places(ids_t):
    pairs = TOK * TOP
    widen = ones_where(iota((TOK, pairs), 1) // TOP == iota((TOK, pairs), 0))
    ranks = dot(places(ids_t).astype(BF), widen)
    ids = dot(ids_t.astype(F32).astype(BF), widen)
    mine = iota((TOP, pairs), 1) % TOP == iota((TOP, pairs), 0)
    flat = jnp.sum(jnp.where(mine, ids, 0.0), axis=0, keepdims=True)
    return jnp.where(flat == iota((OWNERS, pairs), 0).astype(F32), ranks, -1.0)


def spread(table, times):
    shape = (OWNERS * times, OWNERS)
    return dot(ones_where(iota(shape, 0) // times == iota(shape, 1)), table.astype(BF))


def pack_half(pos_ref, ids_ref, tokens_ref, out_ref):
    out_ref[:TOK, :] = tokens_ref[...]
    out_ref[TOK:, :] = jnp.zeros((16, HALF), BF)
    ids = jnp.concatenate([ids_ref[...].astype(F32), jnp.zeros((8, TOK), F32)], 0)
    out_ref[TOK:, :TOK] = ids.astype(BF)


def other_ids(other_ref):
    return other_ref[TOK:, :TOK].astype(F32)[:TOP].astype(jnp.int32)


def send_rows(pos_ref, ids_ref, tokens_ref, other_ref, out_ref, half_ref, half_ids_ref, fold_ref):
    x, c = pos_ref[0], pos_ref[1]
    mine = x // 2 == c
    table = spread(places(ids_ref[...]), FOLD)
    row = iota((ROWS, TOK), 0)
    whole = table == (2 * x + row % 8 // 4).astype(F32)
    picks = jnp.concatenate([ones_where(whole & (row % 4 == b)) for b in range(4)], 1)
    parts = jnp.concatenate([tokens_ref[:, b * SHARE : (b + 1) * SHARE] for b in range(4)], 0)
    out_ref[:, :SHARE] = dot(picks, parts).astype(BF)

    @pl.when(mine)
    def _():
        half_ref[...] = tokens_ref[:, pl.ds(pl.multiple_of(c * HALF, HALF), HALF)]
        half_ids_ref[...] = ids_ref[...]

    @pl.when(jnp.logical_not(mine))
    def _():
        half_ref[...] = other_ref[:TOK, :]
        half_ids_ref[...] = other_ids(other_ref)

    picks = ones_where(places(half_ids_ref[...]) == (FIRST + x % 2).astype(F32))
    rows = dot(picks, half_ref[...])
    for b in range(FOLD):
        for h in range(2):
            start = b * STRIP + h * 128
            fold_ref[h, pl.ds(b, OWNERS, stride=FOLD), :] = rows[:, start : start + 128]
    for h in range(2):
        out_ref[:, SHARE + h * 128 : SHARE + (h + 1) * 128] = fold_ref[h].astype(BF)


def pick_grads(pos_ref, ids_ref, other_ref, grads_ref, other_grads_ref, *outs):
    x, c = pos_ref[0], pos_ref[1]
    pairs = TOK * TOP
    table, other_table = pair_places(ids_ref[...]), pair_places(other_ids(other_ref))
    embed = ones_where(iota((UNITS, 256), 0) == iota((UNITS, 256), 1))
    grads = dot(grads_ref[...], embed).astype(BF)
    other_grads = dot(other_grads_ref[...], embed).astype(BF)
    twice = spread(table, 2)
    second = iota((SLOTS, pairs), 0) % 2
    for k, out in enumerate(outs):
        to = lax.rem(x + k, REPS)
        out[:SLOTS, :] = dot(ones_where(twice == (2 * to + second).astype(F32)), grads).astype(BF)
        shared = FIRST + to % 2
        place = jnp.where(to // 2 == c, shared, -2).astype(F32)
        other_place = jnp.where(to // 2 == c, -2, shared).astype(F32)
        out[SLOTS:, :] = (
            dot(ones_where(table == place), grads)
            + dot(ones_where(other_table == other_place), other_grads)
        ).astype(BF)


def fold_grads(pos_ref, g0, g1, g2, g3, out_ref, fold_ref):
    x, c = pos_ref[0], pos_ref[1]
    for k, got in enumerate((g0, g1, g2, g3)):
        unit = lax.rem(x - k + REPS, REPS)
        for h in range(2):
            block = got[:SLOTS, h * 128 : (h + 1) * 128].astype(F32)
            fold_ref[h, pl.ds(unit, SLOTS, stride=4), :] = block
    for k, got in enumerate((g0, g1, g2, g3)):
        unit = lax.rem(x - k + REPS, REPS)

        @pl.when(unit // 2 == c)
        def _():
            source, lane = iota((256, 128), 0), iota((256, 128), 1)
            for u in range(3):
                move = ones_where((source // 64 == u) & (lane == 64 + source % 64))
                at = pl.ds(unit % 2 * 3 + u, OWNERS, stride=FOLD)
                fold_ref[1, at, :] = fold_ref[1, at, :] + dot(got[SLOTS:, :], move)

    for h in range(2):
        out_ref[:, h * 128 : (h + 1) * 128] = fold_ref[h].astype(BF)


def regroup(source, many, put):
    size = 256 // many
    shape = (256, 256)
    to = iota(shape, 0)
    order = ones_where(iota(shape, 1) == many * (to % size) + to // size)
    for g in range(ROWS // 256):
        got = dot(order, source(slice(g * 256, (g + 1) * 256))).astype(BF)
        for p in range(many):
            put(p, slice(g * size, (g + 1) * size), got[p * size : (p + 1) * size])


def stack_weights(pos_ref, probes_ref, own_ref, right_ref, top_ref, bottom_ref, left_ref, out_ref):
    x = pos_ref[0]
    half = UNITS // 2
    for w, k, start, size in (
        (own_ref, 0, 0, UNITS),
        (right_ref, 1, 0, UNITS),
        (top_ref, 2, 0, half),
        (bottom_ref, 2, half, half),
        (left_ref, 3, 0, UNITS),
    ):
        base = lax.rem(x + k, REPS) * UNITS + start
        out_ref[pl.ds(pl.multiple_of(base, half), size), :] = w[...]
    out_ref[FFW:, :] = probes_ref[...]


def products(
    pos_ref, rows_ref, weights_ref, gate_ref, i0, i1, i2, i3, rows_all_ref, sum_ref
):
    x = pos_ref[0]

    def put_whole(p, at, got):
        rows_all_ref[at, p * SHARE : (p + 1) * SHARE] = got

    def put_shared(p, at, got):
        rows_all_ref[SLOTS + at.start : SLOTS + at.stop, p * STRIP : (p + 1) * STRIP] = got

    regroup(lambda at: rows_ref[at, :SHARE], 4, put_whole)
    regroup(lambda at: rows_ref[at, SHARE:], 16, put_shared)
    rows_all_ref[SLOTS + PAIRS :, :] = jnp.zeros((ALL - SLOTS - PAIRS, D), BF)
    rows = rows_all_ref[...]
    both = dot(weights_ref[...], rows, NT)
    gate_ref[...] = both[:FFW]
    sum_ref[...] = dot(both[FFW:].astype(BF), rows)
    for k, out in enumerate((i0, i1, i2, i3)):
        base = lax.rem(x + k, REPS) * SHARE
        out[...] = sum_ref[:, pl.ds(pl.multiple_of(base, SHARE), SHARE)].astype(out.dtype)


def gate_part(
    pos_ref, grad_probes_ref, gate_ref, got_ref, own_ref, out_ref,
    whole_ref, shared_ref, sketch_ref,
):
    x = pos_ref[0]

    def put_whole(p, at, got):
        whole_ref[p * SLOTS + at.start : p * SLOTS + at.stop, :] = got

    def put_shared(p, at, got):
        shared_ref[p * PAIRS + at.start : p * PAIRS + at.stop, :] = got

    regroup(lambda at: got_ref[at, :], 4, put_whole)
    regroup(lambda at: got_ref[at, :], 16, put_shared)
    same = ones_where(iota((UNITS, 256), 0) == iota((UNITS, 256), 1))
    whole = dot(same, whole_ref[...], NT)
    last = ones_where(iota((64, 256), 0) + UNITS == iota((64, 256), 1))
    shared = dot(last, shared_ref[...], NT)
    turned = pltpu.roll(shared, ROWS - PAIRS, 1)
    parts = []
    for p in (0, 1, 2, 3, 4, 5, 8, 9, 10, 11, 12, 13):
        at = p // 2 * 128
        parts.append((turned if p % 2 else shared)[:, at : at + 128])
    late = jnp.concatenate(parts, 0)
    late = jnp.where(iota((FFW, 128), 1) < PAIRS, late, 0.0)
    early = jnp.concatenate([whole[:, b * SLOTS : (b + 1) * SLOTS] for b in range(4)], 0)
    grads = jnp.concatenate([early, late], 1)
    gate = gate_ref[...]
    s = 1.0 / (1.0 + jnp.exp(-gate))
    gate_grad = (grads * (s * (1.0 + gate * (1.0 - s)))).astype(BF)
    projected = dot(grad_probes_ref[...], gate_grad).astype(BF)
    sketch_ref[...] = dot(gate_grad, projected, NT)
    out_ref[...] = sketch_ref[...].astype(BF)
    own_ref[...] = sketch_ref[pl.ds(pl.multiple_of(x * UNITS, UNITS), UNITS), :]


def finish_input(inverse_ref, i0, i1, i2, i3, out_ref):
    total = i0[...] + (i1[...].astype(F32) + i2[...].astype(F32) + i3[...].astype(F32))
    out_ref[...] = (total * inverse_ref[0]).T


def finish_grad(pos_ref, inverse_ref, own_ref, parts_ref, out_ref):
    total = own_ref[...]
    for k in range(1, REPS):
        total += parts_ref[lax.rem(pos_ref[0] + k, REPS)].astype(F32)
    out_ref[...] = total * inverse_ref[0]


def shift(block, k):
    return lax.ppermute(block, "rep", [(i, (i + k) % REPS) for i in range(REPS)])


def shifted(blocks):
    return [blocks[0]] + [shift(blocks[k], k) for k in range(1, REPS)]


def swap(block):
    return lax.ppermute(block, "ep", [(i, i ^ 1) for i in range(OWNERS)])


def to_owners(rows):
    width = rows.shape[1]
    rows = rows.reshape(OWNERS, FOLD, width)
    return lax.all_to_all(rows, "ep", split_axis=0, concat_axis=0, tiled=True).reshape(ROWS, width)


def local(tokens, expert_ids, hidden_grads, gate_weight, probes, grad_probes, window_counts):
    sds = jax.ShapeDtypeStruct
    pos = jnp.stack([lax.axis_index("rep"), lax.axis_index("ep") % 2]).astype(jnp.int32)
    inverse = 1.0 / window_counts.astype(F32)
    ids_t = expert_ids.T

    packed = pl.pallas_call(
        pack_half,
        out_shape=sds((TOK + 16, HALF), BF),
        grid_spec=pltpu.PrefetchScalarGridSpec(
            num_scalar_prefetch=1,
            grid=(1,),
            in_specs=[VM, pl.BlockSpec((TOK, HALF), lambda i, pos: (0, 1 - pos[1]))],
            out_specs=VM,
        ),
        compiler_params=pltpu.CompilerParams(vmem_limit_bytes=6 * MIB),
        cost_estimate=pl.CostEstimate(flops=1000, bytes_accessed=MIB, transcendentals=0),
    )(pos, ids_t, tokens)
    other = swap(packed)
    out_rows = kernel_call(
        send_rows,
        sds((ROWS, SHARE + STRIP), BF),
        [SM] + [VM] * 3,
        1 << 31,
        5 * MIB,
        20,
        [
            pltpu.VMEM((TOK, HALF), BF),
            pltpu.VMEM((TOP, TOK), jnp.int32),
            pltpu.VMEM((2, ROWS, 128), F32),
        ],
    )(pos, ids_t, tokens, other)
    rows = to_owners(out_rows)

    own, grads = gate_weight[0], hidden_grads.reshape(TOK * TOP, UNITS)
    own, grads, _ = lax.optimization_barrier((own, grads, out_rows))
    left, right = shift(own, 1), shift(own, REPS - 1)
    other_grads = swap(grads)
    picked = kernel_call(
        pick_grads, [sds((SLOTS + OWNERS, 256), BF)] * REPS, [SM] + [VM] * 4, 5 << 30, 3 * MIB, 20
    )(pos, ids_t, other, grads, other_grads)
    left, right, _ = lax.optimization_barrier((left, right, picked[1]))
    top = shift(left[: UNITS // 2], 1)
    bottom = shift(right[UNITS // 2 :], REPS - 1)
    out_grads = kernel_call(
        fold_grads,
        sds((ROWS, 256), BF),
        [SM] + [VM] * 4,
        1 << 27,
        3 * MIB,
        8,
        [pltpu.VMEM((2, ROWS, 128), F32)],
    )(pos, *shifted(picked))
    weights = kernel_call(
        stack_weights, sds((FFW + R, D), BF), [SM] + [VM] * 6, 1000, 14 * MIB, 8
    )(pos, probes, own, right, top, bottom, left)
    got = to_owners(out_grads)

    kinds = [F32, BF, BF, BF]
    gate, *inputs = kernel_call(
        products,
        [sds((FFW, ALL), F32)] + [sds((R, SHARE), kind) for kind in kinds],
        [SM] + [VM] * 2,
        4 << 30,
        12 * MIB,
        20,
        [pltpu.VMEM((ALL, D), BF), pltpu.VMEM((R, D), F32)],
    )(pos, rows, weights)
    inputs = shifted(inputs)

    own_sketch, sketch = kernel_call(
        gate_part,
        [sds((UNITS, R), F32), sds((FFW, R), BF)],
        [SM] + [VM] * 3,
        1 << 30,
        3 * MIB,
        14,
        [pltpu.VMEM((ROWS, 256), BF), pltpu.VMEM((ROWS, 256), BF), pltpu.VMEM((FFW, R), F32)],
    )(pos, grad_probes, gate, got)
    sketches = lax.all_to_all(
        sketch.reshape(REPS, UNITS, R), "rep", split_axis=0, concat_axis=0, tiled=True
    )

    input_sketch = kernel_call(
        finish_input, sds((SHARE, R), F32), [SM] + [VM] * 4, 1 << 20, 2 * MIB, 6
    )(inverse, *inputs)
    own_sketch, input_sketch = lax.optimization_barrier((own_sketch, input_sketch))
    grad_sketch = kernel_call(
        finish_grad, sds((UNITS, R), F32), [SM] * 2 + [VM] * 2, 1 << 18, MIB // 4, 4
    )(pos, inverse, own_sketch, sketches)
    return input_sketch[None], grad_sketch[None]


def solution(mesh):
    placed = (
        P("ep", None),
        P("ep", None),
        P("ep", None, "rep"),
        P("ep", "rep", None),
        P(),
        P(),
        P("ep"),
    )
    return jax.shard_map(
        local,
        mesh=mesh,
        in_specs=placed,
        out_specs=(P("ep", "rep", None), P("ep", "rep", None)),
        check_vma=False,
    )
```
